32 devices in a mesh: section: 2 (over core), dp: 4 (over z), rep: 4 (over y, x).
Axes of the slice: x: 2, y: 2, z: 4, core: 2. Of those that a mesh axis runs over, the one named last changes fastest.
Arguments:
- block_input: bfloat16 [4, 4, 512, 256], P(None, 'rep', 'dp'), may hold values from -6 to 6
- output_grad: bfloat16 [4, 4, 512, 256], P(None, 'rep', 'dp'), may hold values from -6 to 6
- seq_lengths: int32 [4, 4, 4], replicated, may hold values from 1 to 509, as said below
- attn_gain: bfloat16 [2, 256], P('section'), may hold values from 0.5 to 1.5
- qkv_proj: bfloat16 [2, 256, 768], P('section'), may hold values from -0.5 to 0.5
- out_proj: bfloat16 [2, 256, 256], P('section'), may hold values from -1 to 1
- ffn_gain: bfloat16 [2, 256], P('section'), may hold values from 0.5 to 1.5
- up_proj: bfloat16 [2, 256, 1024], P('section'), may hold values from -0.375 to 0.375
- down_proj: bfloat16 [2, 1024, 256], P('section'), may hold values from -0.25 to 0.25
Outputs:
- block_output: bfloat16 [2, 4, 4, 512, 256], P('section', None, 'rep', 'dp')
- input_grad: bfloat16 [2, 4, 4, 512, 256], P('section', None, 'rep', 'dp')
- attn_gain_grad: float32 [2, 256], P('section')
- qkv_proj_grad: float32 [2, 256, 768], P('section')
- out_proj_grad: float32 [2, 256, 256], P('section')
- ffn_gain_grad: float32 [2, 256], P('section')
- up_proj_grad: float32 [2, 256, 1024], P('section')
- down_proj_grad: float32 [2, 1024, 256], P('section')
The draws below stay inside these ranges and needn't reach their ends.
Inputs may be any that keep to these rules, and one draw needn't show every extreme that they name: seq_lengths[m, g] lists in order the lengths of the 4 sequences packed from the start of line g of micro-batch m; their sum is at most 512 and the rest of the line is padding. In every g, one micro-batch, drawn from the seed, has a first sequence that starts at the line's first position and ends among its last 128 positions, followed by sequences of 1 to 32 positions; in line 0 that first sequence is 509 long. In the other micro-batches every sequence is 64 long or more and the line is at least half used.
All inputs are finite; a program needn't handle non-finite values.
Results may differ from the reference program's by a relative error of at most 0.02.
Values may be sent and summed in bfloat16 or wider, within the bound.
No kernel may reach another device: no remote copies, remote signals or barrier semaphores. Data moves between devices by JAX's collectives and lax.ppermute only.
A program may use at most 128 MiB of HBM per device.

```python
import jax
import jax.numpy as jnp
from jax import lax

D = 256
HEADS = 2
HEAD = 128
FF = 1024
STRIDE = 128
SEQS = 4
MB = 4
TOK_DEV = 128
GROUPS = 4
SPAN = 512
MIN_SEQ = 64


def draw_seq_lengths(key, part):
    key = jax.random.fold_in(key, 11)
    key_used, key_expo, key_tail, key_pick = jax.random.split(key, 4)
    used = jax.random.randint(key_used, (MB, GROUPS, 1), SPAN // 2, SPAN + 1)
    expo = jax.random.randint(key_expo, (MB, GROUPS, SEQS), 0, 7)
    weights = jnp.power(2, expo).astype(jnp.int32)
    spare = used - SEQS * MIN_SEQ
    normal_len = MIN_SEQ + spare * weights // jnp.sum(weights, axis=-1, keepdims=True)
    tail = jax.random.randint(key_tail, (MB, GROUPS, SEQS), 1, TOK_DEV // SEQS + 1)
    group_ids = jnp.arange(GROUPS, dtype=jnp.int32)[None, :, None]
    tail = jnp.where(group_ids == 0, 1, tail)
    slot = jnp.arange(SEQS, dtype=jnp.int32)
    tail = jnp.where(slot == 0, 0, tail)
    first_len = SPAN - jnp.sum(tail, axis=-1, keepdims=True)
    span_len = jnp.where(slot == 0, first_len, tail)
    chosen = jax.random.randint(key_pick, (1, GROUPS, 1), 0, MB)
    picked = jnp.arange(MB, dtype=jnp.int32)[:, None, None] == chosen
    return jnp.where(picked, span_len, normal_len).astype(jnp.int32)


def steps_of(own_key, shape, shards, smallest, top_value):
    def one(axis_at, shards_of):
        steps = jax.random.uniform(jax.random.fold_in(jax.random.fold_in(own_key, 6), axis_at), (shards_of,), jnp.float32, smallest / len(shards), top_value / len(shards))
        return jnp.repeat(jnp.exp(steps), shape[axis_at] // shards_of).reshape((-1,) + (1,) * (len(shape) - axis_at - 1))

    loudness = one(*shards[0])
    for cut in shards[1:]:
        loudness = loudness * one(*cut)
    return loudness


def normal_values(key, dims, deviation, reach, cuts=(), held_as=jnp.bfloat16):
    array = deviation * jax.random.normal(key, dims, jnp.float32)
    if cuts:
        array = array * steps_of(key, dims, cuts, -0.22, 0.18)
    return jnp.clip(array, -reach, reach).astype(held_as)


def setup_inputs(seed: int = 0) -> dict:
    arg_keys = jax.random.split(jax.random.key(seed), 10)
    return {
        "block_input": normal_values(arg_keys[0], (MB, GROUPS, SPAN, D), 1.0, 6.0, ((1, 4), (2, 4))),
        "output_grad": normal_values(arg_keys[1], (MB, GROUPS, SPAN, D), 1.0, 6.0, ((1, 4), (2, 4))),
        "seq_lengths": draw_seq_lengths(jax.random.fold_in(arg_keys[9], 71), 0),
        "attn_gain": jnp.clip(1.0 + 0.1 * jax.random.normal(arg_keys[3], (2, D), jnp.float32), 0.5, 1.5).astype(jnp.bfloat16),
        "qkv_proj": normal_values(arg_keys[4], (2, D, 3 * D), (D // 2) ** -0.5, 0.5, ((0, 2),)),
        "out_proj": normal_values(arg_keys[5], (2, D, D), (D // 8) ** -0.5, 1.0, ((0, 2),)),
        "ffn_gain": jnp.clip(1.0 + 0.1 * jax.random.normal(arg_keys[6], (2, D), jnp.float32), 0.5, 1.5).astype(jnp.bfloat16),
        "up_proj": normal_values(arg_keys[7], (2, D, FF), D ** -0.5, 0.375, ((0, 2),)),
        "down_proj": normal_values(arg_keys[8], (2, FF, D), (FF // 2) ** -0.5, 0.25, ((0, 2),)),
    }


HIGHEST = lax.Precision.HIGHEST
NEG = -1e+30

@jax.custom_vjp
def low(v):
    return lax.optimization_barrier(v.astype(jnp.bfloat16)).astype(jnp.float32)

@jax.custom_vjp
def low_back(v):
    return v

def low_keep(v):
    return (low(v), None)

def low_pass(kept, grad):
    return (grad,)

def back_keep(v):
    return (v, None)

def back_low(kept, grad):
    return (low(grad),)
low.defvjp(low_keep, low_pass)
low_back.defvjp(back_keep, back_low)

def rounded(values):
    return low_back(low(values))

def normalize(values):
    centered = values - lax.optimization_barrier(jnp.mean(values, axis=-1, keepdims=True))
    spread = lax.optimization_barrier(jnp.mean(centered * centered, axis=-1, keepdims=True))
    return centered * lax.rsqrt(spread + 1e-05)

def allowed(query_pos, query_seg, key_pos, key_seg, strided):
    offset = query_pos - key_pos
    same_seq = (query_seg == key_seg) & (query_seg < SEQS)
    if strided:
        pattern = (offset >= 0) & (offset % STRIDE == 0)
    else:
        pattern = (offset >= 0) & (offset < STRIDE)
    return same_seq & pattern | (offset == 0)

def apply_layer(hidden, segments, params, strided):
    attn_gain, qkv_proj, out_proj, ffn_gain, up_proj, down_proj = params
    normed = low(normalize(hidden) * attn_gain)
    packed = rounded(jnp.dot(normed, qkv_proj, precision=HIGHEST))
    queries = packed[:, :D].reshape(SPAN, HEADS, HEAD)
    key_rows = packed[:, D:2 * D].reshape(SPAN, HEADS, HEAD)
    values = packed[:, 2 * D:].reshape(SPAN, HEADS, HEAD)
    key_pos = jnp.arange(SPAN, dtype=jnp.int32)
    block_rows = min(512, SPAN)

    def query_block(first_row):
        block_queries = lax.dynamic_slice_in_dim(queries, first_row, block_rows, 0)
        query_pos = first_row + jnp.arange(block_rows, dtype=jnp.int32)
        query_seg = lax.dynamic_slice_in_dim(segments, first_row, block_rows, 0)
        allow_mask = allowed(query_pos[:, None], query_seg[:, None], key_pos[None, :], segments[None, :], strided)
        scores = low_back(jnp.einsum('qhe,khe->hqk', block_queries, key_rows, precision=HIGHEST) * HEAD ** (-0.5))
        scores = jnp.where(allow_mask[None], scores, NEG)
        attn_probs = low(jax.nn.softmax(scores, axis=-1))
        return jnp.einsum('hqk,khe->qhe', attn_probs, values, precision=HIGHEST).reshape(block_rows, D)
    starts = jnp.arange(SPAN // block_rows, dtype=jnp.int32) * block_rows
    attended = rounded(lax.map(jax.checkpoint(query_block), starts).reshape(SPAN, D))
    middle = hidden + jnp.dot(attended, out_proj, precision=HIGHEST)
    second = low(normalize(middle) * ffn_gain)
    pre_act = low_back(jnp.dot(second, up_proj, precision=HIGHEST))
    active = low(jax.nn.gelu(pre_act, approximate=False))
    return middle + jnp.dot(active, down_proj, precision=HIGHEST)

def reference(block_input, output_grad, seq_lengths, attn_gain, qkv_proj, out_proj, ffn_gain, up_proj, down_proj):
    seq_ends = jnp.cumsum(seq_lengths, axis=-1)
    positions = jnp.arange(SPAN, dtype=jnp.int32)
    segments = lax.optimization_barrier(jnp.sum((positions[None, None, :, None] >= seq_ends[:, :, None, :]).astype(jnp.int32), axis=-1))
    segments = segments.reshape(MB * GROUPS, SPAN)
    inputs = block_input.astype(jnp.float32).reshape(MB * GROUPS, SPAN, D)
    stacked = tuple((weight.astype(jnp.float32) for weight in (attn_gain, qkv_proj, out_proj, ffn_gain, up_proj, down_proj)))
    layer_zero = tuple((weight[0] for weight in stacked))
    layer_one = tuple((weight[1] for weight in stacked))

    def run_layer(hidden_lines, params, strided):

        def one_line(line_pair):
            return apply_layer(line_pair[0], line_pair[1], params, strided)
        return lax.map(jax.checkpoint(one_line), (hidden_lines, segments))

    def forward(inputs, layer_zero, layer_one, bump_zero):
        middle = run_layer(inputs, layer_zero, False)
        carried = rounded(middle) + bump_zero
        return (run_layer(carried, layer_one, True), middle)
    bump_zero = jnp.zeros_like(inputs)
    final_out, pullback, middle = jax.vjp(forward, inputs, layer_zero, layer_one, bump_zero, has_aux=True)
    cotangent = output_grad.astype(jnp.float32).reshape(MB * GROUPS, SPAN, D)
    grad_inputs, grad_zero, grad_one, grad_bump = pullback(cotangent)
    out_shape = (2, MB, GROUPS, SPAN, D)
    block_output = jnp.stack([middle, final_out]).reshape(out_shape).astype(jnp.bfloat16)
    input_grad = jnp.stack([grad_inputs, grad_bump]).reshape(out_shape).astype(jnp.bfloat16)
    grads = tuple((jnp.stack([grad_a, grad_b]) for grad_a, grad_b in zip(grad_zero, grad_one)))
    return (block_output, input_grad, grads[0], grads[1], grads[2], grads[3], grads[4], grads[5])
```

```python
from functools import partial

import jax
import jax.numpy as jnp
from jax import lax
from jax.experimental import pallas as pl
from jax.experimental.pallas import tpu as pltpu
from jax.sharding import PartitionSpec as P

HEADS = 2
STRIDE = 128


NEG = -1e30


def from_behind(shard, axis, by):
    length = lax.axis_size(axis)
    pairs = [(i, i + by) for i in range(length) if 0 <= i + by < length]
    return lax.ppermute(shard, axis, pairs)


def normalize(values):
    centered = values - jnp.mean(values, axis=-1, keepdims=True)
    spread = jnp.mean(centered * centered, axis=-1, keepdims=True)
    return centered * lax.rsqrt(spread + 1e-05)


def gained(values, gain):
    return normalize(values) * gain


def allowed(query_pos, query_seg, key_pos, key_seg, strided, seq_slots):
    offset = query_pos - key_pos
    same_seq = (query_seg == key_seg) & (query_seg < seq_slots)
    nearby = (offset >= 0) & (offset < STRIDE)
    spaced = (offset >= 0) & (offset % STRIDE == 0)
    pattern = jnp.where(strided, spaced, nearby)
    return same_seq & pattern | (offset == 0)


def product(left, right):
    return jnp.dot(left, right, preferred_element_type=jnp.float32)


def contract_rows(left, right):
    return lax.dot_general(
        left, right, (((0,), (0,)), ((), ())), preferred_element_type=jnp.float32
    )


def contract_cols(left, right):
    return lax.dot_general(
        left, right, (((1,), (1,)), ((), ())), preferred_element_type=jnp.float32
    )


def put_row(buffer, value, slot_index, is_valid):
    current = lax.dynamic_index_in_dim(buffer, slot_index, 0, keepdims=False)
    return lax.dynamic_update_index_in_dim(
        buffer, jnp.where(is_valid, value, current), slot_index, 0
    )


def softmax_parts(scores):
    row_max = jnp.max(scores, axis=-1, keepdims=True)
    shifted = jnp.exp(scores - row_max)
    row_total = jnp.sum(shifted, axis=-1, keepdims=True)
    return ((shifted / row_total).astype(jnp.bfloat16), (row_max + jnp.log(row_total))[..., 0])


def general(
    block_input,
    output_grad,
    seq_lengths,
    attn_gain,
    qkv_proj,
    out_proj,
    ffn_gain,
    up_proj,
    down_proj,
):
    section_index = lax.axis_index("section")
    line_row = lax.axis_index("dp")
    group_index = lax.axis_index("rep")
    strided = section_index == 1
    micro_count, _, tok_rows, model_width = block_input.shape
    line_count = lax.axis_size("dp")
    line_span = tok_rows * line_count
    head_size = model_width // HEADS
    score_scale = float(head_size) ** (-0.5)
    seq_slots = seq_lengths.shape[-1]
    block_count = line_span // STRIDE
    residues = STRIDE // line_count
    line_lengths = lax.dynamic_index_in_dim(seq_lengths, group_index, 1, keepdims=False)
    all_pos = jnp.arange(line_span, dtype=jnp.int32)
    my_pos = line_row * tok_rows + jnp.arange(tok_rows, dtype=jnp.int32)
    win_pos = line_row * tok_rows - tok_rows + jnp.arange(2 * tok_rows, dtype=jnp.int32)
    res_pos = (
        jnp.arange(block_count, dtype=jnp.int32)[None, :] * STRIDE
        + line_row * residues
        + jnp.arange(residues, dtype=jnp.int32)[:, None]
    )
    gain_attn = attn_gain[0].astype(jnp.float32)
    gain_ffn = ffn_gain[0].astype(jnp.float32)
    w_qkv = qkv_proj[0]
    w_out = out_proj[0]
    w_up = up_proj[0]
    w_down = down_proj[0]

    def segments_of(slot_index):
        seq_ends = jnp.cumsum(lax.dynamic_index_in_dim(line_lengths, slot_index, 0, keepdims=False))
        all_seg = jnp.sum((all_pos[:, None] >= seq_ends[None, :]).astype(jnp.int32), axis=1)
        my_seg = lax.dynamic_slice_in_dim(all_seg, line_row * tok_rows, tok_rows)
        padded = jnp.concatenate([jnp.full((tok_rows,), seq_slots, jnp.int32), all_seg])
        win_seg = lax.dynamic_slice_in_dim(padded, line_row * tok_rows, 2 * tok_rows)
        res_seg = lax.dynamic_slice_in_dim(
            all_seg.reshape(block_count, STRIDE), line_row * residues, residues, 1
        ).T
        dense_mask = allowed(
            my_pos[:, None], my_seg[:, None], all_pos[None, :], all_seg[None, :], strided, seq_slots
        )
        win_mask = allowed(
            my_pos[:, None], my_seg[:, None], win_pos[None, :], win_seg[None, :], False, seq_slots
        )
        res_mask = allowed(
            res_pos[:, :, None],
            res_seg[:, :, None],
            res_pos[:, None, :],
            res_seg[:, None, :],
            True,
            seq_slots,
        )
        return (all_seg, my_seg, dense_mask, win_mask, res_mask)

    def project(hidden):
        normed = gained(hidden, gain_attn).astype(jnp.bfloat16)
        packed = product(normed, w_qkv).astype(jnp.bfloat16)
        return (normed, packed)

    def finish(hidden, attended):
        middle = hidden + product(attended, w_out)
        second = gained(middle, gain_ffn).astype(jnp.bfloat16)
        pre_act = product(second, w_up)
        active = jax.nn.gelu(pre_act, approximate=False).astype(jnp.bfloat16)
        return (middle, second, pre_act, active, middle + product(active, w_down))

    def dense_backward(packed, grad_att, lse_now, masks):
        all_seg, my_seg, dense_mask = (masks[0], masks[1], masks[2])
        queries = packed[:, :model_width]
        key_rows = packed[:, model_width : 2 * model_width]
        values = packed[:, 2 * model_width :]
        keys_all, values_all = (
            lax.all_gather(key_rows, "dp", axis=0, tiled=True),
            lax.all_gather(values, "dp", axis=0, tiled=True),
        )
        grad_q_heads = []
        grad_k_heads = []
        grad_v_heads = []
        delta_heads = []
        for head_index in range(HEADS):
            columns = slice(head_index * head_size, (head_index + 1) * head_size)
            query_head = queries[:, columns]
            out_head = grad_att[:, columns]
            scores = jnp.where(
                dense_mask, contract_cols(query_head, keys_all[:, columns]) * score_scale, NEG
            )
            attn_probs = jnp.exp(scores - lse_now[head_index][:, None])
            grad_probs = contract_cols(out_head, values_all[:, columns])
            delta_row = jnp.sum(attn_probs * grad_probs, axis=1)
            grad_scores = (attn_probs * (grad_probs - delta_row[:, None])).astype(jnp.bfloat16)
            grad_q_heads.append(product(grad_scores, keys_all[:, columns]) * score_scale)
            delta_heads.append(delta_row)
            key_part = contract_rows(grad_scores, query_head) * score_scale
            value_part = contract_rows(attn_probs.astype(jnp.bfloat16), out_head)
            key_mine, value_mine = (
                lax.psum_scatter(
                    key_part.astype(jnp.bfloat16), "dp", scatter_dimension=0, tiled=True
                ).astype(jnp.float32),
                lax.psum_scatter(
                    value_part.astype(jnp.bfloat16), "dp", scatter_dimension=0, tiled=True
                ).astype(jnp.float32),
            )
            grad_k_heads.append(key_mine)
            grad_v_heads.append(value_mine)
        return jnp.concatenate(
            [
                jnp.concatenate(grad_q_heads, axis=1).astype(jnp.bfloat16),
                jnp.concatenate(grad_k_heads, axis=1).astype(jnp.bfloat16),
                jnp.concatenate(grad_v_heads, axis=1).astype(jnp.bfloat16),
            ],
            axis=1,
        )

    received = jnp.zeros((tok_rows, model_width), jnp.bfloat16)
    saved_in = jnp.zeros((micro_count, tok_rows, model_width), jnp.bfloat16)
    saved_att = jnp.zeros((micro_count, tok_rows, model_width), jnp.bfloat16)
    saved_lse = jnp.zeros((micro_count, HEADS, tok_rows), jnp.float32)
    results = jnp.zeros((micro_count, tok_rows, model_width), jnp.bfloat16)
    for tick_index in range(micro_count + 1):
        slot_raw = tick_index - section_index
        is_valid = (slot_raw >= 0) & (slot_raw < micro_count)
        slot_index = jnp.clip(slot_raw, 0, micro_count - 1)
        hidden_low = jnp.where(
            section_index == 0, block_input[min(tick_index, micro_count - 1), 0], received
        )
        hidden = hidden_low.astype(jnp.float32)
        normed, packed = project(hidden)
        masks = segments_of(slot_index)
        dense_dense_mask = masks[2]
        dense_keys_all = lax.all_gather(
            packed[:, model_width : 2 * model_width], "dp", axis=0, tiled=True
        )
        dense_values_all = lax.all_gather(packed[:, 2 * model_width :], "dp", axis=0, tiled=True)
        head_outs = []
        head_lse = []
        for dense_head_index in range(HEADS):
            dense_columns = slice(dense_head_index * head_size, (dense_head_index + 1) * head_size)
            dense_scores = jnp.where(
                dense_dense_mask,
                contract_cols(packed[:, dense_columns], dense_keys_all[:, dense_columns])
                * score_scale,
                NEG,
            )
            dense_attn_probs, lse_row = softmax_parts(dense_scores)
            head_outs.append(product(dense_attn_probs, dense_values_all[:, dense_columns]))
            head_lse.append(lse_row)
        attended = jnp.concatenate(head_outs, axis=1).astype(jnp.bfloat16)
        lse_rows = jnp.stack(head_lse)
        output = finish(hidden, attended)[4].astype(jnp.bfloat16)
        saved_in = put_row(saved_in, hidden_low, slot_index, is_valid)
        saved_att = put_row(saved_att, attended, slot_index, is_valid)
        saved_lse = put_row(saved_lse, lse_rows, slot_index, is_valid)
        results = put_row(results, output, slot_index, is_valid)
        if tick_index < micro_count:
            received = from_behind(output, "section", 1)
    totals = (
        jnp.zeros((model_width,), jnp.float32),
        jnp.zeros(w_qkv.shape, jnp.float32),
        jnp.zeros(w_out.shape, jnp.float32),
        jnp.zeros((model_width,), jnp.float32),
        jnp.zeros(w_up.shape, jnp.float32),
        jnp.zeros(w_down.shape, jnp.float32),
    )
    sent_back = jnp.zeros((tok_rows, model_width), jnp.bfloat16)
    input_grads = jnp.zeros((micro_count, tok_rows, model_width), jnp.bfloat16)
    for tick_index in range(micro_count + 1):
        slot_raw = tick_index - (1 - section_index)
        is_valid = (slot_raw >= 0) & (slot_raw < micro_count)
        slot_index = jnp.clip(slot_raw, 0, micro_count - 1)
        grad_out = jnp.where(
            section_index == 1, output_grad[min(tick_index, micro_count - 1), 0], sent_back
        )
        hidden = lax.dynamic_index_in_dim(saved_in, slot_index, 0, keepdims=False).astype(
            jnp.float32
        )
        attended = lax.dynamic_index_in_dim(saved_att, slot_index, 0, keepdims=False)
        lse_now = lax.dynamic_index_in_dim(saved_lse, slot_index, 0, keepdims=False)
        normed, packed = project(hidden)
        middle, second, pre_act, active, _ = finish(hidden, attended)
        grad_down = contract_rows(active, grad_out)
        grad_active = contract_cols(grad_out, w_down)
        gelu_back = jax.vjp(partial(jax.nn.gelu, approximate=False), pre_act)[1]
        grad_pre = gelu_back(grad_active)[0].astype(jnp.bfloat16)
        grad_up = contract_rows(second, grad_pre)
        ffn_back = jax.vjp(gained, middle, gain_ffn)[1]
        grad_mid_norm, grad_gain_ffn = ffn_back(contract_cols(grad_pre, w_up))
        grad_middle = grad_out.astype(jnp.float32) + grad_mid_norm
        grad_branch = grad_middle.astype(jnp.bfloat16)
        grad_outproj = contract_rows(attended, grad_branch)
        grad_att = contract_cols(grad_branch, w_out).astype(jnp.bfloat16)
        masks = segments_of(slot_index)
        grad_packed = dense_backward(packed, grad_att, lse_now, masks)
        grad_qkv = contract_rows(normed, grad_packed)
        attn_back = jax.vjp(gained, hidden, gain_attn)[1]
        grad_hid_norm, grad_gain_attn = attn_back(contract_cols(grad_packed, w_qkv))
        grad_hidden = (grad_middle + grad_hid_norm).astype(jnp.bfloat16)
        terms = (grad_gain_attn, grad_qkv, grad_outproj, grad_gain_ffn, grad_up, grad_down)
        totals = tuple(
            (
                running + jnp.where(is_valid, term_now, 0.0)
                for running, term_now in zip(totals, terms)
            )
        )
        input_grads = put_row(input_grads, grad_hidden, slot_index, is_valid)
        if tick_index < micro_count:
            sent_back = from_behind(grad_hidden, "section", -1)
    summed = lax.psum(
        (totals[0], totals[1], totals[2], totals[3], totals[4], totals[5]), ("dp", "rep")
    )
    return (
        results[None, :, None],
        input_grads[None, :, None],
        summed[0][None],
        summed[1][None],
        summed[2][None],
        summed[3][None],
        summed[4][None],
        summed[5][None],
    )


BF = jnp.bfloat16
F32 = jnp.float32
VMEM_BYTES = 56 * 1024 * 1024


def vmem_call(body, out_shape, scratch=(), in_specs=None, out_specs=None):
    return pl.pallas_call(
        body,
        out_shape=out_shape,
        in_specs=in_specs,
        out_specs=out_specs,
        scratch_shapes=list(scratch),
        compiler_params=pltpu.CompilerParams(vmem_limit_bytes=VMEM_BYTES),
    )


def smem():
    return pl.BlockSpec(memory_space=pltpu.SMEM)


def vmem():
    return pl.BlockSpec(memory_space=pltpu.VMEM)


def anywhere():
    return pl.BlockSpec(memory_space=pl.ANY)


SEC, ZED, REP, FLIP = 0, 1, 2, 3


def pack_kernel(info, tokens, grads, *pieces):
    half = tokens.shape[1] // 2
    rows = pl.ds(pl.multiple_of(info[SEC] * half, half), half)
    for step, piece in enumerate(pieces):
        micro = info[ZED] ^ step
        piece[:half, :] = tokens[micro, rows, :]
        piece[half:, :] = grads[micro, rows, :]


def unit(values):
    centered = values - jnp.mean(values, axis=-1, keepdims=True)
    inverse = lax.rsqrt(jnp.mean(centered * centered, axis=-1, keepdims=True) + 1e-05)
    return centered * inverse, inverse


def unit_back(grad, normal, inverse):
    return inverse * (
        grad
        - jnp.mean(grad, axis=-1, keepdims=True)
        - normal * jnp.mean(grad * normal, axis=-1, keepdims=True)
    )


def segment_at(ends, position):
    total = jnp.zeros(position.shape, jnp.int32)
    for end in ends:
        total = total + (position >= end).astype(jnp.int32)
    return total


def step_kernel(
    info,
    lengths,
    own0,
    own1,
    own2,
    own3,
    far0,
    far1,
    far2,
    far3,
    gain_attn_own,
    gain_ffn_own,
    gain_attn_far,
    gain_ffn_far,
    qkv_own,
    out_own,
    up_own,
    down_own,
    qkv_far,
    out_far,
    up_far,
    down_far,
    result_keep,
    result_send,
    grad_in_one,
    grad_in_zero,
    ffn_keep,
    ffn_send,
    attn_keep,
    attn_send,
    w_qkv,
    w_out,
    w_up,
    w_down,
    ffn_terms,
    attn_terms,
    line,
    mine,
    cotangent,
    normal_all,
    normed_all,
    padded,
    probs_window,
    probs_strided,
    active,
    slope,
    middle_unit,
    normal_one,
    normed_one,
    packed_one,
    query_zero,
    grad_padded,
    in_sems,
    out_sems,
):
    section = info[SEC]
    half = own0.shape[0] // 2
    width = own0.shape[1]
    blocks = 4
    span = line.shape[0]
    block = span // blocks
    rows = half * blocks
    head = width // HEADS
    hidden_units = w_up.shape[2]
    scale = float(head) ** (-0.5)
    other = 1 - section
    loads = []
    for index, (near, far, held) in enumerate(
        (
            (qkv_own, qkv_far, w_qkv),
            (out_own, out_far, w_out),
            (up_own, up_far, w_up),
            (down_own, down_far, w_down),
        )
    ):
        pair = (
            pltpu.make_async_copy(near, held.at[section], in_sems.at[2 * index]),
            pltpu.make_async_copy(far, held.at[other], in_sems.at[2 * index + 1]),
        )
        for copy in pair:
            copy.start()
        loads.append(pair)

    def arrive(index):
        for copy in loads[index]:
            copy.wait()

    def gain_of(near, far, layer):
        return jnp.where(section == layer, near[...], far[...]).astype(F32)

    gain_attn = [gain_of(gain_attn_own, gain_attn_far, layer) for layer in range(2)]
    gain_ffn = [gain_of(gain_ffn_own, gain_ffn_far, layer) for layer in range(2)]

    for step, (near, far) in enumerate(((own0, far0), (own1, far1), (own2, far2), (own3, far3))):
        spot = info[ZED] ^ step
        base = spot * block
        near_rows = pl.ds(pl.multiple_of(base + section * half, half), half)
        far_rows = pl.ds(pl.multiple_of(base + other * half, half), half)
        mine_rows = pl.ds(pl.multiple_of(spot * half, half), half)
        line[near_rows, :] = near[:half, :]
        line[far_rows, :] = far[:half, :]
        mine[mine_rows, :] = near[:half, :]
        cotangent[mine_rows, :] = near[half:, :]

    ends = []
    so_far = jnp.int32(0)
    for slot in range(lengths.shape[2]):
        so_far = so_far + lengths[info[ZED], info[REP], slot]
        ends.append(so_far)
    slots = len(ends)

    hidden_all = line[...].astype(F32)
    normal, inverse_all = unit(hidden_all)
    normal_all[...] = normal
    normed_all[...] = (normal * gain_attn[0]).astype(BF)
    arrive(0)

    def mine_of(ref, spot, columns=slice(None)):
        start = pl.multiple_of(block * spot + section * half, half)
        return ref[pl.ds(start, half), columns]

    normed_mine = jnp.concatenate([mine_of(normed_all, spot) for spot in range(blocks)], axis=0)
    query_zero[...] = product(normed_mine, w_qkv[0, :, :width]).astype(BF)
    padded[:block, :] = jnp.zeros((block, 2 * width), BF)
    padded[block:, :] = product(normed_all[...], w_qkv[0, :, width:]).astype(BF)
    reach = block + half

    def window(spot):
        return pl.ds(pl.multiple_of(block * spot + section * half, half), reach)

    def window_mask(spot):
        first = block * spot + section * half
        query_pos = first + lax.broadcasted_iota(jnp.int32, (half, reach), 0)
        key_pos = first - block + lax.broadcasted_iota(jnp.int32, (half, reach), 1)
        offset = query_pos - key_pos
        segment = segment_at(ends, query_pos)
        same = (segment == segment_at(ends, key_pos)) & (segment < slots) & (key_pos >= 0)
        return same & (offset >= 0) & (offset < STRIDE) | (offset == 0)

    attended_parts = []
    for spot in range(blocks):
        mask = window_mask(spot)
        spot_parts = []
        for number in range(HEADS):
            columns = slice(number * head, (number + 1) * head)
            value_columns = slice(width + number * head, width + (number + 1) * head)
            scores = contract_cols(
                query_zero[spot * half : (spot + 1) * half, columns], padded[window(spot), columns]
            )
            scores = jnp.where(mask, scores * scale, NEG)
            shifted = jnp.exp(scores - jnp.max(scores, axis=-1, keepdims=True))
            probs = shifted / jnp.sum(shifted, axis=-1, keepdims=True)
            probs_window[spot * HEADS + number] = probs
            spot_parts.append(product(probs.astype(BF), padded[window(spot), value_columns]))
        attended_parts.append(jnp.concatenate(spot_parts, axis=1).astype(BF))
    attended_zero = jnp.concatenate(attended_parts, axis=0)
    chunk = width
    chunks = hidden_units // chunk

    def ffn_forward(layer, hidden, attended):
        middle = hidden + product(attended, w_out[layer])
        normal, inverse = unit(middle)
        middle_unit[layer] = normal
        second = (normal * gain_ffn[layer]).astype(BF)
        result = middle
        for index in range(chunks):
            columns = slice(index * chunk, (index + 1) * chunk)
            pre_act = product(second, w_up[layer, :, columns])
            below = 0.5 + 0.5 * lax.erf(pre_act * (0.5**0.5))
            now = (pre_act * below).astype(BF)
            active[layer, :, columns] = now
            slope[layer, :, columns] = below + pre_act * (
                jnp.exp(-0.5 * pre_act * pre_act) * 0.3989422804014327
            )
            result = result + product(now, w_down[layer, columns, :])
        return result.astype(BF), second, inverse

    arrive(1)
    arrive(2)
    arrive(3)
    result_zero, second_zero, inverse_mid_zero = ffn_forward(
        0, mine[...].astype(F32), attended_zero
    )

    hidden = result_zero.astype(F32)
    normal, inverse_one = unit(hidden)
    normal_one[...] = normal
    normed_one[...] = (normal * gain_attn[1]).astype(BF)
    packed_one[...] = product(normed_one[...], w_qkv[1]).astype(BF)

    def place(axis, shape):
        index = lax.broadcasted_iota(jnp.int32, shape, axis)
        return block * (index // half) + section * half + (index & (half - 1))

    query_pos = place(0, (rows, rows))
    key_pos = place(1, (rows, rows))
    offset = query_pos - key_pos
    segment = segment_at(ends, query_pos)
    same = (segment == segment_at(ends, key_pos)) & (segment < slots)
    strided_mask = same & (offset >= 0) & ((offset & (STRIDE - 1)) == 0) | (offset == 0)
    attended_parts = []
    for number in range(HEADS):
        columns = slice(number * head, (number + 1) * head)
        key_columns = slice(width + number * head, width + (number + 1) * head)
        value_columns = slice(2 * width + number * head, 2 * width + (number + 1) * head)
        scores = contract_cols(packed_one[:, columns], packed_one[:, key_columns])
        scores = jnp.where(strided_mask, scores * scale, NEG)
        shifted = jnp.exp(scores - jnp.max(scores, axis=-1, keepdims=True))
        probs = shifted / jnp.sum(shifted, axis=-1, keepdims=True)
        probs_strided[number] = probs
        attended_parts.append(product(probs.astype(BF), packed_one[:, value_columns]))
    attended_one = jnp.concatenate(attended_parts, axis=1).astype(BF)
    result_one, second_one, inverse_mid_one = ffn_forward(1, hidden, attended_one)

    result_keep[...] = jnp.where(section == 0, result_zero, result_one)
    result_send[...] = jnp.where(section == 0, result_one, result_zero)

    def ffn_backward(layer, grad_out, second, inverse, attended):
        side, flip = section ^ layer, info[FLIP + layer]
        grad_second = None
        for index in range(chunks):
            columns = slice(index * chunk, (index + 1) * chunk)
            grad_active = contract_cols(grad_out, w_down[layer, columns, :])
            grad_pre = (grad_active * slope[layer, :, columns]).astype(BF)
            quarter, part = index // 2, index % 2
            spread = slice(part * chunk, (part + 1) * chunk)
            ffn_terms[side, flip ^ quarter, spread, :] = contract_rows(second, grad_pre).astype(BF)
            ffn_terms[side, flip ^ (quarter + 2), spread, :] = contract_rows(
                active[layer, :, columns], grad_out
            ).astype(BF)
            term = contract_cols(grad_pre, w_up[layer, :, columns])
            grad_second = term if grad_second is None else grad_second + term
        normal = middle_unit[layer]
        gain_term = jnp.sum(grad_second * normal, axis=0, keepdims=True)
        grad_middle = grad_out.astype(F32) + unit_back(
            grad_second * gain_ffn[layer], normal, inverse
        )
        grad_branch = grad_middle.astype(BF)
        attn_terms[side, flip ^ 3, :width, :] = contract_rows(attended, grad_branch).astype(BF)
        grad_att = contract_cols(grad_branch, w_out[layer]).astype(BF)
        return grad_middle, grad_att, gain_term

    def store_gains(layer, attn_term, ffn_term):
        side, flip = section ^ layer, info[FLIP + layer]
        rest = attn_terms.shape[2] - width
        spare = jnp.concatenate([attn_term, ffn_term, jnp.zeros((rest - 2, width), F32)], axis=0)
        for quarter in range(4):
            attn_terms[side, flip ^ quarter, width:, :] = spare.astype(BF)

    def outward(terms, keep, send, index):
        pair = (
            pltpu.make_async_copy(terms.at[0], keep, out_sems.at[index]),
            pltpu.make_async_copy(terms.at[1], send, out_sems.at[index + 1]),
        )
        for copy in pair:
            copy.start()
        return pair

    grad_middle, grad_att, ffn_term = ffn_backward(
        1, cotangent[...], second_one, inverse_mid_one, attended_one
    )
    side, flip = section ^ 1, info[FLIP + 1]
    grad_parts = [[], [], []]
    for number in range(HEADS):
        columns = slice(number * head, (number + 1) * head)
        key_columns = slice(width + number * head, width + (number + 1) * head)
        value_columns = slice(2 * width + number * head, 2 * width + (number + 1) * head)
        probs = probs_strided[number]
        grad_here = grad_att[:, columns]
        grad_probs = contract_cols(grad_here, packed_one[:, value_columns])
        delta = jnp.sum(probs * grad_probs, axis=-1, keepdims=True)
        grad_scores = (probs * (grad_probs - delta)).astype(BF)
        grad_parts[0].append(product(grad_scores, packed_one[:, key_columns]) * scale)
        grad_parts[1].append(contract_rows(grad_scores, packed_one[:, columns]) * scale)
        grad_parts[2].append(contract_rows(probs.astype(BF), grad_here))
    grad_normed = None
    for index in range(3):
        columns = slice(index * width, (index + 1) * width)
        grad_block = jnp.concatenate(grad_parts[index], axis=1).astype(BF)
        attn_terms[side, flip ^ index, :width, :] = contract_rows(
            normed_one[...], grad_block
        ).astype(BF)
        term = contract_cols(grad_block, w_qkv[1, :, columns])
        grad_normed = term if grad_normed is None else grad_normed + term
    normal = normal_one[...]
    store_gains(1, jnp.sum(grad_normed * normal, axis=0, keepdims=True), ffn_term)
    grad_in = (
        grad_middle + unit_back(grad_normed * gain_attn[1], normal, inverse_one)
    ).astype(BF)
    grad_in_one[...] = grad_in

    grad_middle, grad_att, ffn_term = ffn_backward(
        0, grad_in, second_zero, inverse_mid_zero, attended_zero
    )
    ffn_out = outward(ffn_terms, ffn_keep, ffn_send, 0)
    side, flip = section, info[FLIP]
    grad_padded[...] = jnp.zeros(grad_padded.shape, F32)
    grad_query_parts = []
    for spot in range(blocks):
        spot_parts = []
        for number in range(HEADS):
            columns = slice(number * head, (number + 1) * head)
            value_columns = slice(width + number * head, width + (number + 1) * head)
            probs = probs_window[spot * HEADS + number]
            grad_here = grad_att[spot * half : (spot + 1) * half, columns]
            query_here = query_zero[spot * half : (spot + 1) * half, columns]
            grad_probs = contract_cols(grad_here, padded[window(spot), value_columns])
            delta = jnp.sum(probs * grad_probs, axis=-1, keepdims=True)
            grad_scores = (probs * (grad_probs - delta)).astype(BF)
            spot_parts.append(product(grad_scores, padded[window(spot), columns]) * scale)
            grad_padded[window(spot), columns] += contract_rows(grad_scores, query_here) * scale
            grad_padded[window(spot), value_columns] += contract_rows(probs.astype(BF), grad_here)
        grad_query_parts.append(jnp.concatenate(spot_parts, axis=1))
    grad_query = jnp.concatenate(grad_query_parts, axis=0).astype(BF)
    attn_terms[side, flip ^ 0, :width, :] = contract_rows(normed_mine, grad_query).astype(BF)
    grad_keys = grad_padded[block:, :width].astype(BF)
    grad_values = grad_padded[block:, width:].astype(BF)
    attn_terms[side, flip ^ 1, :width, :] = contract_rows(normed_all[...], grad_keys).astype(BF)
    attn_terms[side, flip ^ 2, :width, :] = contract_rows(normed_all[...], grad_values).astype(BF)
    grad_in_zero[...] = contract_cols(grad_keys, w_qkv[0, :, width : 2 * width]) + contract_cols(
        grad_values, w_qkv[0, :, 2 * width :]
    )
    from_query = contract_cols(grad_query, w_qkv[0, :, :width])
    for spot in range(blocks):
        here = pl.ds(pl.multiple_of(block * spot + section * half, half), half)
        grad_in_zero[here, :] += from_query[spot * half : (spot + 1) * half, :]
    grad_normed = grad_in_zero[...]
    normal = normal_all[...]
    store_gains(0, jnp.sum(grad_normed * normal, axis=0, keepdims=True), ffn_term)
    attn_out = outward(attn_terms, attn_keep, attn_send, 2)
    grad_in_zero[...] = unit_back(grad_normed * gain_attn[0], normal, inverse_all)
    for spot in range(blocks):
        here = pl.ds(pl.multiple_of(block * spot + section * half, half), half)
        grad_in_zero[here, :] += grad_middle[spot * half : (spot + 1) * half, :]
    for copy in (*ffn_out, *attn_out):
        copy.wait()


def run_step(info, seq_lengths, near, far, gains, weights):
    width = near[0].shape[1]
    half = near[0].shape[0] // 2
    blocks = len(near)
    rows = blocks * half
    span = 2 * rows
    block = span // blocks
    hidden_units = weights[2].shape[1]
    shape = jax.ShapeDtypeStruct
    ffn_rows = 2 * hidden_units // 4
    attn_rows = width + 16
    outs = (
        shape((rows, width), BF),
        shape((rows, width), BF),
        shape((rows, width), BF),
        shape((span, width), F32),
        shape((4, ffn_rows, width), BF),
        shape((4, ffn_rows, width), BF),
        shape((4, attn_rows, width), BF),
        shape((4, attn_rows, width), BF),
    )
    scratch = (
        pltpu.VMEM((2, width, 3 * width), BF),
        pltpu.VMEM((2, width, width), BF),
        pltpu.VMEM((2, width, hidden_units), BF),
        pltpu.VMEM((2, hidden_units, width), BF),
        pltpu.VMEM((2, 4, ffn_rows, width), BF),
        pltpu.VMEM((2, 4, attn_rows, width), BF),
        pltpu.VMEM((span, width), BF),
        pltpu.VMEM((rows, width), BF),
        pltpu.VMEM((rows, width), BF),
        pltpu.VMEM((span, width), F32),
        pltpu.VMEM((span, width), BF),
        pltpu.VMEM((block + span, 2 * width), BF),
        pltpu.VMEM((blocks * HEADS, half, block + half), F32),
        pltpu.VMEM((HEADS, rows, rows), F32),
        pltpu.VMEM((2, rows, hidden_units), BF),
        pltpu.VMEM((2, rows, hidden_units), F32),
        pltpu.VMEM((2, rows, width), F32),
        pltpu.VMEM((rows, width), F32),
        pltpu.VMEM((rows, width), BF),
        pltpu.VMEM((rows, 3 * width), BF),
        pltpu.VMEM((rows, width), BF),
        pltpu.VMEM((block + span, 2 * width), F32),
        pltpu.SemaphoreType.DMA((8,)),
        pltpu.SemaphoreType.DMA((4,)),
    )
    return vmem_call(
        step_kernel,
        outs,
        scratch,
        in_specs=[smem()] * 2 + [vmem()] * 12 + [anywhere()] * 8,
        out_specs=[vmem()] * 4 + [anywhere()] * 4,
    )(info, seq_lengths, *near, *far, *gains, *weights)


def share_kernel(info, keep, send_back, one_near, one_far, zero_near, zero_far, *pieces):
    half = keep.shape[0] // len(pieces)
    block = 2 * half
    section = info[SEC]
    other = 1 - section
    for step, piece in enumerate(pieces):
        spot = info[ZED] ^ step
        near_rows = pl.ds(pl.multiple_of(section * half, half), half)
        far_rows = pl.ds(pl.multiple_of(other * half, half), half)
        mine = pl.ds(pl.multiple_of(spot * half, half), half)
        whole = pl.ds(pl.multiple_of(spot * block, block), block)
        piece[near_rows, :] = keep[mine, :]
        piece[far_rows, :] = send_back[mine, :]

        @pl.when(section == 0)
        def _():
            piece[block:, :] = (zero_near[whole, :] + zero_far[whole, :]).astype(BF)

        @pl.when(section == 1)
        def _():
            piece[block : block + half, :] = one_far[mine, :]
            piece[block + half :, :] = one_near[mine, :]


def settle_kernel(info, piece0, piece1, piece2, piece3, results, input_grads):
    block = piece0.shape[0] // 2
    for step, piece in enumerate((piece0, piece1, piece2, piece3)):
        micro = info[ZED] ^ step
        results[0, micro, 0] = piece[:block, :]
        input_grads[0, micro, 0] = piece[block:, :]


def ffn_finish_kernel(info, piece0, piece1, piece2, piece3, up, down, held):
    for step, piece in enumerate((piece0, piece1, piece2, piece3)):
        held[info[FLIP + info[SEC]] ^ step] = piece[...]
    rows, width = held.shape[1:]
    blocks = rows // width
    for quarter in range(2):
        for part in range(blocks):
            spread = slice(part * width, (part + 1) * width)
            column = (quarter * blocks + part) * width
            up[0, :, column : column + width] = held[quarter, spread, :].astype(F32)
            down[0, column : column + width, :] = held[quarter + 2, spread, :].astype(F32)


def attn_finish_kernel(info, piece0, piece1, piece2, piece3, gain_attn, gain_ffn, qkv, out, held):
    for step, piece in enumerate((piece0, piece1, piece2, piece3)):
        held[info[FLIP + info[SEC]] ^ step] = piece[...]
    width = held.shape[2]
    for quarter in range(3):
        qkv[0, :, quarter * width : (quarter + 1) * width] = held[quarter, :width, :].astype(F32)
    out[0] = held[3, :width, :].astype(F32)
    spare = held[0, width:, :].astype(F32)
    gain_attn[...] = spare[0:1, :]
    gain_ffn[...] = spare[1:2, :]


SWAP = [(0, 1), (1, 0)]


def crossed(flips):
    return [(4 * s + g, 4 * s + (g ^ flips[s])) for s in range(2) for g in range(4)]


FIRST = crossed((1, 2))
SECOND = crossed((2, 1))


def line_pairs(step):
    return [(z, z ^ step) for z in range(4)]


def reduce_terms(keep, send):
    came = lax.ppermute(send, "section", SWAP)
    from_first = lax.ppermute(keep[2:4] + came[2:4], ("section", "rep"), FIRST)
    from_second = lax.ppermute(
        keep[1] + came[1] + from_first[1], ("section", "rep"), SECOND
    )
    total = lax.optimization_barrier(keep[0] + came[0] + from_first[0] + from_second)
    total = lax.optimization_barrier(total + lax.ppermute(total, "dp", line_pairs(1)))
    total = lax.optimization_barrier(total + lax.ppermute(total, "dp", line_pairs(2)))
    one = lax.ppermute(total, ("section", "rep"), SECOND)
    two = lax.ppermute(total, ("section", "rep"), FIRST)
    three = lax.ppermute(one, ("section", "rep"), FIRST)
    return total, one, two, three


def lines(
    block_input,
    output_grad,
    seq_lengths,
    attn_gain,
    qkv_proj,
    out_proj,
    ffn_gain,
    up_proj,
    down_proj,
):
    section = lax.axis_index("section")
    zed = lax.axis_index("dp")
    rep = lax.axis_index("rep")
    low, high = rep & 1, rep >> 1
    info = jnp.stack([section, zed, rep, 2 * low + high, 2 * high + low]).astype(jnp.int32)
    micro_count, _, block, width = block_input.shape
    hidden_units = up_proj.shape[2]
    shape = jax.ShapeDtypeStruct

    packed = vmem_call(
        pack_kernel,
        (shape((block, width), BF),) * micro_count,
        in_specs=[smem()] + [vmem()] * 2,
        out_specs=[vmem()] * micro_count,
    )(info, block_input[:, 0], output_grad[:, 0])
    near = [packed[0]] + [
        lax.ppermute(packed[step], "dp", line_pairs(step)) for step in range(1, micro_count)
    ]
    far = [lax.ppermute(piece, "section", SWAP) for piece in near]
    own = (attn_gain, ffn_gain, qkv_proj[0], out_proj[0], up_proj[0], down_proj[0])
    swapped = [lax.ppermute(weight, "section", SWAP) for weight in own]
    (
        result_keep,
        result_send,
        grad_in_one,
        grad_in_zero,
        ffn_keep,
        ffn_send,
        attn_keep,
        attn_send,
    ) = run_step(
        info,
        seq_lengths,
        near,
        far,
        (own[0], own[1], swapped[0], swapped[1]),
        (*own[2:], *swapped[2:]),
    )
    ffn_pieces = reduce_terms(ffn_keep, ffn_send)
    attn_pieces = reduce_terms(attn_keep, attn_send)

    result_back = lax.ppermute(result_send, "section", SWAP)
    one_far = lax.ppermute(grad_in_one, "section", [(0, 1)])
    zero_far = lax.ppermute(grad_in_zero, "section", [(1, 0)])
    shared = vmem_call(
        share_kernel,
        (shape((2 * block, width), BF),) * micro_count,
        in_specs=[smem()] + [vmem()] * 6,
        out_specs=[vmem()] * micro_count,
    )(info, result_keep, result_back, grad_in_one, one_far, grad_in_zero, zero_far)
    home = [shared[0]] + [
        lax.ppermute(shared[step], "dp", line_pairs(step)) for step in range(1, micro_count)
    ]
    results, input_grads = vmem_call(
        settle_kernel,
        (shape((1, micro_count, 1, block, width), BF),) * 2,
        in_specs=[smem()] + [vmem()] * micro_count,
        out_specs=[vmem()] * 2,
    )(info, *home)

    up, down = vmem_call(
        ffn_finish_kernel,
        (shape((1, width, hidden_units), F32), shape((1, hidden_units, width), F32)),
        [pltpu.VMEM((4, *ffn_keep.shape[1:]), BF)],
        in_specs=[smem()] + [vmem()] * 4,
        out_specs=[vmem()] * 2,
    )(info, *ffn_pieces)
    gain_attn, gain_ffn, qkv, out = vmem_call(
        attn_finish_kernel,
        (
            shape((1, width), F32),
            shape((1, width), F32),
            shape((1, width, 3 * width), F32),
            shape((1, width, width), F32),
        ),
        [pltpu.VMEM((4, *attn_keep.shape[1:]), BF)],
        in_specs=[smem()] + [vmem()] * 4,
        out_specs=[vmem()] * 4,
    )(info, *attn_pieces)
    return (results, input_grads, gain_attn, qkv, out, gain_ffn, up, down)


def local(*arrays):
    micro_count, _, tok_rows, model_width = arrays[0].shape
    one_line_per_chip = (
        lax.axis_size("section") == 2
        and lax.axis_size("dp") == 4
        and lax.axis_size("rep") == 4
        and micro_count == 4
        and tok_rows == STRIDE
        and model_width == 256
        and arrays[7].shape[2] == 4 * model_width
    )
    return lines(*arrays) if one_line_per_chip else general(*arrays)


def solution(mesh):
    placed = (
        P(None, "rep", "dp", None),
        P(None, "rep", "dp", None),
        P(),
        P("section", None),
        P("section", None, None),
        P("section", None, None),
        P("section", None),
        P("section", None, None),
        P("section", None, None),
    )
    return jax.shard_map(
        local,
        mesh=mesh,
        in_specs=placed,
        out_specs=(
            P("section", None, "rep", "dp", None),
            P("section", None, "rep", "dp", None),
            P("section", None),
            P("section", None, None),
            P("section", None, None),
            P("section", None),
            P("section", None, None),
            P("section", None, None),
        ),
        check_vma=False,
    )
```

```python
from functools import partial

import jax
import jax.numpy as jnp
from jax import lax
from jax.experimental import pallas as pl
from jax.experimental.pallas import tpu as pltpu
from jax.sharding import PartitionSpec as P

HEADS = 2
STRIDE = 128


NEG = -1e30


def from_behind(shard, axis, by):
    length = lax.axis_size(axis)
    pairs = [(i, i + by) for i in range(length) if 0 <= i + by < length]
    return lax.ppermute(shard, axis, pairs)


def normalize(values):
    centered = values - jnp.mean(values, axis=-1, keepdims=True)
    spread = jnp.mean(centered * centered, axis=-1, keepdims=True)
    return centered * lax.rsqrt(spread + 1e-05)


def gained(values, gain):
    return normalize(values) * gain


def allowed(query_pos, query_seg, key_pos, key_seg, strided, seq_slots):
    offset = query_pos - key_pos
    same_seq = (query_seg == key_seg) & (query_seg < seq_slots)
    nearby = (offset >= 0) & (offset < STRIDE)
    spaced = (offset >= 0) & (offset % STRIDE == 0)
    pattern = jnp.where(strided, spaced, nearby)
    return same_seq & pattern | (offset == 0)


def product(left, right):
    return jnp.dot(left, right, preferred_element_type=jnp.float32)


def contract_rows(left, right):
    return lax.dot_general(
        left, right, (((0,), (0,)), ((), ())), preferred_element_type=jnp.float32
    )


def contract_cols(left, right):
    return lax.dot_general(
        left, right, (((1,), (1,)), ((), ())), preferred_element_type=jnp.float32
    )


def put_row(buffer, value, slot_index, is_valid):
    current = lax.dynamic_index_in_dim(buffer, slot_index, 0, keepdims=False)
    return lax.dynamic_update_index_in_dim(
        buffer, jnp.where(is_valid, value, current), slot_index, 0
    )


def softmax_parts(scores):
    row_max = jnp.max(scores, axis=-1, keepdims=True)
    shifted = jnp.exp(scores - row_max)
    row_total = jnp.sum(shifted, axis=-1, keepdims=True)
    return ((shifted / row_total).astype(jnp.bfloat16), (row_max + jnp.log(row_total))[..., 0])


def general(
    block_input,
    output_grad,
    seq_lengths,
    attn_gain,
    qkv_proj,
    out_proj,
    ffn_gain,
    up_proj,
    down_proj,
):
    section_index = lax.axis_index("section")
    line_row = lax.axis_index("dp")
    group_index = lax.axis_index("rep")
    strided = section_index == 1
    micro_count, _, tok_rows, model_width = block_input.shape
    line_count = lax.axis_size("dp")
    line_span = tok_rows * line_count
    head_size = model_width // HEADS
    score_scale = float(head_size) ** (-0.5)
    seq_slots = seq_lengths.shape[-1]
    block_count = line_span // STRIDE
    residues = STRIDE // line_count
    line_lengths = lax.dynamic_index_in_dim(seq_lengths, group_index, 1, keepdims=False)
    all_pos = jnp.arange(line_span, dtype=jnp.int32)
    my_pos = line_row * tok_rows + jnp.arange(tok_rows, dtype=jnp.int32)
    win_pos = line_row * tok_rows - tok_rows + jnp.arange(2 * tok_rows, dtype=jnp.int32)
    res_pos = (
        jnp.arange(block_count, dtype=jnp.int32)[None, :] * STRIDE
        + line_row * residues
        + jnp.arange(residues, dtype=jnp.int32)[:, None]
    )
    gain_attn = attn_gain[0].astype(jnp.float32)
    gain_ffn = ffn_gain[0].astype(jnp.float32)
    w_qkv = qkv_proj[0]
    w_out = out_proj[0]
    w_up = up_proj[0]
    w_down = down_proj[0]

    def segments_of(slot_index):
        seq_ends = jnp.cumsum(lax.dynamic_index_in_dim(line_lengths, slot_index, 0, keepdims=False))
        all_seg = jnp.sum((all_pos[:, None] >= seq_ends[None, :]).astype(jnp.int32), axis=1)
        my_seg = lax.dynamic_slice_in_dim(all_seg, line_row * tok_rows, tok_rows)
        padded = jnp.concatenate([jnp.full((tok_rows,), seq_slots, jnp.int32), all_seg])
        win_seg = lax.dynamic_slice_in_dim(padded, line_row * tok_rows, 2 * tok_rows)
        res_seg = lax.dynamic_slice_in_dim(
            all_seg.reshape(block_count, STRIDE), line_row * residues, residues, 1
        ).T
        dense_mask = allowed(
            my_pos[:, None], my_seg[:, None], all_pos[None, :], all_seg[None, :], strided, seq_slots
        )
        win_mask = allowed(
            my_pos[:, None], my_seg[:, None], win_pos[None, :], win_seg[None, :], False, seq_slots
        )
        res_mask = allowed(
            res_pos[:, :, None],
            res_seg[:, :, None],
            res_pos[:, None, :],
            res_seg[:, None, :],
            True,
            seq_slots,
        )
        return (all_seg, my_seg, dense_mask, win_mask, res_mask)

    def project(hidden):
        normed = gained(hidden, gain_attn).astype(jnp.bfloat16)
        packed = product(normed, w_qkv).astype(jnp.bfloat16)
        return (normed, packed)

    def finish(hidden, attended):
        middle = hidden + product(attended, w_out)
        second = gained(middle, gain_ffn).astype(jnp.bfloat16)
        pre_act = product(second, w_up)
        active = jax.nn.gelu(pre_act, approximate=False).astype(jnp.bfloat16)
        return (middle, second, pre_act, active, middle + product(active, w_down))

    def dense_backward(packed, grad_att, lse_now, masks):
        all_seg, my_seg, dense_mask = (masks[0], masks[1], masks[2])
        queries = packed[:, :model_width]
        key_rows = packed[:, model_width : 2 * model_width]
        values = packed[:, 2 * model_width :]
        keys_all, values_all = (
            lax.all_gather(key_rows, "dp", axis=0, tiled=True),
            lax.all_gather(values, "dp", axis=0, tiled=True),
        )
        grad_q_heads = []
        grad_k_heads = []
        grad_v_heads = []
        delta_heads = []
        for head_index in range(HEADS):
            columns = slice(head_index * head_size, (head_index + 1) * head_size)
            query_head = queries[:, columns]
            out_head = grad_att[:, columns]
            scores = jnp.where(
                dense_mask, contract_cols(query_head, keys_all[:, columns]) * score_scale, NEG
            )
            attn_probs = jnp.exp(scores - lse_now[head_index][:, None])
            grad_probs = contract_cols(out_head, values_all[:, columns])
            delta_row = jnp.sum(attn_probs * grad_probs, axis=1)
            grad_scores = (attn_probs * (grad_probs - delta_row[:, None])).astype(jnp.bfloat16)
            grad_q_heads.append(product(grad_scores, keys_all[:, columns]) * score_scale)
            delta_heads.append(delta_row)
            key_part = contract_rows(grad_scores, query_head) * score_scale
            value_part = contract_rows(attn_probs.astype(jnp.bfloat16), out_head)
            key_mine, value_mine = (
                lax.psum_scatter(
                    key_part.astype(jnp.bfloat16), "dp", scatter_dimension=0, tiled=True
                ).astype(jnp.float32),
                lax.psum_scatter(
                    value_part.astype(jnp.bfloat16), "dp", scatter_dimension=0, tiled=True
                ).astype(jnp.float32),
            )
            grad_k_heads.append(key_mine)
            grad_v_heads.append(value_mine)
        return jnp.concatenate(
            [
                jnp.concatenate(grad_q_heads, axis=1).astype(jnp.bfloat16),
                jnp.concatenate(grad_k_heads, axis=1).astype(jnp.bfloat16),
                jnp.concatenate(grad_v_heads, axis=1).astype(jnp.bfloat16),
            ],
            axis=1,
        )

    received = jnp.zeros((tok_rows, model_width), jnp.bfloat16)
    saved_in = jnp.zeros((micro_count, tok_rows, model_width), jnp.bfloat16)
    saved_att = jnp.zeros((micro_count, tok_rows, model_width), jnp.bfloat16)
    saved_lse = jnp.zeros((micro_count, HEADS, tok_rows), jnp.float32)
    results = jnp.zeros((micro_count, tok_rows, model_width), jnp.bfloat16)
    for tick_index in range(micro_count + 1):
        slot_raw = tick_index - section_index
        is_valid = (slot_raw >= 0) & (slot_raw < micro_count)
        slot_index = jnp.clip(slot_raw, 0, micro_count - 1)
        hidden_low = jnp.where(
            section_index == 0, block_input[min(tick_index, micro_count - 1), 0], received
        )
        hidden = hidden_low.astype(jnp.float32)
        normed, packed = project(hidden)
        masks = segments_of(slot_index)
        dense_dense_mask = masks[2]
        dense_keys_all = lax.all_gather(
            packed[:, model_width : 2 * model_width], "dp", axis=0, tiled=True
        )
        dense_values_all = lax.all_gather(packed[:, 2 * model_width :], "dp", axis=0, tiled=True)
        head_outs = []
        head_lse = []
        for dense_head_index in range(HEADS):
            dense_columns = slice(dense_head_index * head_size, (dense_head_index + 1) * head_size)
            dense_scores = jnp.where(
                dense_dense_mask,
                contract_cols(packed[:, dense_columns], dense_keys_all[:, dense_columns])
                * score_scale,
                NEG,
            )
            dense_attn_probs, lse_row = softmax_parts(dense_scores)
            head_outs.append(product(dense_attn_probs, dense_values_all[:, dense_columns]))
            head_lse.append(lse_row)
        attended = jnp.concatenate(head_outs, axis=1).astype(jnp.bfloat16)
        lse_rows = jnp.stack(head_lse)
        output = finish(hidden, attended)[4].astype(jnp.bfloat16)
        saved_in = put_row(saved_in, hidden_low, slot_index, is_valid)
        saved_att = put_row(saved_att, attended, slot_index, is_valid)
        saved_lse = put_row(saved_lse, lse_rows, slot_index, is_valid)
        results = put_row(results, output, slot_index, is_valid)
        if tick_index < micro_count:
            received = from_behind(output, "section", 1)
    totals = (
        jnp.zeros((model_width,), jnp.float32),
        jnp.zeros(w_qkv.shape, jnp.float32),
        jnp.zeros(w_out.shape, jnp.float32),
        jnp.zeros((model_width,), jnp.float32),
        jnp.zeros(w_up.shape, jnp.float32),
        jnp.zeros(w_down.shape, jnp.float32),
    )
    sent_back = jnp.zeros((tok_rows, model_width), jnp.bfloat16)
    input_grads = jnp.zeros((micro_count, tok_rows, model_width), jnp.bfloat16)
    for tick_index in range(micro_count + 1):
        slot_raw = tick_index - (1 - section_index)
        is_valid = (slot_raw >= 0) & (slot_raw < micro_count)
        slot_index = jnp.clip(slot_raw, 0, micro_count - 1)
        grad_out = jnp.where(
            section_index == 1, output_grad[min(tick_index, micro_count - 1), 0], sent_back
        )
        hidden = lax.dynamic_index_in_dim(saved_in, slot_index, 0, keepdims=False).astype(
            jnp.float32
        )
        attended = lax.dynamic_index_in_dim(saved_att, slot_index, 0, keepdims=False)
        lse_now = lax.dynamic_index_in_dim(saved_lse, slot_index, 0, keepdims=False)
        normed, packed = project(hidden)
        middle, second, pre_act, active, _ = finish(hidden, attended)
        grad_down = contract_rows(active, grad_out)
        grad_active = contract_cols(grad_out, w_down)
        gelu_back = jax.vjp(partial(jax.nn.gelu, approximate=False), pre_act)[1]
        grad_pre = gelu_back(grad_active)[0].astype(jnp.bfloat16)
        grad_up = contract_rows(second, grad_pre)
        ffn_back = jax.vjp(gained, middle, gain_ffn)[1]
        grad_mid_norm, grad_gain_ffn = ffn_back(contract_cols(grad_pre, w_up))
        grad_middle = grad_out.astype(jnp.float32) + grad_mid_norm
        grad_branch = grad_middle.astype(jnp.bfloat16)
        grad_outproj = contract_rows(attended, grad_branch)
        grad_att = contract_cols(grad_branch, w_out).astype(jnp.bfloat16)
        masks = segments_of(slot_index)
        grad_packed = dense_backward(packed, grad_att, lse_now, masks)
        grad_qkv = contract_rows(normed, grad_packed)
        attn_back = jax.vjp(gained, hidden, gain_attn)[1]
        grad_hid_norm, grad_gain_attn = attn_back(contract_cols(grad_packed, w_qkv))
        grad_hidden = (grad_middle + grad_hid_norm).astype(jnp.bfloat16)
        terms = (grad_gain_attn, grad_qkv, grad_outproj, grad_gain_ffn, grad_up, grad_down)
        totals = tuple(
            (
                running + jnp.where(is_valid, term_now, 0.0)
                for running, term_now in zip(totals, terms)
            )
        )
        input_grads = put_row(input_grads, grad_hidden, slot_index, is_valid)
        if tick_index < micro_count:
            sent_back = from_behind(grad_hidden, "section", -1)
    summed = lax.psum(
        (totals[0], totals[1], totals[2], totals[3], totals[4], totals[5]), ("dp", "rep")
    )
    return (
        results[None, :, None],
        input_grads[None, :, None],
        summed[0][None],
        summed[1][None],
        summed[2][None],
        summed[3][None],
        summed[4][None],
        summed[5][None],
    )


BF = jnp.bfloat16
F32 = jnp.float32
MIB = 1024 * 1024
GAIN_ROWS = 32


def call(body, scalars, arrays, shapes, mib=24, micros=1.0, scratch=(), held=0):
    in_specs = [pl.BlockSpec(memory_space=pltpu.SMEM)] * len(scalars)
    in_specs += [pl.BlockSpec(memory_space=pl.ANY)] * held
    in_specs += [pl.BlockSpec(memory_space=pltpu.VMEM)] * (len(arrays) - held)
    return pl.pallas_call(
        body,
        out_shape=tuple(jax.ShapeDtypeStruct(*shape) for shape in shapes),
        in_specs=in_specs,
        out_specs=tuple(pl.BlockSpec(memory_space=pltpu.VMEM) for _ in shapes),
        scratch_shapes=list(scratch),
        compiler_params=pltpu.CompilerParams(vmem_limit_bytes=mib * MIB),
        cost_estimate=pl.CostEstimate(
            flops=int(micros * 1.1e9), bytes_accessed=int(micros * 3.4e6), transcendentals=0
        ),
    )(
        *scalars,
        *(pltpu.with_memory_space_constraint(array, pltpu.HBM) for array in arrays[:held]),
        *arrays[held:],
    )


SEC, ZED, REP, FLIP = 0, 1, 2, 3


def rows_at(start, count):
    return pl.ds(pl.multiple_of(start, count), count)


def pack_kernel(info, tokens, grads, gain_attn, gain_ffn, *rest):
    *pieces, gains, sems, gain_sems = rest
    block = tokens.shape[2]
    half = block // 2
    rows = rows_at(info[SEC] * half, half)
    copies = [
        pltpu.make_async_copy(gain_attn, gains.at[0], gain_sems.at[0]),
        pltpu.make_async_copy(gain_ffn, gains.at[1], gain_sems.at[1]),
    ]
    for step, piece in enumerate(pieces):
        micro = info[ZED] ^ step
        for part, source in enumerate((tokens, grads)):
            copies.append(
                pltpu.make_async_copy(
                    source.at[micro, 0, rows],
                    piece.at[part * half : (part + 1) * half],
                    sems.at[2 * step + part],
                )
            )
    for copy in copies:
        copy.start()
    for copy in copies:
        copy.wait()
    pieces[0][block:, :] = jnp.concatenate(
        [
            gains[0].astype(F32),
            gains[1].astype(F32),
            jnp.zeros((pieces[0].shape[0] - block - 2, gains.shape[2]), F32),
        ],
        axis=0,
    ).astype(BF)


def unit(values):
    centered = values - jnp.mean(values, axis=-1, keepdims=True)
    inverse = lax.rsqrt(jnp.mean(centered * centered, axis=-1, keepdims=True) + 1e-05)
    return centered * inverse, inverse


def unit_back(grad, normal, inverse):
    return inverse * (
        grad
        - jnp.mean(grad, axis=-1, keepdims=True)
        - normal * jnp.mean(grad * normal, axis=-1, keepdims=True)
    )


def widened(column, width):
    return jnp.broadcast_to(column, (column.shape[0], width))


def segment_at(ends, position):
    total = jnp.zeros(position.shape, jnp.int32)
    for end in ends:
        total = total + (position >= end).astype(jnp.int32)
    return total


def ends_of(info, lengths):
    ends = []
    so_far = jnp.int32(0)
    for slot in range(lengths.shape[2]):
        so_far = so_far + lengths[info[ZED], info[REP], slot]
        ends.append(so_far)
    return ends


def normalized_exp(scores):
    shifted = jnp.exp(scores - jnp.max(scores, axis=-1, keepdims=True))
    return shifted * (1.0 / jnp.sum(shifted, axis=-1, keepdims=True))


def ffn_forward(hidden, attended, gain, w_out, w_up, w_down, saved):
    result, middle_unit, middle_inverse, second_ref, active, slope = saved
    middle = hidden + product(attended, w_out)
    normal, inverse = unit(middle)
    middle_unit[...] = normal
    middle_inverse[...] = widened(inverse, middle_inverse.shape[1])
    second = (normal * gain).astype(BF)
    second_ref[...] = second
    chunk = middle.shape[1]
    total = middle
    for index in range(w_up.shape[1] // chunk):
        columns = slice(index * chunk, (index + 1) * chunk)
        pre_act = product(second, w_up[:, columns])
        below = 0.5 + 0.5 * lax.erf(pre_act * (0.5**0.5))
        now = (pre_act * below).astype(BF)
        active[:, columns] = now
        slope[:, columns] = below + pre_act * (
            jnp.exp(-0.5 * pre_act * pre_act) * 0.3989422804014327
        )
        total = total + product(now, w_down[columns, :])
    result[...] = total.astype(BF)


def own_unit(spot, half):
    return slice((2 * spot + 2) * half, (2 * spot + 3) * half)


def key_units(spot, half):
    return slice(2 * spot * half, (2 * spot + 3) * half)


def zero_forward_kernel(
    info,
    lengths,
    own0,
    own1,
    own2,
    own3,
    far0,
    far1,
    far2,
    far3,
    w_qkv,
    w_out,
    w_up,
    w_down,
    gains,
    line,
    normal_all,
    inverse_all,
    normed_all,
    query,
    padded,
    probs_ref,
    attended_ref,
    cotangent,
    *saved,
):
    section = info[SEC]
    reached, width = normal_all.shape
    half = line.shape[0] // 10
    block = 2 * half
    blocks = 4
    rows = blocks * half
    head = width // HEADS
    scale = float(head) ** (-0.5)
    reach = block + half
    line[:block, :] = jnp.zeros((block, width), BF)
    for step, (near, far) in enumerate(((own0, far0), (own1, far1), (own2, far2), (own3, far3))):
        spot = info[ZED] ^ step
        line[rows_at(spot * block + block, half), :] = near[:half, :]
        line[rows_at(spot * block + block + half - section * block, half), :] = far[:half, :]
        cotangent[rows_at(spot * half, half), :] = near[half:block, :]
    normal, inverse = unit(line[:reached, :].astype(F32))
    normal_all[...] = normal
    inverse_all[...] = widened(inverse, inverse_all.shape[1])
    normed = (normal * gains[0, 0:1, :]).astype(BF)
    normed_all[...] = normed
    padded[...] = product(normed, w_qkv[0, :, width:]).astype(BF)
    normed_mine = jnp.concatenate(
        [normed[own_unit(spot, half), :] for spot in range(blocks)], axis=0
    )
    query[...] = product(normed_mine, w_qkv[0, :, :width]).astype(BF)
    ends = ends_of(info, lengths)
    row = lax.broadcasted_iota(jnp.int32, (rows, reach), 0)
    query_pos = block * (row // half) + section * half + (row & (half - 1))
    key_pos = query_pos - (row & (half - 1)) - block
    key_pos = key_pos + lax.broadcasted_iota(jnp.int32, (rows, reach), 1)
    offset = query_pos - key_pos
    segment = segment_at(ends, query_pos)
    same = (segment == segment_at(ends, key_pos)) & (segment < len(ends)) & (key_pos >= 0)
    mask = same & (offset >= 0) & (offset < STRIDE) | (offset == 0)
    spots = [(slice(spot * half, (spot + 1) * half), key_units(spot, half)) for spot in range(blocks)]
    heads = [
        (slice(number * head, (number + 1) * head), slice(width + number * head, width + (number + 1) * head))
        for number in range(HEADS)
    ]
    scores = [
        jnp.concatenate(
            [contract_cols(query[here, columns], padded[window, columns]) for here, window in spots],
            axis=0,
        )
        for columns, _ in heads
    ]
    probs = [normalized_exp(jnp.where(mask, values * scale, NEG)) for values in scores]
    attended = []
    for number, (_, value_columns) in enumerate(heads):
        probs_ref[number] = probs[number]
        low = probs[number].astype(BF)
        attended.append(
            jnp.concatenate(
                [product(low[here, :], padded[window, value_columns]) for here, window in spots], axis=0
            )
        )
    attended = jnp.concatenate(attended, axis=1).astype(BF)
    attended_ref[...] = attended
    hidden = jnp.concatenate([line[own_unit(spot, half), :] for spot in range(blocks)], axis=0)
    ffn_forward(
        hidden.astype(F32), attended, gains[0, 1:2, :], w_out[0], w_up.at[0], w_down.at[0], saved
    )


def one_forward_kernel(
    info,
    lengths,
    hidden_ref,
    w_qkv,
    w_out,
    w_up,
    w_down,
    gains,
    normal_ref,
    inverse_ref,
    normed_ref,
    packed,
    probs_ref,
    attended_ref,
    *saved,
):
    section = info[SEC]
    rows, width = hidden_ref.shape
    half = rows // 4
    block = 2 * half
    head = width // HEADS
    scale = float(head) ** (-0.5)
    hidden = hidden_ref[...].astype(F32)
    normal, inverse = unit(hidden)
    normal_ref[...] = normal
    inverse_ref[...] = widened(inverse, inverse_ref.shape[1])
    normed = (normal * gains[1, 0:1, :]).astype(BF)
    normed_ref[...] = normed
    packed[...] = product(normed, w_qkv[1]).astype(BF)
    ends = ends_of(info, lengths)

    def place(axis):
        index = lax.broadcasted_iota(jnp.int32, (rows, rows), axis)
        return block * (index // half) + section * half + (index & (half - 1))

    query_pos, key_pos = place(0), place(1)
    offset = query_pos - key_pos
    segment = segment_at(ends, query_pos)
    same = (segment == segment_at(ends, key_pos)) & (segment < len(ends))
    mask = same & (offset >= 0) & ((offset & (STRIDE - 1)) == 0) | (offset == 0)
    heads = [
        tuple(
            slice(part * width + number * head, part * width + (number + 1) * head) for part in range(3)
        )
        for number in range(HEADS)
    ]
    scores = [contract_cols(packed[:, near], packed[:, far]) for near, far, _ in heads]
    probs = [normalized_exp(jnp.where(mask, values * scale, NEG)) for values in scores]
    parts = []
    for number, (_, _, value_columns) in enumerate(heads):
        probs_ref[number] = probs[number]
        parts.append(product(probs[number].astype(BF), packed[:, value_columns]))
    attended = jnp.concatenate(parts, axis=1).astype(BF)
    attended_ref[...] = attended
    ffn_forward(hidden, attended, gains[1, 1:2, :], w_out[1], w_up.at[1], w_down.at[1], saved)


def store_block(info, terms, number, value):
    width = value.shape[1]
    unit_rows = width // 2
    core, number = divmod(number, 6)
    side, flip = info[SEC] ^ core, info[FLIP + core]
    value = value.astype(BF)
    for part in range(2):
        quarter, place = divmod(2 * number + part, 3)
        terms[side, flip ^ quarter, place * unit_rows : (place + 1) * unit_rows, :] = value[
            part * unit_rows : (part + 1) * unit_rows, :
        ]


def store_gains(info, terms, attn_term, ffn_term):
    spare, width = terms.shape[2] - GAIN_ROWS, terms.shape[3]
    value = jnp.concatenate(
        [attn_term, ffn_term, jnp.zeros((GAIN_ROWS - 2, width), F32)], axis=0
    ).astype(BF)
    for side in range(2):
        for quarter in range(4):
            terms[side, quarter, spare:, :] = value


def ffn_input_grad(grad_out, saved, gain, w_out, w_up, w_down, grad_pre_ref):
    middle_unit, middle_inverse, slope = saved
    width = grad_out.shape[1]
    grad_second = None
    for index in range(w_up.shape[1] // width):
        columns = slice(index * width, (index + 1) * width)
        grad_active = contract_cols(grad_out, w_down[columns, :])
        grad_pre = (grad_active * slope[:, columns]).astype(BF)
        grad_pre_ref[:, columns] = grad_pre
        term = contract_cols(grad_pre, w_up[:, columns])
        grad_second = term if grad_second is None else grad_second + term
    normal = middle_unit[...]
    gain_term = jnp.sum(grad_second * normal, axis=0, keepdims=True)
    grad_middle = grad_out.astype(F32) + unit_back(
        grad_second * gain, normal, middle_inverse[:, 0:1]
    )
    return grad_middle, contract_cols(grad_middle.astype(BF), w_out).astype(BF), gain_term


def ffn_weight_grads(info, terms, grad_out, grad_middle, second, active, attended, grad_pre):
    width = grad_out.shape[1]
    store_block(info, terms, 3, contract_rows(attended[...], grad_middle.astype(BF)))
    for index in range(active.shape[1] // width):
        columns = slice(index * width, (index + 1) * width)
        store_block(info, terms, 4 + index, contract_rows(second[...], grad_pre[:, columns]))
        store_block(info, terms, 8 + index, contract_rows(active[:, columns], grad_out))


def one_backward_kernel(
    info,
    grad_ref,
    w_qkv,
    w_out,
    w_up,
    w_down,
    gains,
    normal_ref,
    inverse_ref,
    normed_ref,
    packed,
    probs_ref,
    *rest,
):
    middle_unit, middle_inverse, second, active, slope, attended, grad_in, terms, grad_pre = rest
    width = grad_ref.shape[1]
    head = width // HEADS
    scale = float(head) ** (-0.5)
    grad_out = grad_ref[...]
    grad_middle, grad_att, ffn_term = ffn_input_grad(
        grad_out,
        (middle_unit, middle_inverse, slope),
        gains[1, 1:2, :],
        w_out[1],
        w_up.at[1],
        w_down.at[1],
        grad_pre,
    )
    ffn_weight_grads(info, terms, grad_out, grad_middle, second, active, attended, grad_pre)
    heads = [
        tuple(
            slice(part * width + number * head, part * width + (number + 1) * head) for part in range(3)
        )
        for number in range(HEADS)
    ]
    probs = [probs_ref[number] for number in range(HEADS)]
    grad_probs = [
        contract_cols(grad_att[:, near], packed[:, value_columns]) for near, _, value_columns in heads
    ]
    grad_scores = [
        (prob * (grad - jnp.sum(prob * grad, axis=-1, keepdims=True))).astype(BF)
        for prob, grad in zip(probs, grad_probs)
    ]
    grad_parts = [
        [product(grad, packed[:, far]) * scale for grad, (_, far, _) in zip(grad_scores, heads)],
        [contract_rows(grad, packed[:, near]) * scale for grad, (near, _, _) in zip(grad_scores, heads)],
        [contract_rows(prob.astype(BF), grad_att[:, near]) for prob, (near, _, _) in zip(probs, heads)],
    ]
    grad_normed = None
    for index in range(3):
        columns = slice(index * width, (index + 1) * width)
        grad_block = jnp.concatenate(grad_parts[index], axis=1).astype(BF)
        term = contract_cols(grad_block, w_qkv[1, :, columns])
        grad_normed = term if grad_normed is None else grad_normed + term
        store_block(info, terms, index, contract_rows(normed_ref[...], grad_block))
    normal = normal_ref[...]
    store_gains(info, terms, jnp.sum(grad_normed * normal, axis=0, keepdims=True), ffn_term)
    grad_in[...] = (
        grad_middle + unit_back(grad_normed * gains[1, 0:1, :], normal, inverse_ref[:, 0:1])
    ).astype(BF)


def zero_ffn_kernel(
    grad_ref,
    w_out,
    w_up,
    w_down,
    gains,
    middle_unit,
    middle_inverse,
    slope,
    grad_middle_ref,
    grad_att_ref,
    grad_pre,
    gain_term,
):
    grad_middle, grad_att, term = ffn_input_grad(
        grad_ref[...],
        (middle_unit, middle_inverse, slope),
        gains[0, 1:2, :],
        w_out[0],
        w_up.at[0],
        w_down.at[0],
        grad_pre,
    )
    grad_middle_ref[...] = grad_middle
    grad_att_ref[...] = grad_att
    gain_term[...] = term


def zero_backward_kernel(
    info,
    grad_ref,
    w_qkv,
    gains,
    normal_all,
    inverse_all,
    normed_all,
    query,
    padded,
    probs_ref,
    result_zero,
    result_one,
    second,
    active,
    attended,
    grad_middle_ref,
    grad_att_ref,
    grad_pre,
    ffn_term,
    result_keep,
    grad_line,
    swap,
    terms,
):
    section = info[SEC]
    rows, width = grad_ref.shape
    reached = normal_all.shape[0]
    half = rows // 4
    blocks = 4
    head = width // HEADS
    scale = float(head) ** (-0.5)
    grad_out = grad_ref[...]

    @pl.when(section == 0)
    def _():
        result_keep[...] = result_zero[...]
        swap[:rows, :] = result_one[...]

    @pl.when(section == 1)
    def _():
        result_keep[...] = result_one[...]
        swap[:rows, :] = result_zero[...]

    grad_middle = grad_middle_ref[...]
    grad_att = grad_att_ref[...]
    ffn_weight_grads(info, terms, grad_out, grad_middle, second, active, attended, grad_pre)
    spots = [(slice(spot * half, (spot + 1) * half), key_units(spot, half)) for spot in range(blocks)]
    heads = [
        (slice(number * head, (number + 1) * head), slice(width + number * head, width + (number + 1) * head))
        for number in range(HEADS)
    ]
    probs = [probs_ref[number] for number in range(HEADS)]
    grad_probs = [
        jnp.concatenate(
            [
                contract_cols(grad_att[here, columns], padded[window, value_columns])
                for here, window in spots
            ],
            axis=0,
        )
        for columns, value_columns in heads
    ]
    grad_scores = [
        (prob * (grad - jnp.sum(prob * grad, axis=-1, keepdims=True))).astype(BF)
        for prob, grad in zip(probs, grad_probs)
    ]
    grad_query = [
        jnp.concatenate(
            [product(grad[here, :], padded[window, columns]) for here, window in spots], axis=0
        )
        * scale
        for grad, (columns, _) in zip(grad_scores, heads)
    ]
    grad_query = jnp.concatenate(grad_query, axis=1).astype(BF)

    def gathered(lefts, right):
        parts = []
        for left, (columns, _) in zip(lefts, heads):
            terms_of = [contract_rows(left[here, :], right[here, columns]) for here, _ in spots]
            units = []
            for index in range(reached // half):
                spot, place = divmod(index, 2)
                held = None
                if spot < blocks:
                    held = terms_of[spot][place * half : (place + 1) * half, :]
                if place == 0 and spot > 0:
                    last = terms_of[spot - 1][2 * half :, :]
                    held = last if held is None else held + last
                units.append(held)
            parts.append(jnp.concatenate(units, axis=0))
        return jnp.concatenate(parts, axis=1)

    grad_keys = (gathered(grad_scores, query) * scale).astype(BF)
    grad_values = gathered([prob.astype(BF) for prob in probs], grad_att).astype(BF)
    normed = normed_all[...]
    normed_mine = jnp.concatenate(
        [normed[own_unit(spot, half), :] for spot in range(blocks)], axis=0
    )
    store_block(info, terms, 0, contract_rows(normed_mine, grad_query))
    store_block(info, terms, 1, contract_rows(normed, grad_keys))
    store_block(info, terms, 2, contract_rows(normed, grad_values))
    from_query = contract_cols(grad_query, w_qkv[0, :, :width])
    grad_line[:reached, :] = contract_cols(
        grad_keys, w_qkv[0, :, width : 2 * width]
    ) + contract_cols(grad_values, w_qkv[0, :, 2 * width :])
    for spot in range(blocks):
        grad_line[own_unit(spot, half), :] += from_query[spot * half : (spot + 1) * half, :]
    grad_normed = grad_line[:reached, :]
    normal = normal_all[...]
    store_gains(info, terms, jnp.sum(grad_normed * normal, axis=0, keepdims=True), ffn_term[...])
    grad_line[:reached, :] = unit_back(grad_normed * gains[0, 0:1, :], normal, inverse_all[:, 0:1])
    for spot in range(blocks):
        grad_line[own_unit(spot, half), :] += grad_middle[spot * half : (spot + 1) * half, :]
    grad_line[reached:, :] = jnp.zeros((grad_line.shape[0] - reached, width), F32)

    @pl.when(section == 0)
    def _():
        swap[rows : 2 * rows, :] = grad_out

    @pl.when(section == 1)
    def _():
        swap[rows:, :] = grad_line[:reached, :].astype(BF)


def share_kernel(info, keep, one_near, zero_near, came, *pieces):
    rows = keep.shape[0]
    half = rows // 4
    block = 2 * half
    section = info[SEC]
    near_rows = rows_at(section * half, half)
    far_rows = rows_at(half - section * half, half)
    for step, piece in enumerate(pieces):
        spot = info[ZED] ^ step
        mine = rows_at(spot * half, half)
        piece[near_rows, :] = keep[mine, :]
        piece[far_rows, :] = came[mine, :]

    @pl.when(section == 0)
    def _():
        for step, piece in enumerate(pieces):
            base = (info[ZED] ^ step) * block
            near, far = rows_at(base + block, block), rows_at(rows + base + half, half)
            far = pl.ds(far.start, block)
            piece[block:, :] = (zero_near[near, :] + came[far, :].astype(F32)).astype(BF)

    @pl.when(section == 1)
    def _():
        for step, piece in enumerate(pieces):
            spot = info[ZED] ^ step
            piece[block : block + half, :] = came[rows_at(rows + spot * half, half), :]
            piece[block + half :, :] = one_near[rows_at(spot * half, half), :]


def settle_kernel(info, piece0, piece1, piece2, piece3, results, input_grads):
    block = piece0.shape[0] // 2
    for step, piece in enumerate((piece0, piece1, piece2, piece3)):
        micro = info[ZED] ^ step
        results[0, micro, 0] = piece[:block, :]
        input_grads[0, micro, 0] = piece[block:, :]


def collect_kernel(info, piece0, piece1, piece2, piece3, held):
    for step, piece in enumerate((piece0, piece1, piece2, piece3)):
        held[info[FLIP + info[SEC]] ^ step] = piece[...]


def finish_kernel(info, zero_near, zero_far, one_near, one_far, *outs):
    gain_attn, qkv, out, gain_ffn, up, down = outs
    width = zero_near.shape[2]
    unit_rows = width // 2

    def write(halves):
        def units(number):
            core, number = divmod(number, 6)
            for part in range(2):
                quarter, place = divmod(2 * number + part, 3)
                yield part * unit_rows, halves[core][
                    quarter, place * unit_rows : (place + 1) * unit_rows, :
                ].astype(F32)

        for number in range(12):
            for row, value in units(number):
                rows = slice(row, row + unit_rows)
                if number < 3:
                    qkv[0, rows, number * width : (number + 1) * width] = value
                elif number == 3:
                    out[0, rows, :] = value
                elif number < 8:
                    up[0, rows, (number - 4) * width : (number - 3) * width] = value
                else:
                    base = (number - 8) * width + row
                    down[0, base : base + unit_rows, :] = value
        spare = halves[0][0, zero_near.shape[1] - GAIN_ROWS :, :].astype(F32)
        gain_attn[...] = spare[0:1, :]
        gain_ffn[...] = spare[1:2, :]

    @pl.when(info[SEC] == 0)
    def _():
        write((zero_near, zero_far))

    @pl.when(info[SEC] == 1)
    def _():
        write((one_far, one_near))


SWAP = [(0, 1), (1, 0)]
PLANE = ("section", "rep")


def crossed(flips):
    return [(4 * s + g, 4 * s + (g ^ flips[s])) for s in range(2) for g in range(4)]


FIRST = crossed((1, 2))
SECOND = crossed((2, 1))


def along_line(value, step):
    return lax.ppermute(value, "dp", [(z, z ^ step) for z in range(4)])


def reduce_terms(info, terms, came, zed, along=()):
    bar = lax.optimization_barrier
    first = lax.ppermute(terms[0, 2:4] + came[2:4], PLANE, FIRST)
    second = lax.ppermute(terms[0, 1] + came[1] + first[1], PLANE, SECOND)
    total = bar(terms[0, 0] + came[0] + first[0] + second)
    total = bar(total + along_line(total, 1))
    if along:
        total, *along = bar((total, *along))
    half = total.shape[0] // 2
    odd = zed & 1
    mine = lax.dynamic_slice_in_dim(total, odd * half, half, 0)
    mine = bar(mine + along_line(mine, 2))
    other = along_line(mine, 1)
    total = bar(
        jnp.where(
            odd == 0, jnp.concatenate([mine, other]), jnp.concatenate([other, mine])
        )
    )
    one = lax.ppermute(total, PLANE, SECOND)
    two = lax.ppermute(total, PLANE, FIRST)
    three = lax.ppermute(one, PLANE, FIRST)
    shape = ((4, *total.shape), BF)
    return call(collect_kernel, (info,), (total, one, two, three), (shape,), 8)[0], along


def lines(
    block_input,
    output_grad,
    seq_lengths,
    attn_gain,
    qkv_proj,
    out_proj,
    ffn_gain,
    up_proj,
    down_proj,
):
    section = lax.axis_index("section")
    zed = lax.axis_index("dp")
    rep = lax.axis_index("rep")
    low, high = rep & 1, rep >> 1
    info = jnp.stack([section, zed, rep, 2 * low + high, 2 * high + low]).astype(jnp.int32)
    micro_count, _, block, width = block_input.shape
    hidden_units = up_proj.shape[2]
    half = block // 2
    rows, reach = micro_count * half, block + half
    reached = rows + rows + half
    term_rows = 6 * width // 4 + GAIN_ROWS

    packed = call(
        pack_kernel,
        (info,),
        (block_input, output_grad, attn_gain, ffn_gain),
        (((block + 16, width), BF),) + (((block, width), BF),) * (micro_count - 1),
        8,
        scratch=(
            pltpu.VMEM((2, 1, width), BF),
            pltpu.SemaphoreType.DMA((2 * micro_count,)),
            pltpu.SemaphoreType.DMA((2,)),
        ),
        held=4,
    )
    near = [packed[0]] + [along_line(packed[step], step) for step in range(1, micro_count)]
    far = [lax.ppermute(piece, "section", SWAP) for piece in near]
    own = (qkv_proj[0], out_proj[0], up_proj[0], down_proj[0])
    swapped = [lax.ppermute(weight, "section", SWAP) for weight in own]
    weights = tuple(
        jnp.stack([jnp.where(section == 0, a, b), jnp.where(section == 0, b, a)])
        for a, b in zip(own, swapped)
    )
    gains_near, gains_far = near[0][block:].astype(F32), far[0][block:].astype(F32)
    weights += (
        jnp.stack(
            [
                jnp.where(section == 0, gains_near, gains_far),
                jnp.where(section == 0, gains_far, gains_near),
            ]
        ),
    )
    ffn_saved = (
        ((rows, width), BF),
        ((rows, width), F32),
        ((rows, 128), F32),
        ((rows, width), BF),
        ((rows, hidden_units), BF),
        ((rows, hidden_units), F32),
    )
    (
        _,
        normal_all,
        inverse_all,
        normed_all,
        query,
        padded,
        probs_zero,
        attended_zero,
        cotangent,
        result_zero,
        *saved_zero,
    ) = call(
        zero_forward_kernel,
        (info, seq_lengths),
        (*near, *far, *weights),
        (
            ((reached + half, width), BF),
            ((reached, width), F32),
            ((reached, 128), F32),
            ((reached, width), BF),
            ((rows, width), BF),
            ((reached, 2 * width), BF),
            ((HEADS, rows, reach), F32),
            ((rows, width), BF),
            ((rows, width), BF),
            *ffn_saved,
        ),
    )
    (
        normal_one,
        inverse_one,
        normed_one,
        packed_one,
        probs_one,
        attended_one,
        result_one,
        *saved_one,
    ) = call(
        one_forward_kernel,
        (info, seq_lengths),
        (result_zero, *weights),
        (
            ((rows, width), F32),
            ((rows, 128), F32),
            ((rows, width), BF),
            ((rows, 3 * width), BF),
            ((HEADS, rows, rows), F32),
            ((rows, width), BF),
            *ffn_saved,
        ),
    )
    middle_one, mid_inverse_one, second_one, active_one, slope_one = saved_one
    grad_one, terms_one, _ = call(
        one_backward_kernel,
        (info,),
        (
            cotangent,
            *weights,
            normal_one,
            inverse_one,
            normed_one,
            packed_one,
            probs_one,
            middle_one,
            mid_inverse_one,
            second_one,
            active_one,
            slope_one,
            attended_one,
        ),
        (((rows, width), BF), ((2, 4, term_rows, width), BF), ((rows, hidden_units), BF)),
        micros=3.0,
    )
    middle_zero, mid_inverse_zero, second_zero, active_zero, slope_zero = saved_zero
    came_one = lax.ppermute(terms_one[1], "section", SWAP)
    w_qkv, w_out, w_up, w_down, gains = weights
    zero_ffn = call(
        zero_ffn_kernel,
        (),
        (grad_one, w_out, w_up, w_down, gains, middle_zero, mid_inverse_zero, slope_zero),
        (
            ((rows, width), F32),
            ((rows, width), BF),
            ((rows, hidden_units), BF),
            ((1, width), F32),
        ),
        micros=2.0,
    )
    came_one, *zero_ffn = lax.optimization_barrier((came_one, *zero_ffn))
    result_keep, grad_line, swap, terms_zero = call(
        zero_backward_kernel,
        (info,),
        (
            grad_one,
            w_qkv,
            gains,
            normal_all,
            inverse_all,
            normed_all,
            query,
            padded,
            probs_zero,
            result_zero,
            result_one,
            second_zero,
            active_zero,
            attended_zero,
            *zero_ffn,
        ),
        (
            ((rows, width), BF),
            ((reached + half, width), F32),
            ((rows + reached, width), BF),
            ((2, 4, term_rows, width), BF),
        ),
        micros=4.0,
    )
    came = lax.ppermute(swap, "section", SWAP)
    shared = call(
        share_kernel,
        (info,),
        (result_keep, grad_one, grad_line, came),
        (((2 * block, width), BF),) * micro_count,
        8,
    )
    home = [shared[0]] + [along_line(shared[step], step) for step in range(1, micro_count)]
    came_zero = lax.ppermute(terms_zero[1], "section", SWAP)
    one_near, home = reduce_terms(info, terms_one, came_one, zed, home)
    results, input_grads = call(
        settle_kernel,
        (info,),
        home,
        (((1, micro_count, 1, block, width), BF),) * 2,
        8,
    )
    zero_near, _ = reduce_terms(info, terms_zero, came_zero, zed)
    one_far = lax.ppermute(one_near, "section", [(0, 1)])
    zero_far = lax.ppermute(zero_near, "section", [(1, 0)])
    sums = call(
        finish_kernel,
        (info,),
        (zero_near, zero_far, one_near, one_far),
        (
            ((1, width), F32),
            ((1, width, 3 * width), F32),
            ((1, width, width), F32),
            ((1, width), F32),
            ((1, width, hidden_units), F32),
            ((1, hidden_units, width), F32),
        ),
        16,
    )
    return (results, input_grads, *sums)


def local(*arrays):
    micro_count, _, tok_rows, model_width = arrays[0].shape
    one_line_per_chip = (
        lax.axis_size("section") == 2
        and lax.axis_size("dp") == 4
        and lax.axis_size("rep") == 4
        and micro_count == 4
        and tok_rows == STRIDE
        and model_width == 256
        and arrays[7].shape[2] == 4 * model_width
    )
    return lines(*arrays) if one_line_per_chip else general(*arrays)


def solution(mesh):
    placed = (
        P(None, "rep", "dp", None),
        P(None, "rep", "dp", None),
        P(),
        P("section", None),
        P("section", None, None),
        P("section", None, None),
        P("section", None),
        P("section", None, None),
        P("section", None, None),
    )
    return jax.shard_map(
        local,
        mesh=mesh,
        in_specs=placed,
        out_specs=(
            P("section", None, "rep", "dp", None),
            P("section", None, "rep", "dp", None),
            P("section", None),
            P("section", None, None),
            P("section", None, None),
            P("section", None),
            P("section", None, None),
            P("section", None, None),
        ),
        check_vma=False,
    )
```

```python
from functools import partial

import jax
import jax.numpy as jnp
from jax import lax
from jax.experimental import pallas as pl
from jax.experimental.pallas import tpu as pltpu
from jax.sharding import PartitionSpec as P

HEADS = 2
STRIDE = 128


NEG = -1e30


def from_behind(shard, axis, by):
    length = lax.axis_size(axis)
    pairs = [(i, i + by) for i in range(length) if 0 <= i + by < length]
    return lax.ppermute(shard, axis, pairs)


def normalize(values):
    centered = values - jnp.mean(values, axis=-1, keepdims=True)
    spread = jnp.mean(centered * centered, axis=-1, keepdims=True)
    return centered * lax.rsqrt(spread + 1e-05)


def gained(values, gain):
    return normalize(values) * gain


def allowed(query_pos, query_seg, key_pos, key_seg, strided, seq_slots):
    offset = query_pos - key_pos
    same_seq = (query_seg == key_seg) & (query_seg < seq_slots)
    nearby = (offset >= 0) & (offset < STRIDE)
    spaced = (offset >= 0) & (offset % STRIDE == 0)
    pattern = jnp.where(strided, spaced, nearby)
    return same_seq & pattern | (offset == 0)


def product(left, right):
    return jnp.dot(left, right, preferred_element_type=jnp.float32)


def contract_rows(left, right):
    return lax.dot_general(
        left, right, (((0,), (0,)), ((), ())), preferred_element_type=jnp.float32
    )


def contract_cols(left, right):
    return lax.dot_general(
        left, right, (((1,), (1,)), ((), ())), preferred_element_type=jnp.float32
    )


def put_row(buffer, value, slot_index, is_valid):
    current = lax.dynamic_index_in_dim(buffer, slot_index, 0, keepdims=False)
    return lax.dynamic_update_index_in_dim(
        buffer, jnp.where(is_valid, value, current), slot_index, 0
    )


def softmax_parts(scores):
    row_max = jnp.max(scores, axis=-1, keepdims=True)
    shifted = jnp.exp(scores - row_max)
    row_total = jnp.sum(shifted, axis=-1, keepdims=True)
    return ((shifted / row_total).astype(jnp.bfloat16), (row_max + jnp.log(row_total))[..., 0])


def general(
    block_input,
    output_grad,
    seq_lengths,
    attn_gain,
    qkv_proj,
    out_proj,
    ffn_gain,
    up_proj,
    down_proj,
):
    section_index = lax.axis_index("section")
    line_row = lax.axis_index("dp")
    group_index = lax.axis_index("rep")
    strided = section_index == 1
    micro_count, _, tok_rows, model_width = block_input.shape
    line_count = lax.axis_size("dp")
    line_span = tok_rows * line_count
    head_size = model_width // HEADS
    score_scale = float(head_size) ** (-0.5)
    seq_slots = seq_lengths.shape[-1]
    block_count = line_span // STRIDE
    residues = STRIDE // line_count
    line_lengths = lax.dynamic_index_in_dim(seq_lengths, group_index, 1, keepdims=False)
    all_pos = jnp.arange(line_span, dtype=jnp.int32)
    my_pos = line_row * tok_rows + jnp.arange(tok_rows, dtype=jnp.int32)
    win_pos = line_row * tok_rows - tok_rows + jnp.arange(2 * tok_rows, dtype=jnp.int32)
    res_pos = (
        jnp.arange(block_count, dtype=jnp.int32)[None, :] * STRIDE
        + line_row * residues
        + jnp.arange(residues, dtype=jnp.int32)[:, None]
    )
    gain_attn = attn_gain[0].astype(jnp.float32)
    gain_ffn = ffn_gain[0].astype(jnp.float32)
    w_qkv = qkv_proj[0]
    w_out = out_proj[0]
    w_up = up_proj[0]
    w_down = down_proj[0]

    def segments_of(slot_index):
        seq_ends = jnp.cumsum(lax.dynamic_index_in_dim(line_lengths, slot_index, 0, keepdims=False))
        all_seg = jnp.sum((all_pos[:, None] >= seq_ends[None, :]).astype(jnp.int32), axis=1)
        my_seg = lax.dynamic_slice_in_dim(all_seg, line_row * tok_rows, tok_rows)
        padded = jnp.concatenate([jnp.full((tok_rows,), seq_slots, jnp.int32), all_seg])
        win_seg = lax.dynamic_slice_in_dim(padded, line_row * tok_rows, 2 * tok_rows)
        res_seg = lax.dynamic_slice_in_dim(
            all_seg.reshape(block_count, STRIDE), line_row * residues, residues, 1
        ).T
        dense_mask = allowed(
            my_pos[:, None], my_seg[:, None], all_pos[None, :], all_seg[None, :], strided, seq_slots
        )
        win_mask = allowed(
            my_pos[:, None], my_seg[:, None], win_pos[None, :], win_seg[None, :], False, seq_slots
        )
        res_mask = allowed(
            res_pos[:, :, None],
            res_seg[:, :, None],
            res_pos[:, None, :],
            res_seg[:, None, :],
            True,
            seq_slots,
        )
        return (all_seg, my_seg, dense_mask, win_mask, res_mask)

    def project(hidden):
        normed = gained(hidden, gain_attn).astype(jnp.bfloat16)
        packed = product(normed, w_qkv).astype(jnp.bfloat16)
        return (normed, packed)

    def finish(hidden, attended):
        middle = hidden + product(attended, w_out)
        second = gained(middle, gain_ffn).astype(jnp.bfloat16)
        pre_act = product(second, w_up)
        active = jax.nn.gelu(pre_act, approximate=False).astype(jnp.bfloat16)
        return (middle, second, pre_act, active, middle + product(active, w_down))

    def dense_backward(packed, grad_att, lse_now, masks):
        all_seg, my_seg, dense_mask = (masks[0], masks[1], masks[2])
        queries = packed[:, :model_width]
        key_rows = packed[:, model_width : 2 * model_width]
        values = packed[:, 2 * model_width :]
        keys_all, values_all = (
            lax.all_gather(key_rows, "dp", axis=0, tiled=True),
            lax.all_gather(values, "dp", axis=0, tiled=True),
        )
        grad_q_heads = []
        grad_k_heads = []
        grad_v_heads = []
        delta_heads = []
        for head_index in range(HEADS):
            columns = slice(head_index * head_size, (head_index + 1) * head_size)
            query_head = queries[:, columns]
            out_head = grad_att[:, columns]
            scores = jnp.where(
                dense_mask, contract_cols(query_head, keys_all[:, columns]) * score_scale, NEG
            )
            attn_probs = jnp.exp(scores - lse_now[head_index][:, None])
            grad_probs = contract_cols(out_head, values_all[:, columns])
            delta_row = jnp.sum(attn_probs * grad_probs, axis=1)
            grad_scores = (attn_probs * (grad_probs - delta_row[:, None])).astype(jnp.bfloat16)
            grad_q_heads.append(product(grad_scores, keys_all[:, columns]) * score_scale)
            delta_heads.append(delta_row)
            key_part = contract_rows(grad_scores, query_head) * score_scale
            value_part = contract_rows(attn_probs.astype(jnp.bfloat16), out_head)
            key_mine, value_mine = (
                lax.psum_scatter(
                    key_part.astype(jnp.bfloat16), "dp", scatter_dimension=0, tiled=True
                ).astype(jnp.float32),
                lax.psum_scatter(
                    value_part.astype(jnp.bfloat16), "dp", scatter_dimension=0, tiled=True
                ).astype(jnp.float32),
            )
            grad_k_heads.append(key_mine)
            grad_v_heads.append(value_mine)
        return jnp.concatenate(
            [
                jnp.concatenate(grad_q_heads, axis=1).astype(jnp.bfloat16),
                jnp.concatenate(grad_k_heads, axis=1).astype(jnp.bfloat16),
                jnp.concatenate(grad_v_heads, axis=1).astype(jnp.bfloat16),
            ],
            axis=1,
        )

    received = jnp.zeros((tok_rows, model_width), jnp.bfloat16)
    saved_in = jnp.zeros((micro_count, tok_rows, model_width), jnp.bfloat16)
    saved_att = jnp.zeros((micro_count, tok_rows, model_width), jnp.bfloat16)
    saved_lse = jnp.zeros((micro_count, HEADS, tok_rows), jnp.float32)
    results = jnp.zeros((micro_count, tok_rows, model_width), jnp.bfloat16)
    for tick_index in range(micro_count + 1):
        slot_raw = tick_index - section_index
        is_valid = (slot_raw >= 0) & (slot_raw < micro_count)
        slot_index = jnp.clip(slot_raw, 0, micro_count - 1)
        hidden_low = jnp.where(
            section_index == 0, block_input[min(tick_index, micro_count - 1), 0], received
        )
        hidden = hidden_low.astype(jnp.float32)
        normed, packed = project(hidden)
        masks = segments_of(slot_index)
        dense_dense_mask = masks[2]
        dense_keys_all = lax.all_gather(
            packed[:, model_width : 2 * model_width], "dp", axis=0, tiled=True
        )
        dense_values_all = lax.all_gather(packed[:, 2 * model_width :], "dp", axis=0, tiled=True)
        head_outs = []
        head_lse = []
        for dense_head_index in range(HEADS):
            dense_columns = slice(dense_head_index * head_size, (dense_head_index + 1) * head_size)
            dense_scores = jnp.where(
                dense_dense_mask,
                contract_cols(packed[:, dense_columns], dense_keys_all[:, dense_columns])
                * score_scale,
                NEG,
            )
            dense_attn_probs, lse_row = softmax_parts(dense_scores)
            head_outs.append(product(dense_attn_probs, dense_values_all[:, dense_columns]))
            head_lse.append(lse_row)
        attended = jnp.concatenate(head_outs, axis=1).astype(jnp.bfloat16)
        lse_rows = jnp.stack(head_lse)
        output = finish(hidden, attended)[4].astype(jnp.bfloat16)
        saved_in = put_row(saved_in, hidden_low, slot_index, is_valid)
        saved_att = put_row(saved_att, attended, slot_index, is_valid)
        saved_lse = put_row(saved_lse, lse_rows, slot_index, is_valid)
        results = put_row(results, output, slot_index, is_valid)
        if tick_index < micro_count:
            received = from_behind(output, "section", 1)
    totals = (
        jnp.zeros((model_width,), jnp.float32),
        jnp.zeros(w_qkv.shape, jnp.float32),
        jnp.zeros(w_out.shape, jnp.float32),
        jnp.zeros((model_width,), jnp.float32),
        jnp.zeros(w_up.shape, jnp.float32),
        jnp.zeros(w_down.shape, jnp.float32),
    )
    sent_back = jnp.zeros((tok_rows, model_width), jnp.bfloat16)
    input_grads = jnp.zeros((micro_count, tok_rows, model_width), jnp.bfloat16)
    for tick_index in range(micro_count + 1):
        slot_raw = tick_index - (1 - section_index)
        is_valid = (slot_raw >= 0) & (slot_raw < micro_count)
        slot_index = jnp.clip(slot_raw, 0, micro_count - 1)
        grad_out = jnp.where(
            section_index == 1, output_grad[min(tick_index, micro_count - 1), 0], sent_back
        )
        hidden = lax.dynamic_index_in_dim(saved_in, slot_index, 0, keepdims=False).astype(
            jnp.float32
        )
        attended = lax.dynamic_index_in_dim(saved_att, slot_index, 0, keepdims=False)
        lse_now = lax.dynamic_index_in_dim(saved_lse, slot_index, 0, keepdims=False)
        normed, packed = project(hidden)
        middle, second, pre_act, active, _ = finish(hidden, attended)
        grad_down = contract_rows(active, grad_out)
        grad_active = contract_cols(grad_out, w_down)
        gelu_back = jax.vjp(partial(jax.nn.gelu, approximate=False), pre_act)[1]
        grad_pre = gelu_back(grad_active)[0].astype(jnp.bfloat16)
        grad_up = contract_rows(second, grad_pre)
        ffn_back = jax.vjp(gained, middle, gain_ffn)[1]
        grad_mid_norm, grad_gain_ffn = ffn_back(contract_cols(grad_pre, w_up))
        grad_middle = grad_out.astype(jnp.float32) + grad_mid_norm
        grad_branch = grad_middle.astype(jnp.bfloat16)
        grad_outproj = contract_rows(attended, grad_branch)
        grad_att = contract_cols(grad_branch, w_out).astype(jnp.bfloat16)
        masks = segments_of(slot_index)
        grad_packed = dense_backward(packed, grad_att, lse_now, masks)
        grad_qkv = contract_rows(normed, grad_packed)
        attn_back = jax.vjp(gained, hidden, gain_attn)[1]
        grad_hid_norm, grad_gain_attn = attn_back(contract_cols(grad_packed, w_qkv))
        grad_hidden = (grad_middle + grad_hid_norm).astype(jnp.bfloat16)
        terms = (grad_gain_attn, grad_qkv, grad_outproj, grad_gain_ffn, grad_up, grad_down)
        totals = tuple(
            (
                running + jnp.where(is_valid, term_now, 0.0)
                for running, term_now in zip(totals, terms)
            )
        )
        input_grads = put_row(input_grads, grad_hidden, slot_index, is_valid)
        if tick_index < micro_count:
            sent_back = from_behind(grad_hidden, "section", -1)
    summed = lax.psum(
        (totals[0], totals[1], totals[2], totals[3], totals[4], totals[5]), ("dp", "rep")
    )
    return (
        results[None, :, None],
        input_grads[None, :, None],
        summed[0][None],
        summed[1][None],
        summed[2][None],
        summed[3][None],
        summed[4][None],
        summed[5][None],
    )


BF = jnp.bfloat16
F32 = jnp.float32
MIB = 1024 * 1024
GAIN_ROWS = 16


def call(body, scalars, arrays, shapes, mib=24, micros=1.0, scratch=(), held=0, out_held=()):
    in_specs = [pl.BlockSpec(memory_space=pltpu.SMEM)] * len(scalars)
    in_specs += [pl.BlockSpec(memory_space=pl.ANY)] * held
    in_specs += [pl.BlockSpec(memory_space=pltpu.VMEM)] * (len(arrays) - held)
    return pl.pallas_call(
        body,
        out_shape=tuple(jax.ShapeDtypeStruct(*shape) for shape in shapes),
        in_specs=in_specs,
        out_specs=tuple(
            pl.BlockSpec(memory_space=pl.ANY if index in out_held else pltpu.VMEM)
            for index in range(len(shapes))
        ),
        scratch_shapes=list(scratch),
        compiler_params=pltpu.CompilerParams(vmem_limit_bytes=mib * MIB),
        cost_estimate=pl.CostEstimate(
            flops=int(micros * 1.1e9), bytes_accessed=int(micros * 3.4e6), transcendentals=0
        ),
    )(
        *scalars,
        *(pltpu.with_memory_space_constraint(array, pltpu.HBM) for array in arrays[:held]),
        *arrays[held:],
    )


def my_section():
    return lax.axis_index("section")


def my_line():
    return lax.axis_index("dp")


def my_flip(core):
    rep = lax.axis_index("rep")
    low, high = rep & 1, rep >> 1
    return 2 * low + high if core == 0 else 2 * high + low


def rows_at(start, count):
    return pl.ds(pl.multiple_of(start, count), count)


def segment_at(ends, position):
    total = jnp.zeros(position.shape, jnp.int32)
    for end in ends:
        total = total + (position >= end).astype(jnp.int32)
    return total


def ends_of(lengths):
    ends = []
    so_far = jnp.int32(0)
    for slot in range(lengths.shape[2]):
        so_far = so_far + lengths[my_line(), lax.axis_index("rep"), slot]
        ends.append(so_far)
    return ends


def write_masks(lengths, window_mask, strided_mask):
    section = my_section()
    rows, reach = window_mask.shape
    half = rows // 4
    block = 2 * half
    ends = ends_of(lengths)
    row = lax.broadcasted_iota(jnp.int32, (rows, reach), 0)
    query_pos = block * (row // half) + section * half + (row & (half - 1))
    key_pos = query_pos - (row & (half - 1)) - block
    key_pos = key_pos + lax.broadcasted_iota(jnp.int32, (rows, reach), 1)
    offset = query_pos - key_pos
    segment = segment_at(ends, query_pos)
    same = (segment == segment_at(ends, key_pos)) & (segment < len(ends)) & (key_pos >= 0)
    allow = same & (offset >= 0) & (offset < STRIDE) | (offset == 0)
    window_mask[...] = allow.astype(F32)

    def place(axis):
        index = lax.broadcasted_iota(jnp.int32, (rows, rows), axis)
        return block * (index // half) + section * half + (index & (half - 1))

    query_pos, key_pos = place(0), place(1)
    offset = query_pos - key_pos
    segment = segment_at(ends, query_pos)
    same = (segment == segment_at(ends, key_pos)) & (segment < len(ends))
    allow = same & (offset >= 0) & ((offset & (STRIDE - 1)) == 0) | (offset == 0)
    strided_mask[...] = allow.astype(F32)


def pack_kernel(tokens, grads, gain_attn, gain_ffn, lengths, *rest):
    *pieces, window_mask, strided_mask, gains, lengths_held, sems, side_sems = rest
    block = tokens.shape[2]
    half = block // 2
    rows = rows_at(my_section() * half, half)
    side = [
        pltpu.make_async_copy(lengths, lengths_held, side_sems.at[2]),
        pltpu.make_async_copy(gain_attn, gains.at[0], side_sems.at[0]),
        pltpu.make_async_copy(gain_ffn, gains.at[1], side_sems.at[1]),
    ]
    copies = []
    for step, piece in enumerate(pieces):
        micro = my_line() ^ step
        for part, source in enumerate((tokens, grads)):
            copies.append(
                pltpu.make_async_copy(
                    source.at[micro, 0, rows],
                    piece.at[part * half : (part + 1) * half],
                    sems.at[2 * step + part],
                )
            )
    for copy in (*side, *copies):
        copy.start()
    for copy in side:
        copy.wait()
    write_masks(lengths_held, window_mask, strided_mask)
    pieces[0][block:, :] = jnp.concatenate(
        [
            gains[0].astype(F32),
            gains[1].astype(F32),
            jnp.zeros((pieces[0].shape[0] - block - 2, gains.shape[2]), F32),
        ],
        axis=0,
    ).astype(BF)
    for copy in copies:
        copy.wait()


def unit(values):
    centered = values - jnp.mean(values, axis=-1, keepdims=True)
    inverse = lax.rsqrt(jnp.mean(centered * centered, axis=-1, keepdims=True) + 1e-05)
    return centered * inverse, inverse


def unit_back(grad, normal, inverse):
    return inverse * (
        grad
        - jnp.mean(grad, axis=-1, keepdims=True)
        - normal * jnp.mean(grad * normal, axis=-1, keepdims=True)
    )


def widened(column, width):
    return jnp.broadcast_to(column, (column.shape[0], width))


def normalized_exp(scores):
    shifted = jnp.exp(scores - jnp.max(scores, axis=-1, keepdims=True))
    return shifted * (1.0 / jnp.sum(shifted, axis=-1, keepdims=True))


def ffn_forward(hidden, attended, gain, w_out, w_up, w_down, saved):
    result, middle_unit, middle_inverse, second_ref, active, slope = saved
    middle = hidden + product(attended, w_out)
    normal, inverse = unit(middle)
    middle_unit[...] = normal
    middle_inverse[...] = widened(inverse, middle_inverse.shape[1])
    second = (normal * gain).astype(BF)
    second_ref[...] = second
    chunk = middle.shape[1]
    total = middle
    for index in range(w_up.shape[1] // chunk):
        columns = slice(index * chunk, (index + 1) * chunk)
        pre_act = product(second, w_up[:, columns])
        below = 0.5 + 0.5 * lax.erf(pre_act * (0.5**0.5))
        now = (pre_act * below).astype(BF)
        active[:, columns] = now
        slope[:, columns] = below + pre_act * (
            jnp.exp(-0.5 * pre_act * pre_act) * 0.3989422804014327
        )
        total = total + product(now, w_down[columns, :])
    result[...] = total.astype(BF)


def own_unit(spot, half):
    return slice((2 * spot + 2) * half, (2 * spot + 3) * half)


def key_units(spot, half):
    return slice(2 * spot * half, (2 * spot + 3) * half)


def zero_forward_kernel(
    mask,
    own0,
    own1,
    own2,
    own3,
    far0,
    far1,
    far2,
    far3,
    w_qkv,
    w_out,
    w_up,
    w_down,
    gains,
    line,
    normal_all,
    inverse_all,
    normed_all,
    query,
    padded,
    probs_ref,
    attended_ref,
    cotangent,
    *saved,
):
    section = my_section()
    reached, width = normal_all.shape
    half = line.shape[0] // 10
    block = 2 * half
    blocks = 4
    rows = blocks * half
    head = width // HEADS
    scale = float(head) ** (-0.5)
    reach = block + half
    line[:block, :] = jnp.zeros((block, width), BF)
    for step, (near, far) in enumerate(((own0, far0), (own1, far1), (own2, far2), (own3, far3))):
        spot = my_line() ^ step
        line[rows_at(spot * block + block, half), :] = near[:half, :]
        line[rows_at(spot * block + block + half - section * block, half), :] = far[:half, :]
        cotangent[rows_at(spot * half, half), :] = near[half:block, :]
    normal, inverse = unit(line[:reached, :].astype(F32))
    normal_all[...] = normal
    inverse_all[...] = widened(inverse, inverse_all.shape[1])
    normed = (normal * gains[0, 0:1, :]).astype(BF)
    normed_all[...] = normed
    padded[...] = product(normed, w_qkv[0, :, width:]).astype(BF)
    normed_mine = jnp.concatenate(
        [normed[own_unit(spot, half), :] for spot in range(blocks)], axis=0
    )
    query[...] = product(normed_mine, w_qkv[0, :, :width]).astype(BF)
    spots = [(slice(spot * half, (spot + 1) * half), key_units(spot, half)) for spot in range(blocks)]
    heads = [
        (slice(number * head, (number + 1) * head), slice(width + number * head, width + (number + 1) * head))
        for number in range(HEADS)
    ]
    scores = [
        jnp.concatenate(
            [contract_cols(query[here, columns], padded[window, columns]) for here, window in spots],
            axis=0,
        )
        for columns, _ in heads
    ]
    probs = [normalized_exp(jnp.where(mask[...] > 0.5, values * scale, NEG)) for values in scores]
    attended = []
    for number, (_, value_columns) in enumerate(heads):
        probs_ref[number] = probs[number]
        low = probs[number].astype(BF)
        attended.append(
            jnp.concatenate(
                [product(low[here, :], padded[window, value_columns]) for here, window in spots], axis=0
            )
        )
    attended = jnp.concatenate(attended, axis=1).astype(BF)
    attended_ref[...] = attended
    hidden = jnp.concatenate([line[own_unit(spot, half), :] for spot in range(blocks)], axis=0)
    ffn_forward(
        hidden.astype(F32), attended, gains[0, 1:2, :], w_out[0], w_up.at[0], w_down.at[0], saved
    )


def one_forward_kernel(
    mask,
    hidden_ref,
    w_qkv,
    w_out,
    w_up,
    w_down,
    gains,
    normal_ref,
    inverse_ref,
    normed_ref,
    packed,
    probs_ref,
    attended_ref,
    *saved,
):
    section = my_section()
    rows, width = hidden_ref.shape
    half = rows // 4
    block = 2 * half
    head = width // HEADS
    scale = float(head) ** (-0.5)
    hidden = hidden_ref[...].astype(F32)
    normal, inverse = unit(hidden)
    normal_ref[...] = normal
    inverse_ref[...] = widened(inverse, inverse_ref.shape[1])
    normed = (normal * gains[1, 0:1, :]).astype(BF)
    normed_ref[...] = normed
    packed[...] = product(normed, w_qkv[1]).astype(BF)
    heads = [
        tuple(
            slice(part * width + number * head, part * width + (number + 1) * head) for part in range(3)
        )
        for number in range(HEADS)
    ]
    scores = [contract_cols(packed[:, near], packed[:, far]) for near, far, _ in heads]
    probs = [normalized_exp(jnp.where(mask[...] > 0.5, values * scale, NEG)) for values in scores]
    parts = []
    for number, (_, _, value_columns) in enumerate(heads):
        probs_ref[number] = probs[number]
        parts.append(product(probs[number].astype(BF), packed[:, value_columns]))
    attended = jnp.concatenate(parts, axis=1).astype(BF)
    attended_ref[...] = attended
    ffn_forward(hidden, attended, gains[1, 1:2, :], w_out[1], w_up.at[1], w_down.at[1], saved)


def store_block(terms, number, value):
    width = value.shape[1]
    unit_rows = width // 2
    core, number = divmod(number, 6)
    side, flip = my_section() ^ core, my_flip(core)
    value = value.astype(BF)
    for part in range(2):
        quarter, place = divmod(2 * number + part, 3)
        terms[side, flip ^ quarter, place * unit_rows : (place + 1) * unit_rows, :] = value[
            part * unit_rows : (part + 1) * unit_rows, :
        ]


def store_gains(terms, attn_term, ffn_term):
    spare, width = terms.shape[2] - GAIN_ROWS, terms.shape[3]
    value = jnp.concatenate(
        [attn_term, ffn_term, jnp.zeros((GAIN_ROWS - 2, width), F32)], axis=0
    ).astype(BF)
    for side in range(2):
        for quarter in range(4):
            terms[side, quarter, spare:, :] = value


def ffn_input_grad(grad_out, saved, gain, w_out, w_up, w_down, grad_pre_ref):
    middle_unit, middle_inverse, slope = saved
    width = grad_out.shape[1]
    grad_second = None
    for index in range(w_up.shape[1] // width):
        columns = slice(index * width, (index + 1) * width)
        grad_active = contract_cols(grad_out, w_down[columns, :])
        grad_pre = (grad_active * slope[:, columns]).astype(BF)
        grad_pre_ref[:, columns] = grad_pre
        term = contract_cols(grad_pre, w_up[:, columns])
        grad_second = term if grad_second is None else grad_second + term
    normal = middle_unit[...]
    gain_term = jnp.sum(grad_second * normal, axis=0, keepdims=True)
    grad_middle = grad_out.astype(F32) + unit_back(
        grad_second * gain, normal, middle_inverse[:, 0:1]
    )
    return grad_middle, contract_cols(grad_middle.astype(BF), w_out).astype(BF), gain_term


def ffn_weight_grads(terms, grad_out, grad_middle, second, active, attended, grad_pre):
    width = grad_out.shape[1]
    store_block(terms, 3, contract_rows(attended[...], grad_middle.astype(BF)))
    for index in range(active.shape[1] // width):
        columns = slice(index * width, (index + 1) * width)
        store_block(terms, 4 + index, contract_rows(second[...], grad_pre[:, columns]))
        store_block(terms, 8 + index, contract_rows(active[:, columns], grad_out))


def one_backward_kernel(
    grad_ref,
    w_qkv,
    w_out,
    w_up,
    w_down,
    gains,
    normal_ref,
    inverse_ref,
    normed_ref,
    packed,
    probs_ref,
    *rest,
):
    middle_unit, middle_inverse, second, active, slope, attended, grad_in, terms, grad_pre = rest
    width = grad_ref.shape[1]
    head = width // HEADS
    scale = float(head) ** (-0.5)
    grad_out = grad_ref[...]
    grad_middle, grad_att, ffn_term = ffn_input_grad(
        grad_out,
        (middle_unit, middle_inverse, slope),
        gains[1, 1:2, :],
        w_out[1],
        w_up.at[1],
        w_down.at[1],
        grad_pre,
    )
    ffn_weight_grads(terms, grad_out, grad_middle, second, active, attended, grad_pre)
    heads = [
        tuple(
            slice(part * width + number * head, part * width + (number + 1) * head) for part in range(3)
        )
        for number in range(HEADS)
    ]
    probs = [probs_ref[number] for number in range(HEADS)]
    grad_probs = [
        contract_cols(grad_att[:, near], packed[:, value_columns]) for near, _, value_columns in heads
    ]
    grad_scores = [
        (prob * (grad - jnp.sum(prob * grad, axis=-1, keepdims=True))).astype(BF)
        for prob, grad in zip(probs, grad_probs)
    ]
    grad_parts = [
        [product(grad, packed[:, far]) * scale for grad, (_, far, _) in zip(grad_scores, heads)],
        [contract_rows(grad, packed[:, near]) * scale for grad, (near, _, _) in zip(grad_scores, heads)],
        [contract_rows(prob.astype(BF), grad_att[:, near]) for prob, (near, _, _) in zip(probs, heads)],
    ]
    grad_normed = None
    for index in range(3):
        columns = slice(index * width, (index + 1) * width)
        grad_block = jnp.concatenate(grad_parts[index], axis=1).astype(BF)
        term = contract_cols(grad_block, w_qkv[1, :, columns])
        grad_normed = term if grad_normed is None else grad_normed + term
        store_block(terms, index, contract_rows(normed_ref[...], grad_block))
    normal = normal_ref[...]
    store_gains(terms, jnp.sum(grad_normed * normal, axis=0, keepdims=True), ffn_term)
    grad_in[...] = (
        grad_middle + unit_back(grad_normed * gains[1, 0:1, :], normal, inverse_ref[:, 0:1])
    ).astype(BF)


def zero_ffn_kernel(
    grad_ref,
    w_out,
    w_up,
    w_down,
    gains,
    middle_unit,
    middle_inverse,
    slope,
    grad_middle_ref,
    grad_att_ref,
    grad_pre,
    gain_term,
):
    grad_middle, grad_att, term = ffn_input_grad(
        grad_ref[...],
        (middle_unit, middle_inverse, slope),
        gains[0, 1:2, :],
        w_out[0],
        w_up.at[0],
        w_down.at[0],
        grad_pre,
    )
    grad_middle_ref[...] = grad_middle
    grad_att_ref[...] = grad_att
    gain_term[...] = term


def zero_backward_kernel(
    grad_ref,
    w_qkv,
    gains,
    normal_all,
    inverse_all,
    normed_all,
    query,
    padded,
    probs_ref,
    result_zero,
    result_one,
    second,
    active,
    attended,
    grad_middle_ref,
    grad_att_ref,
    grad_pre,
    ffn_term,
    result_keep,
    grad_line,
    swap,
    terms,
):
    section = my_section()
    rows, width = grad_ref.shape
    reached = normal_all.shape[0]
    half = rows // 4
    blocks = 4
    head = width // HEADS
    scale = float(head) ** (-0.5)
    grad_out = grad_ref[...]

    @pl.when(section == 0)
    def _():
        result_keep[...] = result_zero[...]
        swap[:rows, :] = result_one[...]

    @pl.when(section == 1)
    def _():
        result_keep[...] = result_one[...]
        swap[:rows, :] = result_zero[...]

    grad_middle = grad_middle_ref[...]
    grad_att = grad_att_ref[...]
    ffn_weight_grads(terms, grad_out, grad_middle, second, active, attended, grad_pre)
    spots = [(slice(spot * half, (spot + 1) * half), key_units(spot, half)) for spot in range(blocks)]
    heads = [
        (slice(number * head, (number + 1) * head), slice(width + number * head, width + (number + 1) * head))
        for number in range(HEADS)
    ]
    probs = [probs_ref[number] for number in range(HEADS)]
    grad_probs = [
        jnp.concatenate(
            [
                contract_cols(grad_att[here, columns], padded[window, value_columns])
                for here, window in spots
            ],
            axis=0,
        )
        for columns, value_columns in heads
    ]
    grad_scores = [
        (prob * (grad - jnp.sum(prob * grad, axis=-1, keepdims=True))).astype(BF)
        for prob, grad in zip(probs, grad_probs)
    ]
    grad_query = [
        jnp.concatenate(
            [product(grad[here, :], padded[window, columns]) for here, window in spots], axis=0
        )
        * scale
        for grad, (columns, _) in zip(grad_scores, heads)
    ]
    grad_query = jnp.concatenate(grad_query, axis=1).astype(BF)

    def gathered(lefts, right):
        parts = []
        for left, (columns, _) in zip(lefts, heads):
            terms_of = [contract_rows(left[here, :], right[here, columns]) for here, _ in spots]
            units = []
            for index in range(reached // half):
                spot, place = divmod(index, 2)
                held = None
                if spot < blocks:
                    held = terms_of[spot][place * half : (place + 1) * half, :]
                if place == 0 and spot > 0:
                    last = terms_of[spot - 1][2 * half :, :]
                    held = last if held is None else held + last
                units.append(held)
            parts.append(jnp.concatenate(units, axis=0))
        return jnp.concatenate(parts, axis=1)

    grad_keys = (gathered(grad_scores, query) * scale).astype(BF)
    grad_values = gathered([prob.astype(BF) for prob in probs], grad_att).astype(BF)
    normed = normed_all[...]
    normed_mine = jnp.concatenate(
        [normed[own_unit(spot, half), :] for spot in range(blocks)], axis=0
    )
    store_block(terms, 0, contract_rows(normed_mine, grad_query))
    store_block(terms, 1, contract_rows(normed, grad_keys))
    store_block(terms, 2, contract_rows(normed, grad_values))
    from_query = contract_cols(grad_query, w_qkv[0, :, :width])
    grad_line[:reached, :] = contract_cols(
        grad_keys, w_qkv[0, :, width : 2 * width]
    ) + contract_cols(grad_values, w_qkv[0, :, 2 * width :])
    for spot in range(blocks):
        grad_line[own_unit(spot, half), :] += from_query[spot * half : (spot + 1) * half, :]
    grad_normed = grad_line[:reached, :]
    normal = normal_all[...]
    store_gains(terms, jnp.sum(grad_normed * normal, axis=0, keepdims=True), ffn_term[...])
    grad_line[:reached, :] = unit_back(grad_normed * gains[0, 0:1, :], normal, inverse_all[:, 0:1])
    for spot in range(blocks):
        grad_line[own_unit(spot, half), :] += grad_middle[spot * half : (spot + 1) * half, :]
    grad_line[reached:, :] = jnp.zeros((grad_line.shape[0] - reached, width), F32)

    @pl.when(section == 0)
    def _():
        swap[rows : 2 * rows, :] = grad_out

    @pl.when(section == 1)
    def _():
        swap[rows:, :] = grad_line[:reached, :].astype(BF)


def share_kernel(keep, one_near, zero_near, came, *pieces):
    rows = keep.shape[0]
    half = rows // 4
    block = 2 * half
    section = my_section()
    near_rows = rows_at(section * half, half)
    far_rows = rows_at(half - section * half, half)
    for step, piece in enumerate(pieces):
        spot = my_line() ^ step
        mine = rows_at(spot * half, half)
        piece[near_rows, :] = keep[mine, :]
        piece[far_rows, :] = came[mine, :]

    @pl.when(section == 0)
    def _():
        for step, piece in enumerate(pieces):
            base = (my_line() ^ step) * block
            near, far = rows_at(base + block, block), rows_at(rows + base + half, half)
            far = pl.ds(far.start, block)
            piece[block:, :] = (zero_near[near, :] + came[far, :].astype(F32)).astype(BF)

    @pl.when(section == 1)
    def _():
        for step, piece in enumerate(pieces):
            spot = my_line() ^ step
            piece[block : block + half, :] = came[rows_at(rows + spot * half, half), :]
            piece[block + half :, :] = one_near[rows_at(spot * half, half), :]


def settle_kernel(piece0, piece1, piece2, piece3, results, input_grads):
    block = piece0.shape[0] // 2
    for step, piece in enumerate((piece0, piece1, piece2, piece3)):
        micro = my_line() ^ step
        results[0, micro, 0] = piece[:block, :]
        input_grads[0, micro, 0] = piece[block:, :]


def finish_kernel(zero_near, zero_far, one_near, one_far, *rest):
    gain_attn, qkv, out, gain_ffn, up, down, qkv_held, out_held, up_held, down_held, sems = rest
    width = zero_near.shape[2]
    unit_rows = width // 2
    targets = [(qkv_held, qkv, (slice(None), slice(n * width, (n + 1) * width))) for n in range(3)]
    targets.append((out_held, out, (slice(None), slice(None))))
    targets += [(up_held, up, (slice(None), slice(n * width, (n + 1) * width))) for n in range(4)]
    targets += [(down_held, down, (slice(n * width, (n + 1) * width), slice(None))) for n in range(4)]

    def write(halves):
        copies = []
        for number, (held, target, (rows, columns)) in enumerate(targets):
            core, place = divmod(number, 6)
            start = rows.start or 0
            for part in range(2):
                quarter, spot = divmod(2 * place + part, 3)
                value = halves[core][
                    my_flip(core) ^ quarter, spot * unit_rows : (spot + 1) * unit_rows, :
                ]
                first = start + part * unit_rows
                held[first : first + unit_rows, columns] = value.astype(F32)
            copies.append(
                pltpu.make_async_copy(
                    held.at[rows, columns], target.at[0, rows, columns], sems.at[number]
                )
            )
            copies[-1].start()
        spare = halves[0][my_flip(0), zero_near.shape[1] - GAIN_ROWS :, :].astype(F32)
        gain_attn[...] = spare[0:1, :]
        gain_ffn[...] = spare[1:2, :]
        for copy in copies:
            copy.wait()

    @pl.when(my_section() == 0)
    def _():
        write((zero_near, zero_far))

    @pl.when(my_section() == 1)
    def _():
        write((one_far, one_near))


SWAP = [(0, 1), (1, 0)]
PLANE = ("section", "rep")


def crossed(flips):
    return [(4 * s + g, 4 * s + (g ^ flips[s])) for s in range(2) for g in range(4)]


FIRST = crossed((1, 2))
SECOND = crossed((2, 1))


def along_line(value, step):
    return lax.ppermute(value, "dp", [(z, z ^ step) for z in range(4)])


def reduce_terms(terms, came, zed, along=()):
    bar = lax.optimization_barrier
    first = lax.ppermute(terms[0, 2:4] + came[2:4], PLANE, FIRST)
    second = lax.ppermute(terms[0, 1] + came[1] + first[1], PLANE, SECOND)
    total = bar(terms[0, 0] + came[0] + first[0] + second)
    if along:
        total, *along = bar((total, *along))
    total = bar(total + along_line(total, 1))
    half = total.shape[0] // 2
    odd = zed & 1
    mine = lax.dynamic_slice_in_dim(total, odd * half, half, 0)
    mine = bar(mine + along_line(mine, 2))
    other = along_line(mine, 1)
    total = bar(
        jnp.where(
            odd == 0, jnp.concatenate([mine, other]), jnp.concatenate([other, mine])
        )
    )
    pair = jnp.stack([total, lax.ppermute(total, PLANE, SECOND)])
    return pair, lax.ppermute(pair, PLANE, FIRST), along


def lines(
    block_input,
    output_grad,
    seq_lengths,
    attn_gain,
    qkv_proj,
    out_proj,
    ffn_gain,
    up_proj,
    down_proj,
):
    section = lax.axis_index("section")
    zed = lax.axis_index("dp")
    micro_count, _, block, width = block_input.shape
    hidden_units = up_proj.shape[2]
    half = block // 2
    rows, reach = micro_count * half, block + half
    reached = rows + rows + half
    term_rows = 6 * width // 4 + GAIN_ROWS

    *packed, window_mask, strided_mask = call(
        pack_kernel,
        (),
        (block_input, output_grad, attn_gain, ffn_gain, seq_lengths),
        (
            ((block + 16, width), BF),
            *((((block, width), BF),) * (micro_count - 1)),
            ((rows, reach), F32),
            ((rows, rows), F32),
        ),
        8,
        scratch=(
            pltpu.VMEM((2, 1, width), BF),
            pltpu.SMEM(seq_lengths.shape, jnp.int32),
            pltpu.SemaphoreType.DMA((2 * micro_count,)),
            pltpu.SemaphoreType.DMA((3,)),
        ),
        held=5,
    )
    near = [packed[0]] + [along_line(packed[step], step) for step in range(1, micro_count)]
    far = [lax.ppermute(piece, "section", SWAP) for piece in near]
    own = (qkv_proj[0], out_proj[0], up_proj[0], down_proj[0])
    near[1], *own = lax.optimization_barrier((near[1], *own))
    swapped = [lax.ppermute(weight, "section", SWAP) for weight in own]
    weights = tuple(
        jnp.stack([jnp.where(section == 0, a, b), jnp.where(section == 0, b, a)])
        for a, b in zip(own, swapped)
    )
    gains_near, gains_far = near[0][block:].astype(F32), far[0][block:].astype(F32)
    weights += (
        jnp.stack(
            [
                jnp.where(section == 0, gains_near, gains_far),
                jnp.where(section == 0, gains_far, gains_near),
            ]
        ),
    )
    ffn_saved = (
        ((rows, width), BF),
        ((rows, width), F32),
        ((rows, 128), F32),
        ((rows, width), BF),
        ((rows, hidden_units), BF),
        ((rows, hidden_units), F32),
    )
    (
        _,
        normal_all,
        inverse_all,
        normed_all,
        query,
        padded,
        probs_zero,
        attended_zero,
        cotangent,
        result_zero,
        *saved_zero,
    ) = call(
        zero_forward_kernel,
        (),
        (window_mask, *near, *far, *weights),
        (
            ((reached + half, width), BF),
            ((reached, width), F32),
            ((reached, 128), F32),
            ((reached, width), BF),
            ((rows, width), BF),
            ((reached, 2 * width), BF),
            ((HEADS, rows, reach), F32),
            ((rows, width), BF),
            ((rows, width), BF),
            *ffn_saved,
        ),
    )
    (
        normal_one,
        inverse_one,
        normed_one,
        packed_one,
        probs_one,
        attended_one,
        result_one,
        *saved_one,
    ) = call(
        one_forward_kernel,
        (),
        (strided_mask, result_zero, *weights),
        (
            ((rows, width), F32),
            ((rows, 128), F32),
            ((rows, width), BF),
            ((rows, 3 * width), BF),
            ((HEADS, rows, rows), F32),
            ((rows, width), BF),
            *ffn_saved,
        ),
    )
    middle_one, mid_inverse_one, second_one, active_one, slope_one = saved_one
    grad_one, terms_one, _ = call(
        one_backward_kernel,
        (),
        (
            cotangent,
            *weights,
            normal_one,
            inverse_one,
            normed_one,
            packed_one,
            probs_one,
            middle_one,
            mid_inverse_one,
            second_one,
            active_one,
            slope_one,
            attended_one,
        ),
        (((rows, width), BF), ((2, 4, term_rows, width), BF), ((rows, hidden_units), BF)),
        micros=3.0,
    )
    middle_zero, mid_inverse_zero, second_zero, active_zero, slope_zero = saved_zero
    came_one = lax.ppermute(terms_one[1], "section", SWAP)
    w_qkv, w_out, w_up, w_down, gains = weights
    zero_ffn = call(
        zero_ffn_kernel,
        (),
        (grad_one, w_out, w_up, w_down, gains, middle_zero, mid_inverse_zero, slope_zero),
        (
            ((rows, width), F32),
            ((rows, width), BF),
            ((rows, hidden_units), BF),
            ((1, width), F32),
        ),
        micros=2.0,
    )
    result_keep, grad_line, swap, terms_zero = call(
        zero_backward_kernel,
        (),
        (
            grad_one,
            w_qkv,
            gains,
            normal_all,
            inverse_all,
            normed_all,
            query,
            padded,
            probs_zero,
            result_zero,
            result_one,
            second_zero,
            active_zero,
            attended_zero,
            *zero_ffn,
        ),
        (
            ((rows, width), BF),
            ((reached + half, width), F32),
            ((rows + reached, width), BF),
            ((2, 4, term_rows, width), BF),
        ),
        micros=4.0,
    )
    came = lax.ppermute(swap, "section", SWAP)
    shared = call(
        share_kernel,
        (),
        (result_keep, grad_one, grad_line, came),
        (((2 * block, width), BF),) * micro_count,
        8,
    )
    home = [shared[0]] + [along_line(shared[step], step) for step in range(1, micro_count)]
    came_zero = lax.ppermute(terms_zero[1], "section", SWAP)
    one_pair, one_first, home = reduce_terms(terms_one, came_one, zed, home)
    results, input_grads = call(
        settle_kernel,
        (),
        home,
        (((1, micro_count, 1, block, width), BF),) * 2,
        8,
    )
    zero_pair, zero_first, _ = reduce_terms(terms_zero, came_zero, zed)

    def both_cores(parts, pairs):
        near = jnp.concatenate(parts)
        return near, jnp.concatenate([lax.ppermute(part, "section", pairs) for part in parts])

    sums = call(
        finish_kernel,
        (),
        (*both_cores((zero_pair, zero_first), [(1, 0)]), *both_cores((one_pair, one_first), [(0, 1)])),
        (
            ((1, width), F32),
            ((1, width, 3 * width), F32),
            ((1, width, width), F32),
            ((1, width), F32),
            ((1, width, hidden_units), F32),
            ((1, hidden_units, width), F32),
        ),
        24,
        scratch=(
            pltpu.VMEM((width, 3 * width), F32),
            pltpu.VMEM((width, width), F32),
            pltpu.VMEM((width, hidden_units), F32),
            pltpu.VMEM((hidden_units, width), F32),
            pltpu.SemaphoreType.DMA((12,)),
        ),
        out_held=(1, 2, 4, 5),
    )
    return (results, input_grads, *sums)


def local(*arrays):
    micro_count, _, tok_rows, model_width = arrays[0].shape
    one_line_per_chip = (
        lax.axis_size("section") == 2
        and lax.axis_size("dp") == 4
        and lax.axis_size("rep") == 4
        and micro_count == 4
        and tok_rows == STRIDE
        and model_width == 256
        and arrays[7].shape[2] == 4 * model_width
    )
    return lines(*arrays) if one_line_per_chip else general(*arrays)


def solution(mesh):
    placed = (
        P(None, "rep", "dp", None),
        P(None, "rep", "dp", None),
        P(),
        P("section", None),
        P("section", None, None),
        P("section", None, None),
        P("section", None),
        P("section", None, None),
        P("section", None, None),
    )
    return jax.shard_map(
        local,
        mesh=mesh,
        in_specs=placed,
        out_specs=(
            P("section", None, "rep", "dp", None),
            P("section", None, "rep", "dp", None),
            P("section", None),
            P("section", None, None),
            P("section", None, None),
            P("section", None),
            P("section", None, None),
            P("section", None, None),
        ),
        check_vma=False,
    )
```

```python
from functools import partial

import jax
import jax.numpy as jnp
from jax import lax
from jax.experimental import pallas as pl
from jax.experimental.pallas import tpu as pltpu
from jax.sharding import PartitionSpec as P

HEADS = 2
STRIDE = 128


NEG = -1e30


def from_behind(shard, axis, by):
    length = lax.axis_size(axis)
    pairs = [(i, i + by) for i in range(length) if 0 <= i + by < length]
    return lax.ppermute(shard, axis, pairs)


def normalize(values):
    centered = values - jnp.mean(values, axis=-1, keepdims=True)
    spread = jnp.mean(centered * centered, axis=-1, keepdims=True)
    return centered * lax.rsqrt(spread + 1e-05)


def gained(values, gain):
    return normalize(values) * gain


def allowed(query_pos, query_seg, key_pos, key_seg, strided, seq_slots):
    offset = query_pos - key_pos
    same_seq = (query_seg == key_seg) & (query_seg < seq_slots)
    nearby = (offset >= 0) & (offset < STRIDE)
    spaced = (offset >= 0) & (offset % STRIDE == 0)
    pattern = jnp.where(strided, spaced, nearby)
    return same_seq & pattern | (offset == 0)


def product(left, right):
    return jnp.dot(left, right, preferred_element_type=jnp.float32)


def contract_rows(left, right):
    return lax.dot_general(
        left, right, (((0,), (0,)), ((), ())), preferred_element_type=jnp.float32
    )


def contract_cols(left, right):
    return lax.dot_general(
        left, right, (((1,), (1,)), ((), ())), preferred_element_type=jnp.float32
    )


def put_row(buffer, value, slot_index, is_valid):
    current = lax.dynamic_index_in_dim(buffer, slot_index, 0, keepdims=False)
    return lax.dynamic_update_index_in_dim(
        buffer, jnp.where(is_valid, value, current), slot_index, 0
    )


def softmax_parts(scores):
    row_max = jnp.max(scores, axis=-1, keepdims=True)
    shifted = jnp.exp(scores - row_max)
    row_total = jnp.sum(shifted, axis=-1, keepdims=True)
    return ((shifted / row_total).astype(jnp.bfloat16), (row_max + jnp.log(row_total))[..., 0])


def general(
    block_input,
    output_grad,
    seq_lengths,
    attn_gain,
    qkv_proj,
    out_proj,
    ffn_gain,
    up_proj,
    down_proj,
):
    section_index = lax.axis_index("section")
    line_row = lax.axis_index("dp")
    group_index = lax.axis_index("rep")
    strided = section_index == 1
    micro_count, _, tok_rows, model_width = block_input.shape
    line_count = lax.axis_size("dp")
    line_span = tok_rows * line_count
    head_size = model_width // HEADS
    score_scale = float(head_size) ** (-0.5)
    seq_slots = seq_lengths.shape[-1]
    block_count = line_span // STRIDE
    residues = STRIDE // line_count
    line_lengths = lax.dynamic_index_in_dim(seq_lengths, group_index, 1, keepdims=False)
    all_pos = jnp.arange(line_span, dtype=jnp.int32)
    my_pos = line_row * tok_rows + jnp.arange(tok_rows, dtype=jnp.int32)
    win_pos = line_row * tok_rows - tok_rows + jnp.arange(2 * tok_rows, dtype=jnp.int32)
    res_pos = (
        jnp.arange(block_count, dtype=jnp.int32)[None, :] * STRIDE
        + line_row * residues
        + jnp.arange(residues, dtype=jnp.int32)[:, None]
    )
    gain_attn = attn_gain[0].astype(jnp.float32)
    gain_ffn = ffn_gain[0].astype(jnp.float32)
    w_qkv = qkv_proj[0]
    w_out = out_proj[0]
    w_up = up_proj[0]
    w_down = down_proj[0]

    def segments_of(slot_index):
        seq_ends = jnp.cumsum(lax.dynamic_index_in_dim(line_lengths, slot_index, 0, keepdims=False))
        all_seg = jnp.sum((all_pos[:, None] >= seq_ends[None, :]).astype(jnp.int32), axis=1)
        my_seg = lax.dynamic_slice_in_dim(all_seg, line_row * tok_rows, tok_rows)
        padded = jnp.concatenate([jnp.full((tok_rows,), seq_slots, jnp.int32), all_seg])
        win_seg = lax.dynamic_slice_in_dim(padded, line_row * tok_rows, 2 * tok_rows)
        res_seg = lax.dynamic_slice_in_dim(
            all_seg.reshape(block_count, STRIDE), line_row * residues, residues, 1
        ).T
        dense_mask = allowed(
            my_pos[:, None], my_seg[:, None], all_pos[None, :], all_seg[None, :], strided, seq_slots
        )
        win_mask = allowed(
            my_pos[:, None], my_seg[:, None], win_pos[None, :], win_seg[None, :], False, seq_slots
        )
        res_mask = allowed(
            res_pos[:, :, None],
            res_seg[:, :, None],
            res_pos[:, None, :],
            res_seg[:, None, :],
            True,
            seq_slots,
        )
        return (all_seg, my_seg, dense_mask, win_mask, res_mask)

    def project(hidden):
        normed = gained(hidden, gain_attn).astype(jnp.bfloat16)
        packed = product(normed, w_qkv).astype(jnp.bfloat16)
        return (normed, packed)

    def finish(hidden, attended):
        middle = hidden + product(attended, w_out)
        second = gained(middle, gain_ffn).astype(jnp.bfloat16)
        pre_act = product(second, w_up)
        active = jax.nn.gelu(pre_act, approximate=False).astype(jnp.bfloat16)
        return (middle, second, pre_act, active, middle + product(active, w_down))

    def dense_backward(packed, grad_att, lse_now, masks):
        all_seg, my_seg, dense_mask = (masks[0], masks[1], masks[2])
        queries = packed[:, :model_width]
        key_rows = packed[:, model_width : 2 * model_width]
        values = packed[:, 2 * model_width :]
        keys_all, values_all = (
            lax.all_gather(key_rows, "dp", axis=0, tiled=True),
            lax.all_gather(values, "dp", axis=0, tiled=True),
        )
        grad_q_heads = []
        grad_k_heads = []
        grad_v_heads = []
        delta_heads = []
        for head_index in range(HEADS):
            columns = slice(head_index * head_size, (head_index + 1) * head_size)
            query_head = queries[:, columns]
            out_head = grad_att[:, columns]
            scores = jnp.where(
                dense_mask, contract_cols(query_head, keys_all[:, columns]) * score_scale, NEG
            )
            attn_probs = jnp.exp(scores - lse_now[head_index][:, None])
            grad_probs = contract_cols(out_head, values_all[:, columns])
            delta_row = jnp.sum(attn_probs * grad_probs, axis=1)
            grad_scores = (attn_probs * (grad_probs - delta_row[:, None])).astype(jnp.bfloat16)
            grad_q_heads.append(product(grad_scores, keys_all[:, columns]) * score_scale)
            delta_heads.append(delta_row)
            key_part = contract_rows(grad_scores, query_head) * score_scale
            value_part = contract_rows(attn_probs.astype(jnp.bfloat16), out_head)
            key_mine, value_mine = (
                lax.psum_scatter(
                    key_part.astype(jnp.bfloat16), "dp", scatter_dimension=0, tiled=True
                ).astype(jnp.float32),
                lax.psum_scatter(
                    value_part.astype(jnp.bfloat16), "dp", scatter_dimension=0, tiled=True
                ).astype(jnp.float32),
            )
            grad_k_heads.append(key_mine)
            grad_v_heads.append(value_mine)
        return jnp.concatenate(
            [
                jnp.concatenate(grad_q_heads, axis=1).astype(jnp.bfloat16),
                jnp.concatenate(grad_k_heads, axis=1).astype(jnp.bfloat16),
                jnp.concatenate(grad_v_heads, axis=1).astype(jnp.bfloat16),
            ],
            axis=1,
        )

    received = jnp.zeros((tok_rows, model_width), jnp.bfloat16)
    saved_in = jnp.zeros((micro_count, tok_rows, model_width), jnp.bfloat16)
    saved_att = jnp.zeros((micro_count, tok_rows, model_width), jnp.bfloat16)
    saved_lse = jnp.zeros((micro_count, HEADS, tok_rows), jnp.float32)
    results = jnp.zeros((micro_count, tok_rows, model_width), jnp.bfloat16)
    for tick_index in range(micro_count + 1):
        slot_raw = tick_index - section_index
        is_valid = (slot_raw >= 0) & (slot_raw < micro_count)
        slot_index = jnp.clip(slot_raw, 0, micro_count - 1)
        hidden_low = jnp.where(
            section_index == 0, block_input[min(tick_index, micro_count - 1), 0], received
        )
        hidden = hidden_low.astype(jnp.float32)
        normed, packed = project(hidden)
        masks = segments_of(slot_index)
        dense_dense_mask = masks[2]
        dense_keys_all = lax.all_gather(
            packed[:, model_width : 2 * model_width], "dp", axis=0, tiled=True
        )
        dense_values_all = lax.all_gather(packed[:, 2 * model_width :], "dp", axis=0, tiled=True)
        head_outs = []
        head_lse = []
        for dense_head_index in range(HEADS):
            dense_columns = slice(dense_head_index * head_size, (dense_head_index + 1) * head_size)
            dense_scores = jnp.where(
                dense_dense_mask,
                contract_cols(packed[:, dense_columns], dense_keys_all[:, dense_columns])
                * score_scale,
                NEG,
            )
            dense_attn_probs, lse_row = softmax_parts(dense_scores)
            head_outs.append(product(dense_attn_probs, dense_values_all[:, dense_columns]))
            head_lse.append(lse_row)
        attended = jnp.concatenate(head_outs, axis=1).astype(jnp.bfloat16)
        lse_rows = jnp.stack(head_lse)
        output = finish(hidden, attended)[4].astype(jnp.bfloat16)
        saved_in = put_row(saved_in, hidden_low, slot_index, is_valid)
        saved_att = put_row(saved_att, attended, slot_index, is_valid)
        saved_lse = put_row(saved_lse, lse_rows, slot_index, is_valid)
        results = put_row(results, output, slot_index, is_valid)
        if tick_index < micro_count:
            received = from_behind(output, "section", 1)
    totals = (
        jnp.zeros((model_width,), jnp.float32),
        jnp.zeros(w_qkv.shape, jnp.float32),
        jnp.zeros(w_out.shape, jnp.float32),
        jnp.zeros((model_width,), jnp.float32),
        jnp.zeros(w_up.shape, jnp.float32),
        jnp.zeros(w_down.shape, jnp.float32),
    )
    sent_back = jnp.zeros((tok_rows, model_width), jnp.bfloat16)
    input_grads = jnp.zeros((micro_count, tok_rows, model_width), jnp.bfloat16)
    for tick_index in range(micro_count + 1):
        slot_raw = tick_index - (1 - section_index)
        is_valid = (slot_raw >= 0) & (slot_raw < micro_count)
        slot_index = jnp.clip(slot_raw, 0, micro_count - 1)
        grad_out = jnp.where(
            section_index == 1, output_grad[min(tick_index, micro_count - 1), 0], sent_back
        )
        hidden = lax.dynamic_index_in_dim(saved_in, slot_index, 0, keepdims=False).astype(
            jnp.float32
        )
        attended = lax.dynamic_index_in_dim(saved_att, slot_index, 0, keepdims=False)
        lse_now = lax.dynamic_index_in_dim(saved_lse, slot_index, 0, keepdims=False)
        normed, packed = project(hidden)
        middle, second, pre_act, active, _ = finish(hidden, attended)
        grad_down = contract_rows(active, grad_out)
        grad_active = contract_cols(grad_out, w_down)
        gelu_back = jax.vjp(partial(jax.nn.gelu, approximate=False), pre_act)[1]
        grad_pre = gelu_back(grad_active)[0].astype(jnp.bfloat16)
        grad_up = contract_rows(second, grad_pre)
        ffn_back = jax.vjp(gained, middle, gain_ffn)[1]
        grad_mid_norm, grad_gain_ffn = ffn_back(contract_cols(grad_pre, w_up))
        grad_middle = grad_out.astype(jnp.float32) + grad_mid_norm
        grad_branch = grad_middle.astype(jnp.bfloat16)
        grad_outproj = contract_rows(attended, grad_branch)
        grad_att = contract_cols(grad_branch, w_out).astype(jnp.bfloat16)
        masks = segments_of(slot_index)
        grad_packed = dense_backward(packed, grad_att, lse_now, masks)
        grad_qkv = contract_rows(normed, grad_packed)
        attn_back = jax.vjp(gained, hidden, gain_attn)[1]
        grad_hid_norm, grad_gain_attn = attn_back(contract_cols(grad_packed, w_qkv))
        grad_hidden = (grad_middle + grad_hid_norm).astype(jnp.bfloat16)
        terms = (grad_gain_attn, grad_qkv, grad_outproj, grad_gain_ffn, grad_up, grad_down)
        totals = tuple(
            (
                running + jnp.where(is_valid, term_now, 0.0)
                for running, term_now in zip(totals, terms)
            )
        )
        input_grads = put_row(input_grads, grad_hidden, slot_index, is_valid)
        if tick_index < micro_count:
            sent_back = from_behind(grad_hidden, "section", -1)
    summed = lax.psum(
        (totals[0], totals[1], totals[2], totals[3], totals[4], totals[5]), ("dp", "rep")
    )
    return (
        results[None, :, None],
        input_grads[None, :, None],
        summed[0][None],
        summed[1][None],
        summed[2][None],
        summed[3][None],
        summed[4][None],
        summed[5][None],
    )


BF = jnp.bfloat16
F32 = jnp.float32
MIB = 1024 * 1024
GAIN_ROWS = 16


def in_hbm(array):
    return pltpu.with_memory_space_constraint(array, pltpu.HBM)


def call(body, scalars, arrays, shapes, mib=24, micros=1.0, scratch=(), held=0, out_held=(), aliases=None):
    in_specs = [pl.BlockSpec(memory_space=pltpu.SMEM)] * len(scalars)
    in_specs += [pl.BlockSpec(memory_space=pl.ANY)] * held
    in_specs += [pl.BlockSpec(memory_space=pltpu.VMEM)] * (len(arrays) - held)
    return pl.pallas_call(
        body,
        out_shape=tuple(jax.ShapeDtypeStruct(*shape) for shape in shapes),
        in_specs=in_specs,
        out_specs=tuple(
            pl.BlockSpec(memory_space=pl.ANY if index in out_held else pltpu.VMEM)
            for index in range(len(shapes))
        ),
        scratch_shapes=list(scratch),
        input_output_aliases=aliases or {},
        compiler_params=pltpu.CompilerParams(vmem_limit_bytes=mib * MIB),
        cost_estimate=pl.CostEstimate(
            flops=int(micros * 1.1e9), bytes_accessed=int(micros * 3.4e6), transcendentals=0
        ),
    )(
        *scalars,
        *(array if aliases else in_hbm(array) for array in arrays[:held]),
        *arrays[held:],
    )


def my_section():
    return lax.axis_index("section")


def my_line():
    return lax.axis_index("dp")


def my_flip(core):
    rep = lax.axis_index("rep")
    low, high = rep & 1, rep >> 1
    return 2 * low + high if core == 0 else 2 * high + low


def rows_at(start, count):
    return pl.ds(pl.multiple_of(start, count), count)


def segment_at(ends, position):
    total = jnp.zeros(position.shape, jnp.int32)
    for end in ends:
        total = total + (position >= end).astype(jnp.int32)
    return total


def ends_of(lengths):
    ends = []
    so_far = jnp.int32(0)
    for slot in range(lengths.shape[2]):
        so_far = so_far + lengths[my_line(), lax.axis_index("rep"), slot]
        ends.append(so_far)
    return ends


def write_masks(lengths, window_mask, strided_mask):
    section = my_section()
    rows, reach = window_mask.shape
    half = rows // 4
    block = 2 * half
    ends = ends_of(lengths)
    row = lax.broadcasted_iota(jnp.int32, (rows, reach), 0)
    query_pos = block * (row // half) + section * half + (row & (half - 1))
    key_pos = query_pos - (row & (half - 1)) - block
    key_pos = key_pos + lax.broadcasted_iota(jnp.int32, (rows, reach), 1)
    offset = query_pos - key_pos
    segment = segment_at(ends, query_pos)
    same = (segment == segment_at(ends, key_pos)) & (segment < len(ends)) & (key_pos >= 0)
    allow = same & (offset >= 0) & (offset < STRIDE) | (offset == 0)
    window_mask[...] = allow.astype(F32)

    def place(axis):
        index = lax.broadcasted_iota(jnp.int32, (rows, rows), axis)
        return block * (index // half) + section * half + (index & (half - 1))

    query_pos, key_pos = place(0), place(1)
    offset = query_pos - key_pos
    segment = segment_at(ends, query_pos)
    same = (segment == segment_at(ends, key_pos)) & (segment < len(ends))
    allow = same & (offset >= 0) & ((offset & (STRIDE - 1)) == 0) | (offset == 0)
    strided_mask[...] = allow.astype(F32)


def pack_kernel(tokens, grads, gain_attn, gain_ffn, lengths, *rest):
    *pieces, window_mask, strided_mask, gains, lengths_held, sems, side_sems = rest
    block = tokens.shape[2]
    half = block // 2
    rows = rows_at(my_section() * half, half)
    side = [
        pltpu.make_async_copy(lengths, lengths_held, side_sems.at[2]),
        pltpu.make_async_copy(gain_attn, gains.at[0], side_sems.at[0]),
        pltpu.make_async_copy(gain_ffn, gains.at[1], side_sems.at[1]),
    ]
    copies = []
    for step, piece in enumerate(pieces):
        micro = my_line() ^ step
        for part, source in enumerate((tokens, grads)):
            copies.append(
                pltpu.make_async_copy(
                    source.at[micro, 0, rows],
                    piece.at[part * half : (part + 1) * half],
                    sems.at[2 * step + part],
                )
            )
    for copy in (*side, *copies):
        copy.start()
    for copy in side:
        copy.wait()
    write_masks(lengths_held, window_mask, strided_mask)
    pieces[0][block:, :] = jnp.concatenate(
        [
            gains[0].astype(F32),
            gains[1].astype(F32),
            jnp.zeros((pieces[0].shape[0] - block - 2, gains.shape[2]), F32),
        ],
        axis=0,
    ).astype(BF)
    for copy in copies:
        copy.wait()


def unit(values):
    centered = values - jnp.mean(values, axis=-1, keepdims=True)
    inverse = lax.rsqrt(jnp.mean(centered * centered, axis=-1, keepdims=True) + 1e-05)
    return centered * inverse, inverse


def unit_back(grad, normal, inverse):
    return inverse * (
        grad
        - jnp.mean(grad, axis=-1, keepdims=True)
        - normal * jnp.mean(grad * normal, axis=-1, keepdims=True)
    )


def widened(column, width):
    return jnp.broadcast_to(column, (column.shape[0], width))


def normalized_exp(scores):
    shifted = jnp.exp(scores - jnp.max(scores, axis=-1, keepdims=True))
    return shifted * (1.0 / jnp.sum(shifted, axis=-1, keepdims=True))


def ffn_forward(hidden, attended, gain, w_out, w_up, w_down, saved):
    result, middle_unit, middle_inverse, second_ref, active, slope = saved
    middle = hidden + product(attended, w_out)
    normal, inverse = unit(middle)
    middle_unit[...] = normal
    middle_inverse[...] = widened(inverse, middle_inverse.shape[1])
    second = (normal * gain).astype(BF)
    second_ref[...] = second
    chunk = middle.shape[1]
    total = middle
    for index in range(w_up.shape[1] // chunk):
        columns = slice(index * chunk, (index + 1) * chunk)
        pre_act = product(second, w_up[:, columns])
        below = 0.5 + 0.5 * lax.erf(pre_act * (0.5**0.5))
        now = (pre_act * below).astype(BF)
        active[:, columns] = now
        slope[:, columns] = below + pre_act * (
            jnp.exp(-0.5 * pre_act * pre_act) * 0.3989422804014327
        )
        total = total + product(now, w_down[columns, :])
    result[...] = total.astype(BF)


def own_unit(spot, half):
    return slice((2 * spot + 2) * half, (2 * spot + 3) * half)


def key_units(spot, half):
    return slice(2 * spot * half, (2 * spot + 3) * half)


def zero_forward_kernel(
    mask,
    own0,
    own1,
    own2,
    own3,
    far0,
    far1,
    far2,
    far3,
    w_qkv,
    w_out,
    w_up,
    w_down,
    gains,
    line,
    normal_all,
    inverse_all,
    normed_all,
    query,
    padded,
    probs_ref,
    attended_ref,
    cotangent,
    *saved,
):
    section = my_section()
    reached, width = normal_all.shape
    half = line.shape[0] // 10
    block = 2 * half
    blocks = 4
    rows = blocks * half
    head = width // HEADS
    scale = float(head) ** (-0.5)
    reach = block + half
    line[:block, :] = jnp.zeros((block, width), BF)
    for step, (near, far) in enumerate(((own0, far0), (own1, far1), (own2, far2), (own3, far3))):
        spot = my_line() ^ step
        line[rows_at(spot * block + block, half), :] = near[:half, :]
        line[rows_at(spot * block + block + half - section * block, half), :] = far[:half, :]
        cotangent[rows_at(spot * half, half), :] = near[half:block, :]
    normal, inverse = unit(line[:reached, :].astype(F32))
    normal_all[...] = normal
    inverse_all[...] = widened(inverse, inverse_all.shape[1])
    normed = (normal * gains[0, 0:1, :]).astype(BF)
    normed_all[...] = normed
    padded[...] = product(normed, w_qkv[0, :, width:]).astype(BF)
    normed_mine = jnp.concatenate(
        [normed[own_unit(spot, half), :] for spot in range(blocks)], axis=0
    )
    query[...] = product(normed_mine, w_qkv[0, :, :width]).astype(BF)
    spots = [(slice(spot * half, (spot + 1) * half), key_units(spot, half)) for spot in range(blocks)]
    heads = [
        (slice(number * head, (number + 1) * head), slice(width + number * head, width + (number + 1) * head))
        for number in range(HEADS)
    ]
    scores = [
        jnp.concatenate(
            [contract_cols(query[here, columns], padded[window, columns]) for here, window in spots],
            axis=0,
        )
        for columns, _ in heads
    ]
    probs = [normalized_exp(jnp.where(mask[...] > 0.5, values * scale, NEG)) for values in scores]
    attended = []
    for number, (_, value_columns) in enumerate(heads):
        probs_ref[number] = probs[number]
        low = probs[number].astype(BF)
        attended.append(
            jnp.concatenate(
                [product(low[here, :], padded[window, value_columns]) for here, window in spots], axis=0
            )
        )
    attended = jnp.concatenate(attended, axis=1).astype(BF)
    attended_ref[...] = attended
    hidden = jnp.concatenate([line[own_unit(spot, half), :] for spot in range(blocks)], axis=0)
    ffn_forward(
        hidden.astype(F32), attended, gains[0, 1:2, :], w_out[0], w_up.at[0], w_down.at[0], saved
    )


def one_forward_kernel(
    mask,
    hidden_ref,
    w_qkv,
    w_out,
    w_up,
    w_down,
    gains,
    normal_ref,
    inverse_ref,
    normed_ref,
    packed,
    probs_ref,
    attended_ref,
    *saved,
):
    section = my_section()
    rows, width = hidden_ref.shape
    half = rows // 4
    block = 2 * half
    head = width // HEADS
    scale = float(head) ** (-0.5)
    hidden = hidden_ref[...].astype(F32)
    normal, inverse = unit(hidden)
    normal_ref[...] = normal
    inverse_ref[...] = widened(inverse, inverse_ref.shape[1])
    normed = (normal * gains[1, 0:1, :]).astype(BF)
    normed_ref[...] = normed
    packed[...] = product(normed, w_qkv[1]).astype(BF)
    heads = [
        tuple(
            slice(part * width + number * head, part * width + (number + 1) * head) for part in range(3)
        )
        for number in range(HEADS)
    ]
    scores = [contract_cols(packed[:, near], packed[:, far]) for near, far, _ in heads]
    probs = [normalized_exp(jnp.where(mask[...] > 0.5, values * scale, NEG)) for values in scores]
    parts = []
    for number, (_, _, value_columns) in enumerate(heads):
        probs_ref[number] = probs[number]
        parts.append(product(probs[number].astype(BF), packed[:, value_columns]))
    attended = jnp.concatenate(parts, axis=1).astype(BF)
    attended_ref[...] = attended
    ffn_forward(hidden, attended, gains[1, 1:2, :], w_out[1], w_up.at[1], w_down.at[1], saved)


def store_block(terms, number, value):
    width = value.shape[1]
    unit_rows = width // 2
    core, number = divmod(number, 6)
    side, flip = my_section() ^ core, my_flip(core)
    value = value.astype(BF)
    for part in range(2):
        quarter, place = divmod(2 * number + part, 3)
        terms[side, flip ^ quarter, place * unit_rows : (place + 1) * unit_rows, :] = value[
            part * unit_rows : (part + 1) * unit_rows, :
        ]


def store_gains(terms, attn_term, ffn_term):
    spare, width = terms.shape[2] - GAIN_ROWS, terms.shape[3]
    value = jnp.concatenate(
        [attn_term, ffn_term, jnp.zeros((GAIN_ROWS - 2, width), F32)], axis=0
    ).astype(BF)
    for side in range(2):
        for quarter in range(4):
            terms[side, quarter, spare:, :] = value


def ffn_input_grad(grad_out, saved, gain, w_out, w_up, w_down, grad_pre_ref):
    middle_unit, middle_inverse, slope = saved
    width = grad_out.shape[1]
    grad_second = None
    for index in range(w_up.shape[1] // width):
        columns = slice(index * width, (index + 1) * width)
        grad_active = contract_cols(grad_out, w_down[columns, :])
        grad_pre = (grad_active * slope[:, columns]).astype(BF)
        grad_pre_ref[:, columns] = grad_pre
        term = contract_cols(grad_pre, w_up[:, columns])
        grad_second = term if grad_second is None else grad_second + term
    normal = middle_unit[...]
    gain_term = jnp.sum(grad_second * normal, axis=0, keepdims=True)
    grad_middle = grad_out.astype(F32) + unit_back(
        grad_second * gain, normal, middle_inverse[:, 0:1]
    )
    return grad_middle, contract_cols(grad_middle.astype(BF), w_out).astype(BF), gain_term


def ffn_weight_grads(terms, grad_out, grad_middle, second, active, attended, grad_pre):
    width = grad_out.shape[1]
    store_block(terms, 3, contract_rows(attended[...], grad_middle.astype(BF)))
    for index in range(active.shape[1] // width):
        columns = slice(index * width, (index + 1) * width)
        store_block(terms, 4 + index, contract_rows(second[...], grad_pre[:, columns]))
        store_block(terms, 8 + index, contract_rows(active[:, columns], grad_out))


def one_backward_kernel(
    grad_ref,
    w_qkv,
    w_out,
    w_up,
    w_down,
    gains,
    normal_ref,
    inverse_ref,
    normed_ref,
    packed,
    probs_ref,
    *rest,
):
    middle_unit, middle_inverse, second, active, slope, attended, grad_in, terms, grad_pre = rest
    width = grad_ref.shape[1]
    head = width // HEADS
    scale = float(head) ** (-0.5)
    grad_out = grad_ref[...]
    grad_middle, grad_att, ffn_term = ffn_input_grad(
        grad_out,
        (middle_unit, middle_inverse, slope),
        gains[1, 1:2, :],
        w_out[1],
        w_up.at[1],
        w_down.at[1],
        grad_pre,
    )
    ffn_weight_grads(terms, grad_out, grad_middle, second, active, attended, grad_pre)
    heads = [
        tuple(
            slice(part * width + number * head, part * width + (number + 1) * head) for part in range(3)
        )
        for number in range(HEADS)
    ]
    probs = [probs_ref[number] for number in range(HEADS)]
    grad_probs = [
        contract_cols(grad_att[:, near], packed[:, value_columns]) for near, _, value_columns in heads
    ]
    grad_scores = [
        (prob * (grad - jnp.sum(prob * grad, axis=-1, keepdims=True))).astype(BF)
        for prob, grad in zip(probs, grad_probs)
    ]
    grad_parts = [
        [product(grad, packed[:, far]) * scale for grad, (_, far, _) in zip(grad_scores, heads)],
        [contract_rows(grad, packed[:, near]) * scale for grad, (near, _, _) in zip(grad_scores, heads)],
        [contract_rows(prob.astype(BF), grad_att[:, near]) for prob, (near, _, _) in zip(probs, heads)],
    ]
    grad_normed = None
    for index in range(3):
        columns = slice(index * width, (index + 1) * width)
        grad_block = jnp.concatenate(grad_parts[index], axis=1).astype(BF)
        term = contract_cols(grad_block, w_qkv[1, :, columns])
        grad_normed = term if grad_normed is None else grad_normed + term
        store_block(terms, index, contract_rows(normed_ref[...], grad_block))
    normal = normal_ref[...]
    store_gains(terms, jnp.sum(grad_normed * normal, axis=0, keepdims=True), ffn_term)
    grad_in[...] = (
        grad_middle + unit_back(grad_normed * gains[1, 0:1, :], normal, inverse_ref[:, 0:1])
    ).astype(BF)


def zero_ffn_kernel(
    grad_ref,
    w_out,
    w_up,
    w_down,
    gains,
    middle_unit,
    middle_inverse,
    slope,
    grad_middle_ref,
    grad_att_ref,
    grad_pre,
    gain_term,
):
    grad_middle, grad_att, term = ffn_input_grad(
        grad_ref[...],
        (middle_unit, middle_inverse, slope),
        gains[0, 1:2, :],
        w_out[0],
        w_up.at[0],
        w_down.at[0],
        grad_pre,
    )
    grad_middle_ref[...] = grad_middle
    grad_att_ref[...] = grad_att
    gain_term[...] = term


def zero_backward_kernel(
    grad_ref,
    w_qkv,
    gains,
    normal_all,
    inverse_all,
    normed_all,
    query,
    padded,
    probs_ref,
    result_zero,
    result_one,
    second,
    active,
    attended,
    grad_middle_ref,
    grad_att_ref,
    grad_pre,
    ffn_term,
    result_keep,
    grad_line,
    swap,
    terms,
):
    section = my_section()
    rows, width = grad_ref.shape
    reached = normal_all.shape[0]
    half = rows // 4
    blocks = 4
    head = width // HEADS
    scale = float(head) ** (-0.5)
    grad_out = grad_ref[...]

    @pl.when(section == 0)
    def _():
        result_keep[...] = result_zero[...]
        swap[:rows, :] = result_one[...]

    @pl.when(section == 1)
    def _():
        result_keep[...] = result_one[...]
        swap[:rows, :] = result_zero[...]

    grad_middle = grad_middle_ref[...]
    grad_att = grad_att_ref[...]
    ffn_weight_grads(terms, grad_out, grad_middle, second, active, attended, grad_pre)
    spots = [(slice(spot * half, (spot + 1) * half), key_units(spot, half)) for spot in range(blocks)]
    heads = [
        (slice(number * head, (number + 1) * head), slice(width + number * head, width + (number + 1) * head))
        for number in range(HEADS)
    ]
    probs = [probs_ref[number] for number in range(HEADS)]
    grad_probs = [
        jnp.concatenate(
            [
                contract_cols(grad_att[here, columns], padded[window, value_columns])
                for here, window in spots
            ],
            axis=0,
        )
        for columns, value_columns in heads
    ]
    grad_scores = [
        (prob * (grad - jnp.sum(prob * grad, axis=-1, keepdims=True))).astype(BF)
        for prob, grad in zip(probs, grad_probs)
    ]
    grad_query = [
        jnp.concatenate(
            [product(grad[here, :], padded[window, columns]) for here, window in spots], axis=0
        )
        * scale
        for grad, (columns, _) in zip(grad_scores, heads)
    ]
    grad_query = jnp.concatenate(grad_query, axis=1).astype(BF)

    def gathered(lefts, right):
        parts = []
        for left, (columns, _) in zip(lefts, heads):
            terms_of = [contract_rows(left[here, :], right[here, columns]) for here, _ in spots]
            units = []
            for index in range(reached // half):
                spot, place = divmod(index, 2)
                held = None
                if spot < blocks:
                    held = terms_of[spot][place * half : (place + 1) * half, :]
                if place == 0 and spot > 0:
                    last = terms_of[spot - 1][2 * half :, :]
                    held = last if held is None else held + last
                units.append(held)
            parts.append(jnp.concatenate(units, axis=0))
        return jnp.concatenate(parts, axis=1)

    grad_keys = (gathered(grad_scores, query) * scale).astype(BF)
    grad_values = gathered([prob.astype(BF) for prob in probs], grad_att).astype(BF)
    normed = normed_all[...]
    normed_mine = jnp.concatenate(
        [normed[own_unit(spot, half), :] for spot in range(blocks)], axis=0
    )
    store_block(terms, 0, contract_rows(normed_mine, grad_query))
    store_block(terms, 1, contract_rows(normed, grad_keys))
    store_block(terms, 2, contract_rows(normed, grad_values))
    from_query = contract_cols(grad_query, w_qkv[0, :, :width])
    grad_line[:reached, :] = contract_cols(
        grad_keys, w_qkv[0, :, width : 2 * width]
    ) + contract_cols(grad_values, w_qkv[0, :, 2 * width :])
    for spot in range(blocks):
        grad_line[own_unit(spot, half), :] += from_query[spot * half : (spot + 1) * half, :]
    grad_normed = grad_line[:reached, :]
    normal = normal_all[...]
    store_gains(terms, jnp.sum(grad_normed * normal, axis=0, keepdims=True), ffn_term[...])
    grad_line[:reached, :] = unit_back(grad_normed * gains[0, 0:1, :], normal, inverse_all[:, 0:1])
    for spot in range(blocks):
        grad_line[own_unit(spot, half), :] += grad_middle[spot * half : (spot + 1) * half, :]
    grad_line[reached:, :] = jnp.zeros((grad_line.shape[0] - reached, width), F32)

    @pl.when(section == 0)
    def _():
        swap[rows : 2 * rows, :] = grad_out

    @pl.when(section == 1)
    def _():
        swap[rows:, :] = grad_line[:reached, :].astype(BF)


def share_kernel(keep, one_near, zero_near, came, *pieces):
    rows = keep.shape[0]
    half = rows // 4
    block = 2 * half
    section = my_section()
    near_rows = rows_at(section * half, half)
    far_rows = rows_at(half - section * half, half)
    for step, piece in enumerate(pieces):
        spot = my_line() ^ step
        mine = rows_at(spot * half, half)
        piece[near_rows, :] = keep[mine, :]
        piece[far_rows, :] = came[mine, :]

    @pl.when(section == 0)
    def _():
        for step, piece in enumerate(pieces):
            base = (my_line() ^ step) * block
            near, far = rows_at(base + block, block), rows_at(rows + base + half, half)
            far = pl.ds(far.start, block)
            piece[block:, :] = (zero_near[near, :] + came[far, :].astype(F32)).astype(BF)

    @pl.when(section == 1)
    def _():
        for step, piece in enumerate(pieces):
            spot = my_line() ^ step
            piece[block : block + half, :] = came[rows_at(rows + spot * half, half), :]
            piece[block + half :, :] = one_near[rows_at(spot * half, half), :]


def settle_kernel(piece0, piece1, piece2, piece3, results, input_grads):
    block = piece0.shape[0] // 2
    for step, piece in enumerate((piece0, piece1, piece2, piece3)):
        micro = my_line() ^ step
        results[0, micro, 0] = piece[:block, :]
        input_grads[0, micro, 0] = piece[block:, :]


def write_half(core, terms, targets, held, sems):
    width = terms.shape[2]
    unit_rows = width // 2
    copies = []
    for place in range(6):
        number = 6 * core + place
        for part in range(2):
            quarter, spot = divmod(2 * place + part, 3)
            value = terms[my_flip(core) ^ quarter, spot * unit_rows : (spot + 1) * unit_rows, :]
            held[place, part * unit_rows : (part + 1) * unit_rows, :] = value.astype(F32)
        which = 0 if number < 3 else 1 if number == 3 else 2 if number < 8 else 3
        first = (number, 0, number - 4, number - 8)[which] * width
        rows = pl.ds(first if which == 3 else 0, width)
        columns = pl.ds(0 if which in (1, 3) else first, width)
        copies.append(
            pltpu.make_async_copy(
                held.at[place], targets[which].at[0, rows, columns], sems.at[place]
            )
        )
        copies[-1].start()
    for copy in copies:
        copy.wait()


def by_section(body):
    for core in range(2):
        pl.when(my_section() == core)(partial(body, core))


def near_kernel(zero, one, gain_attn, qkv, out, gain_ffn, up, down, held, sems):
    spare = zero.shape[1] - GAIN_ROWS

    def body(core):
        terms = (zero, one)[core]
        gains = terms[0, spare:, :].astype(F32)
        gain_attn[...] = gains[0:1, :]
        gain_ffn[...] = gains[1:2, :]
        write_half(core, terms, (qkv, out, up, down), held, sems)

    by_section(body)


def far_kernel(qkv_in, out_in, up_in, down_in, zero, one, qkv, out, up, down, held, sems):
    by_section(
        lambda core: write_half(1 - core, (zero, one)[core], (qkv, out, up, down), held, sems)
    )


SWAP = [(0, 1), (1, 0)]
PLANE = ("section", "rep")


def crossed(flips):
    return [(4 * s + g, 4 * s + (g ^ flips[s])) for s in range(2) for g in range(4)]


FIRST = crossed((1, 2))
SECOND = crossed((2, 1))


def along_line(value, step):
    return lax.ppermute(value, "dp", [(z, z ^ step) for z in range(4)])


def reduce_terms(terms, came, zed, home, before, between=None):
    bar = lax.optimization_barrier
    first = lax.ppermute(terms[0, 2:4] + came[2:4], PLANE, FIRST)
    second = lax.ppermute(terms[0, 1] + came[1] + first[1], PLANE, SECOND)
    total = bar(terms[0, 0] + came[0] + first[0] + second)
    total, home[before] = bar((total, home[before]))
    total = bar(total + along_line(total, 1))
    if between is not None:
        total, home[between] = bar((total, home[between]))
    half = total.shape[0] // 2
    odd = zed & 1
    mine = lax.dynamic_slice_in_dim(total, odd * half, half, 0)
    mine = bar(mine + along_line(mine, 2))
    other = along_line(mine, 1)
    total = bar(
        jnp.where(
            odd == 0, jnp.concatenate([mine, other]), jnp.concatenate([other, mine])
        )
    )
    pair = jnp.stack([total, lax.ppermute(total, PLANE, SECOND)])
    return pair, lax.ppermute(pair, PLANE, FIRST)


def lines(
    block_input,
    output_grad,
    seq_lengths,
    attn_gain,
    qkv_proj,
    out_proj,
    ffn_gain,
    up_proj,
    down_proj,
):
    section = lax.axis_index("section")
    zed = lax.axis_index("dp")
    micro_count, _, block, width = block_input.shape
    hidden_units = up_proj.shape[2]
    half = block // 2
    rows, reach = micro_count * half, block + half
    reached = rows + rows + half
    term_rows = 6 * width // 4 + GAIN_ROWS

    *packed, window_mask, strided_mask = call(
        pack_kernel,
        (),
        (block_input, output_grad, attn_gain, ffn_gain, seq_lengths),
        (
            ((block + 16, width), BF),
            *((((block, width), BF),) * (micro_count - 1)),
            ((rows, reach), F32),
            ((rows, rows), F32),
        ),
        8,
        scratch=(
            pltpu.VMEM((2, 1, width), BF),
            pltpu.SMEM(seq_lengths.shape, jnp.int32),
            pltpu.SemaphoreType.DMA((2 * micro_count,)),
            pltpu.SemaphoreType.DMA((3,)),
        ),
        held=5,
    )
    near = [packed[0]] + [along_line(packed[step], step) for step in range(1, micro_count)]
    far = [lax.ppermute(piece, "section", SWAP) for piece in near]
    own = (qkv_proj[0], out_proj[0], up_proj[0], down_proj[0])
    near[1], *own = lax.optimization_barrier((near[1], *own))
    swapped = [lax.ppermute(weight, "section", SWAP) for weight in own]
    weights = tuple(
        jnp.stack([jnp.where(section == 0, a, b), jnp.where(section == 0, b, a)])
        for a, b in zip(own, swapped)
    )
    gains_near, gains_far = near[0][block:].astype(F32), far[0][block:].astype(F32)
    weights += (
        jnp.stack(
            [
                jnp.where(section == 0, gains_near, gains_far),
                jnp.where(section == 0, gains_far, gains_near),
            ]
        ),
    )
    ffn_saved = (
        ((rows, width), BF),
        ((rows, width), F32),
        ((rows, 128), F32),
        ((rows, width), BF),
        ((rows, hidden_units), BF),
        ((rows, hidden_units), F32),
    )
    (
        _,
        normal_all,
        inverse_all,
        normed_all,
        query,
        padded,
        probs_zero,
        attended_zero,
        cotangent,
        result_zero,
        *saved_zero,
    ) = call(
        zero_forward_kernel,
        (),
        (window_mask, *near, *far, *weights),
        (
            ((reached + half, width), BF),
            ((reached, width), F32),
            ((reached, 128), F32),
            ((reached, width), BF),
            ((rows, width), BF),
            ((reached, 2 * width), BF),
            ((HEADS, rows, reach), F32),
            ((rows, width), BF),
            ((rows, width), BF),
            *ffn_saved,
        ),
    )
    (
        normal_one,
        inverse_one,
        normed_one,
        packed_one,
        probs_one,
        attended_one,
        result_one,
        *saved_one,
    ) = call(
        one_forward_kernel,
        (),
        (strided_mask, result_zero, *weights),
        (
            ((rows, width), F32),
            ((rows, 128), F32),
            ((rows, width), BF),
            ((rows, 3 * width), BF),
            ((HEADS, rows, rows), F32),
            ((rows, width), BF),
            *ffn_saved,
        ),
    )
    middle_one, mid_inverse_one, second_one, active_one, slope_one = saved_one
    grad_one, terms_one, _ = call(
        one_backward_kernel,
        (),
        (
            cotangent,
            *weights,
            normal_one,
            inverse_one,
            normed_one,
            packed_one,
            probs_one,
            middle_one,
            mid_inverse_one,
            second_one,
            active_one,
            slope_one,
            attended_one,
        ),
        (((rows, width), BF), ((2, 4, term_rows, width), BF), ((rows, hidden_units), BF)),
        micros=3.0,
    )
    middle_zero, mid_inverse_zero, second_zero, active_zero, slope_zero = saved_zero
    came_one = lax.ppermute(terms_one[1], "section", SWAP)
    w_qkv, w_out, w_up, w_down, gains = weights
    zero_ffn = call(
        zero_ffn_kernel,
        (),
        (grad_one, w_out, w_up, w_down, gains, middle_zero, mid_inverse_zero, slope_zero),
        (
            ((rows, width), F32),
            ((rows, width), BF),
            ((rows, hidden_units), BF),
            ((1, width), F32),
        ),
        micros=2.0,
    )
    result_keep, grad_line, swap, terms_zero = call(
        zero_backward_kernel,
        (),
        (
            grad_one,
            w_qkv,
            gains,
            normal_all,
            inverse_all,
            normed_all,
            query,
            padded,
            probs_zero,
            result_zero,
            result_one,
            second_zero,
            active_zero,
            attended_zero,
            *zero_ffn,
        ),
        (
            ((rows, width), BF),
            ((reached + half, width), F32),
            ((rows + reached, width), BF),
            ((2, 4, term_rows, width), BF),
        ),
        micros=4.0,
    )
    came = lax.ppermute(swap, "section", SWAP)
    shared = call(
        share_kernel,
        (),
        (result_keep, grad_one, grad_line, came),
        (((2 * block, width), BF),) * micro_count,
        8,
    )
    home = [shared[0]] + [along_line(shared[step], step) for step in range(1, micro_count)]
    came_zero = lax.ppermute(terms_zero[1], "section", SWAP)
    one_pair, one_first = reduce_terms(terms_one, came_one, zed, home, 1, 3)
    zero_pair, zero_first = reduce_terms(terms_zero, came_zero, zed, home, 2)
    results, input_grads = call(
        settle_kernel,
        (),
        home,
        (((1, micro_count, 1, block, width), BF),) * 2,
        8,
    )

    def both_cores(parts):
        near = jnp.concatenate(parts)
        return near, jnp.concatenate([lax.ppermute(part, "section", SWAP) for part in parts])

    zero_near, zero_far = both_cores((zero_pair, zero_first))
    one_near, one_far = both_cores((one_pair, one_first))
    sums = (
        ((1, width, 3 * width), F32),
        ((1, width, width), F32),
        ((1, width, hidden_units), F32),
        ((1, hidden_units, width), F32),
    )
    held = (pltpu.VMEM((6, width, width), F32), pltpu.SemaphoreType.DMA((6,)))
    gain_attn_sum, qkv_half, out_half, gain_ffn_sum, up_half, down_half = call(
        near_kernel,
        (),
        (zero_near, one_near),
        (((1, width), F32), *sums[:2], ((1, width), F32), *sums[2:]),
        16,
        scratch=held,
        out_held=(1, 2, 4, 5),
    )
    qkv_sum, out_sum, up_sum, down_sum = call(
        far_kernel,
        (),
        (qkv_half, out_half, up_half, down_half, zero_far, one_far),
        sums,
        16,
        scratch=held,
        held=4,
        out_held=(0, 1, 2, 3),
        aliases={0: 0, 1: 1, 2: 2, 3: 3},
    )
    return (
        results,
        input_grads,
        gain_attn_sum,
        qkv_sum,
        out_sum,
        gain_ffn_sum,
        up_sum,
        down_sum,
    )


def local(*arrays):
    micro_count, _, tok_rows, model_width = arrays[0].shape
    one_line_per_chip = (
        lax.axis_size("section") == 2
        and lax.axis_size("dp") == 4
        and lax.axis_size("rep") == 4
        and micro_count == 4
        and tok_rows == STRIDE
        and model_width == 256
        and arrays[7].shape[2] == 4 * model_width
    )
    return lines(*arrays) if one_line_per_chip else general(*arrays)


def solution(mesh):
    placed = (
        P(None, "rep", "dp", None),
        P(None, "rep", "dp", None),
        P(),
        P("section", None),
        P("section", None, None),
        P("section", None, None),
        P("section", None),
        P("section", None, None),
        P("section", None, None),
    )
    return jax.shard_map(
        local,
        mesh=mesh,
        in_specs=placed,
        out_specs=(
            P("section", None, "rep", "dp", None),
            P("section", None, "rep", "dp", None),
            P("section", None),
            P("section", None, None),
            P("section", None, None),
            P("section", None),
            P("section", None, None),
            P("section", None, None),
        ),
        check_vma=False,
    )
```

```python
from functools import partial

import jax
import jax.numpy as jnp
from jax import lax
from jax.experimental import pallas as pl
from jax.experimental.pallas import tpu as pltpu
from jax.sharding import PartitionSpec as P

HEADS = 2
STRIDE = 128


NEG = -1e30


def from_behind(shard, axis, by):
    length = lax.axis_size(axis)
    pairs = [(i, i + by) for i in range(length) if 0 <= i + by < length]
    return lax.ppermute(shard, axis, pairs)


def normalize(values):
    centered = values - jnp.mean(values, axis=-1, keepdims=True)
    spread = jnp.mean(centered * centered, axis=-1, keepdims=True)
    return centered * lax.rsqrt(spread + 1e-05)


def gained(values, gain):
    return normalize(values) * gain


def allowed(query_pos, query_seg, key_pos, key_seg, strided, seq_slots):
    offset = query_pos - key_pos
    same_seq = (query_seg == key_seg) & (query_seg < seq_slots)
    nearby = (offset >= 0) & (offset < STRIDE)
    spaced = (offset >= 0) & (offset % STRIDE == 0)
    pattern = jnp.where(strided, spaced, nearby)
    return same_seq & pattern | (offset == 0)


def product(left, right):
    return jnp.dot(left, right, preferred_element_type=jnp.float32)


def contract_rows(left, right):
    return lax.dot_general(
        left, right, (((0,), (0,)), ((), ())), preferred_element_type=jnp.float32
    )


def contract_cols(left, right):
    return lax.dot_general(
        left, right, (((1,), (1,)), ((), ())), preferred_element_type=jnp.float32
    )


def put_row(buffer, value, slot_index, is_valid):
    current = lax.dynamic_index_in_dim(buffer, slot_index, 0, keepdims=False)
    return lax.dynamic_update_index_in_dim(
        buffer, jnp.where(is_valid, value, current), slot_index, 0
    )


def softmax_parts(scores):
    row_max = jnp.max(scores, axis=-1, keepdims=True)
    shifted = jnp.exp(scores - row_max)
    row_total = jnp.sum(shifted, axis=-1, keepdims=True)
    return ((shifted / row_total).astype(jnp.bfloat16), (row_max + jnp.log(row_total))[..., 0])


def general(
    block_input,
    output_grad,
    seq_lengths,
    attn_gain,
    qkv_proj,
    out_proj,
    ffn_gain,
    up_proj,
    down_proj,
):
    section_index = lax.axis_index("section")
    line_row = lax.axis_index("dp")
    group_index = lax.axis_index("rep")
    strided = section_index == 1
    micro_count, _, tok_rows, model_width = block_input.shape
    line_count = lax.axis_size("dp")
    line_span = tok_rows * line_count
    head_size = model_width // HEADS
    score_scale = float(head_size) ** (-0.5)
    seq_slots = seq_lengths.shape[-1]
    block_count = line_span // STRIDE
    residues = STRIDE // line_count
    line_lengths = lax.dynamic_index_in_dim(seq_lengths, group_index, 1, keepdims=False)
    all_pos = jnp.arange(line_span, dtype=jnp.int32)
    my_pos = line_row * tok_rows + jnp.arange(tok_rows, dtype=jnp.int32)
    win_pos = line_row * tok_rows - tok_rows + jnp.arange(2 * tok_rows, dtype=jnp.int32)
    res_pos = (
        jnp.arange(block_count, dtype=jnp.int32)[None, :] * STRIDE
        + line_row * residues
        + jnp.arange(residues, dtype=jnp.int32)[:, None]
    )
    gain_attn = attn_gain[0].astype(jnp.float32)
    gain_ffn = ffn_gain[0].astype(jnp.float32)
    w_qkv = qkv_proj[0]
    w_out = out_proj[0]
    w_up = up_proj[0]
    w_down = down_proj[0]

    def segments_of(slot_index):
        seq_ends = jnp.cumsum(lax.dynamic_index_in_dim(line_lengths, slot_index, 0, keepdims=False))
        all_seg = jnp.sum((all_pos[:, None] >= seq_ends[None, :]).astype(jnp.int32), axis=1)
        my_seg = lax.dynamic_slice_in_dim(all_seg, line_row * tok_rows, tok_rows)
        padded = jnp.concatenate([jnp.full((tok_rows,), seq_slots, jnp.int32), all_seg])
        win_seg = lax.dynamic_slice_in_dim(padded, line_row * tok_rows, 2 * tok_rows)
        res_seg = lax.dynamic_slice_in_dim(
            all_seg.reshape(block_count, STRIDE), line_row * residues, residues, 1
        ).T
        dense_mask = allowed(
            my_pos[:, None], my_seg[:, None], all_pos[None, :], all_seg[None, :], strided, seq_slots
        )
        win_mask = allowed(
            my_pos[:, None], my_seg[:, None], win_pos[None, :], win_seg[None, :], False, seq_slots
        )
        res_mask = allowed(
            res_pos[:, :, None],
            res_seg[:, :, None],
            res_pos[:, None, :],
            res_seg[:, None, :],
            True,
            seq_slots,
        )
        return (all_seg, my_seg, dense_mask, win_mask, res_mask)

    def project(hidden):
        normed = gained(hidden, gain_attn).astype(jnp.bfloat16)
        packed = product(normed, w_qkv).astype(jnp.bfloat16)
        return (normed, packed)

    def finish(hidden, attended):
        middle = hidden + product(attended, w_out)
        second = gained(middle, gain_ffn).astype(jnp.bfloat16)
        pre_act = product(second, w_up)
        active = jax.nn.gelu(pre_act, approximate=False).astype(jnp.bfloat16)
        return (middle, second, pre_act, active, middle + product(active, w_down))

    def dense_backward(packed, grad_att, lse_now, masks):
        all_seg, my_seg, dense_mask = (masks[0], masks[1], masks[2])
        queries = packed[:, :model_width]
        key_rows = packed[:, model_width : 2 * model_width]
        values = packed[:, 2 * model_width :]
        keys_all, values_all = (
            lax.all_gather(key_rows, "dp", axis=0, tiled=True),
            lax.all_gather(values, "dp", axis=0, tiled=True),
        )
        grad_q_heads = []
        grad_k_heads = []
        grad_v_heads = []
        delta_heads = []
        for head_index in range(HEADS):
            columns = slice(head_index * head_size, (head_index + 1) * head_size)
            query_head = queries[:, columns]
            out_head = grad_att[:, columns]
            scores = jnp.where(
                dense_mask, contract_cols(query_head, keys_all[:, columns]) * score_scale, NEG
            )
            attn_probs = jnp.exp(scores - lse_now[head_index][:, None])
            grad_probs = contract_cols(out_head, values_all[:, columns])
            delta_row = jnp.sum(attn_probs * grad_probs, axis=1)
            grad_scores = (attn_probs * (grad_probs - delta_row[:, None])).astype(jnp.bfloat16)
            grad_q_heads.append(product(grad_scores, keys_all[:, columns]) * score_scale)
            delta_heads.append(delta_row)
            key_part = contract_rows(grad_scores, query_head) * score_scale
            value_part = contract_rows(attn_probs.astype(jnp.bfloat16), out_head)
            key_mine, value_mine = (
                lax.psum_scatter(
                    key_part.astype(jnp.bfloat16), "dp", scatter_dimension=0, tiled=True
                ).astype(jnp.float32),
                lax.psum_scatter(
                    value_part.astype(jnp.bfloat16), "dp", scatter_dimension=0, tiled=True
                ).astype(jnp.float32),
            )
            grad_k_heads.append(key_mine)
            grad_v_heads.append(value_mine)
        return jnp.concatenate(
            [
                jnp.concatenate(grad_q_heads, axis=1).astype(jnp.bfloat16),
                jnp.concatenate(grad_k_heads, axis=1).astype(jnp.bfloat16),
                jnp.concatenate(grad_v_heads, axis=1).astype(jnp.bfloat16),
            ],
            axis=1,
        )

    received = jnp.zeros((tok_rows, model_width), jnp.bfloat16)
    saved_in = jnp.zeros((micro_count, tok_rows, model_width), jnp.bfloat16)
    saved_att = jnp.zeros((micro_count, tok_rows, model_width), jnp.bfloat16)
    saved_lse = jnp.zeros((micro_count, HEADS, tok_rows), jnp.float32)
    results = jnp.zeros((micro_count, tok_rows, model_width), jnp.bfloat16)
    for tick_index in range(micro_count + 1):
        slot_raw = tick_index - section_index
        is_valid = (slot_raw >= 0) & (slot_raw < micro_count)
        slot_index = jnp.clip(slot_raw, 0, micro_count - 1)
        hidden_low = jnp.where(
            section_index == 0, block_input[min(tick_index, micro_count - 1), 0], received
        )
        hidden = hidden_low.astype(jnp.float32)
        normed, packed = project(hidden)
        masks = segments_of(slot_index)
        dense_dense_mask = masks[2]
        dense_keys_all = lax.all_gather(
            packed[:, model_width : 2 * model_width], "dp", axis=0, tiled=True
        )
        dense_values_all = lax.all_gather(packed[:, 2 * model_width :], "dp", axis=0, tiled=True)
        head_outs = []
        head_lse = []
        for dense_head_index in range(HEADS):
            dense_columns = slice(dense_head_index * head_size, (dense_head_index + 1) * head_size)
            dense_scores = jnp.where(
                dense_dense_mask,
                contract_cols(packed[:, dense_columns], dense_keys_all[:, dense_columns])
                * score_scale,
                NEG,
            )
            dense_attn_probs, lse_row = softmax_parts(dense_scores)
            head_outs.append(product(dense_attn_probs, dense_values_all[:, dense_columns]))
            head_lse.append(lse_row)
        attended = jnp.concatenate(head_outs, axis=1).astype(jnp.bfloat16)
        lse_rows = jnp.stack(head_lse)
        output = finish(hidden, attended)[4].astype(jnp.bfloat16)
        saved_in = put_row(saved_in, hidden_low, slot_index, is_valid)
        saved_att = put_row(saved_att, attended, slot_index, is_valid)
        saved_lse = put_row(saved_lse, lse_rows, slot_index, is_valid)
        results = put_row(results, output, slot_index, is_valid)
        if tick_index < micro_count:
            received = from_behind(output, "section", 1)
    totals = (
        jnp.zeros((model_width,), jnp.float32),
        jnp.zeros(w_qkv.shape, jnp.float32),
        jnp.zeros(w_out.shape, jnp.float32),
        jnp.zeros((model_width,), jnp.float32),
        jnp.zeros(w_up.shape, jnp.float32),
        jnp.zeros(w_down.shape, jnp.float32),
    )
    sent_back = jnp.zeros((tok_rows, model_width), jnp.bfloat16)
    input_grads = jnp.zeros((micro_count, tok_rows, model_width), jnp.bfloat16)
    for tick_index in range(micro_count + 1):
        slot_raw = tick_index - (1 - section_index)
        is_valid = (slot_raw >= 0) & (slot_raw < micro_count)
        slot_index = jnp.clip(slot_raw, 0, micro_count - 1)
        grad_out = jnp.where(
            section_index == 1, output_grad[min(tick_index, micro_count - 1), 0], sent_back
        )
        hidden = lax.dynamic_index_in_dim(saved_in, slot_index, 0, keepdims=False).astype(
            jnp.float32
        )
        attended = lax.dynamic_index_in_dim(saved_att, slot_index, 0, keepdims=False)
        lse_now = lax.dynamic_index_in_dim(saved_lse, slot_index, 0, keepdims=False)
        normed, packed = project(hidden)
        middle, second, pre_act, active, _ = finish(hidden, attended)
        grad_down = contract_rows(active, grad_out)
        grad_active = contract_cols(grad_out, w_down)
        gelu_back = jax.vjp(partial(jax.nn.gelu, approximate=False), pre_act)[1]
        grad_pre = gelu_back(grad_active)[0].astype(jnp.bfloat16)
        grad_up = contract_rows(second, grad_pre)
        ffn_back = jax.vjp(gained, middle, gain_ffn)[1]
        grad_mid_norm, grad_gain_ffn = ffn_back(contract_cols(grad_pre, w_up))
        grad_middle = grad_out.astype(jnp.float32) + grad_mid_norm
        grad_branch = grad_middle.astype(jnp.bfloat16)
        grad_outproj = contract_rows(attended, grad_branch)
        grad_att = contract_cols(grad_branch, w_out).astype(jnp.bfloat16)
        masks = segments_of(slot_index)
        grad_packed = dense_backward(packed, grad_att, lse_now, masks)
        grad_qkv = contract_rows(normed, grad_packed)
        attn_back = jax.vjp(gained, hidden, gain_attn)[1]
        grad_hid_norm, grad_gain_attn = attn_back(contract_cols(grad_packed, w_qkv))
        grad_hidden = (grad_middle + grad_hid_norm).astype(jnp.bfloat16)
        terms = (grad_gain_attn, grad_qkv, grad_outproj, grad_gain_ffn, grad_up, grad_down)
        totals = tuple(
            (
                running + jnp.where(is_valid, term_now, 0.0)
                for running, term_now in zip(totals, terms)
            )
        )
        input_grads = put_row(input_grads, grad_hidden, slot_index, is_valid)
        if tick_index < micro_count:
            sent_back = from_behind(grad_hidden, "section", -1)
    summed = lax.psum(
        (totals[0], totals[1], totals[2], totals[3], totals[4], totals[5]), ("dp", "rep")
    )
    return (
        results[None, :, None],
        input_grads[None, :, None],
        summed[0][None],
        summed[1][None],
        summed[2][None],
        summed[3][None],
        summed[4][None],
        summed[5][None],
    )


BF = jnp.bfloat16
F32 = jnp.float32
MIB = 1024 * 1024
GAIN_ROWS = 16


def in_hbm(array):
    return pltpu.with_memory_space_constraint(array, pltpu.HBM)


def call(body, scalars, arrays, shapes, mib=16, micros=1.0, scratch=(), held=0, out_held=(), aliases=None):
    in_specs = [pl.BlockSpec(memory_space=pltpu.SMEM)] * len(scalars)
    in_specs += [pl.BlockSpec(memory_space=pl.ANY)] * held
    in_specs += [pl.BlockSpec(memory_space=pltpu.VMEM)] * (len(arrays) - held)
    return pl.pallas_call(
        body,
        out_shape=tuple(jax.ShapeDtypeStruct(*shape) for shape in shapes),
        in_specs=in_specs,
        out_specs=tuple(
            pl.BlockSpec(memory_space=pl.ANY if index in out_held else pltpu.VMEM)
            for index in range(len(shapes))
        ),
        scratch_shapes=list(scratch),
        input_output_aliases=aliases or {},
        compiler_params=pltpu.CompilerParams(vmem_limit_bytes=mib * MIB),
        cost_estimate=pl.CostEstimate(
            flops=int(micros * 1.1e9), bytes_accessed=int(micros * 3.4e6), transcendentals=0
        ),
    )(
        *scalars,
        *(array if aliases else in_hbm(array) for array in arrays[:held]),
        *arrays[held:],
    )


def my_section():
    return lax.axis_index("section")


def my_line():
    return lax.axis_index("dp")


def my_flip(core):
    rep = lax.axis_index("rep")
    low, high = rep & 1, rep >> 1
    return 2 * low + high if core == 0 else 2 * high + low


def rows_at(start, count):
    return pl.ds(pl.multiple_of(start, count), count)


def segment_at(ends, position):
    total = jnp.zeros(position.shape, jnp.int32)
    for end in ends:
        total = total + (position >= end).astype(jnp.int32)
    return total


def ends_of(lengths):
    ends = []
    so_far = jnp.int32(0)
    for slot in range(lengths.shape[2]):
        so_far = so_far + lengths[my_line(), lax.axis_index("rep"), slot]
        ends.append(so_far)
    return ends


def write_masks(lengths, window_mask, strided_mask):
    section = my_section()
    rows, reach = window_mask.shape
    half = rows // 4
    block = 2 * half
    ends = ends_of(lengths)
    slots = len(ends)
    query_index = lax.broadcasted_iota(jnp.int32, (half, 1), 0)
    key_index = lax.broadcasted_iota(jnp.int32, (1, reach), 1)
    offset = block + query_index - key_index
    near = (offset >= 0) & (offset < STRIDE)
    for spot in range(4):
        first = block * spot + section * half
        key_pos = first - block + key_index
        query_segment = segment_at(ends, first + query_index)
        key_segment = jnp.where(key_pos >= 0, segment_at(ends, key_pos), slots)
        same = (query_segment == key_segment) & (query_segment < slots)
        window_mask[spot * half : (spot + 1) * half, :] = (same & near | (offset == 0)).astype(F32)

    def place(axis):
        shape = (rows, 1) if axis == 0 else (1, rows)
        index = lax.broadcasted_iota(jnp.int32, shape, axis)
        return block * (index // half) + section * half + (index & (half - 1))

    query_pos, key_pos = place(0), place(1)
    offset = query_pos - key_pos
    segment = segment_at(ends, query_pos)
    same = (segment == segment_at(ends, key_pos)) & (segment < slots)
    allow = same & (offset >= 0) & ((offset & (STRIDE - 1)) == 0) | (offset == 0)
    strided_mask[...] = allow.astype(F32)


def pack_kernel(tokens, grads, gain_attn, gain_ffn, lengths, *rest):
    *pieces, window_mask, strided_mask, gains, lengths_held, sems, side_sems = rest
    block = tokens.shape[2]
    half = block // 2
    rows = rows_at(my_section() * half, half)
    side = [
        pltpu.make_async_copy(lengths, lengths_held, side_sems.at[2]),
        pltpu.make_async_copy(gain_attn, gains.at[0], side_sems.at[0]),
        pltpu.make_async_copy(gain_ffn, gains.at[1], side_sems.at[1]),
    ]
    copies = []
    for step, piece in enumerate(pieces):
        micro = my_line() ^ step
        for part, source in enumerate((tokens, grads)):
            copies.append(
                pltpu.make_async_copy(
                    source.at[micro, 0, rows],
                    piece.at[part * half : (part + 1) * half],
                    sems.at[2 * step + part],
                )
            )
    for copy in (*side, *copies):
        copy.start()
    for copy in side:
        copy.wait()
    write_masks(lengths_held, window_mask, strided_mask)
    pieces[0][block:, :] = jnp.concatenate(
        [
            gains[0].astype(F32),
            gains[1].astype(F32),
            jnp.zeros((pieces[0].shape[0] - block - 2, gains.shape[2]), F32),
        ],
        axis=0,
    ).astype(BF)
    for copy in copies:
        copy.wait()


def unit(values):
    centered = values - jnp.mean(values, axis=-1, keepdims=True)
    inverse = lax.rsqrt(jnp.mean(centered * centered, axis=-1, keepdims=True) + 1e-05)
    return centered * inverse, inverse


def unit_back(grad, normal, inverse):
    return inverse * (
        grad
        - jnp.mean(grad, axis=-1, keepdims=True)
        - normal * jnp.mean(grad * normal, axis=-1, keepdims=True)
    )


def widened(column, width):
    return jnp.broadcast_to(column, (column.shape[0], width))


def normalized_exp(scores):
    shifted = jnp.exp(scores - jnp.max(scores, axis=-1, keepdims=True))
    return shifted * (1.0 / jnp.sum(shifted, axis=-1, keepdims=True))


def ffn_forward(hidden, attended, gain, w_out, w_up, w_down, saved):
    result, middle_unit, middle_inverse, second_ref, active, slope = saved
    middle = hidden + product(attended, w_out)
    normal, inverse = unit(middle)
    middle_unit[...] = normal
    middle_inverse[...] = widened(inverse, middle_inverse.shape[1])
    second = (normal * gain).astype(BF)
    second_ref[...] = second
    chunk = middle.shape[1]
    total = middle
    for index in range(w_up.shape[1] // chunk):
        columns = slice(index * chunk, (index + 1) * chunk)
        pre_act = product(second, w_up[:, columns])
        below = 0.5 + 0.5 * lax.erf(pre_act * (0.5**0.5))
        now = (pre_act * below).astype(BF)
        active[:, columns] = now
        slope[:, columns] = below + pre_act * (
            jnp.exp(-0.5 * pre_act * pre_act) * 0.3989422804014327
        )
        total = total + product(now, w_down[columns, :])
    result[...] = total.astype(BF)


def own_unit(spot, half):
    return slice((2 * spot + 2) * half, (2 * spot + 3) * half)


def key_units(spot, half):
    return slice(2 * spot * half, (2 * spot + 3) * half)


def zero_forward_kernel(
    mask,
    own0,
    own1,
    own2,
    own3,
    far0,
    far1,
    far2,
    far3,
    w_qkv,
    w_out,
    w_up,
    w_down,
    gains,
    line,
    normal_all,
    inverse_all,
    normed_all,
    query,
    padded,
    probs_ref,
    attended_ref,
    cotangent,
    *saved,
):
    section = my_section()
    reached, width = normal_all.shape
    half = line.shape[0] // 10
    block = 2 * half
    blocks = 4
    rows = blocks * half
    head = width // HEADS
    scale = float(head) ** (-0.5)
    reach = block + half
    line[:block, :] = jnp.zeros((block, width), BF)
    for step, (near, far) in enumerate(((own0, far0), (own1, far1), (own2, far2), (own3, far3))):
        spot = my_line() ^ step
        line[rows_at(spot * block + block, half), :] = near[:half, :]
        line[rows_at(spot * block + block + half - section * block, half), :] = far[:half, :]
        cotangent[rows_at(spot * half, half), :] = near[half:block, :]
    normal, inverse = unit(line[:reached, :].astype(F32))
    normal_all[...] = normal
    inverse_all[...] = widened(inverse, inverse_all.shape[1])
    normed = (normal * gains[0, 0:1, :]).astype(BF)
    normed_all[...] = normed
    padded[...] = product(normed, w_qkv[0, :, width:]).astype(BF)
    normed_mine = jnp.concatenate(
        [normed[own_unit(spot, half), :] for spot in range(blocks)], axis=0
    )
    query[...] = product(normed_mine, w_qkv[0, :, :width]).astype(BF)
    spots = [(slice(spot * half, (spot + 1) * half), key_units(spot, half)) for spot in range(blocks)]
    heads = [
        (slice(number * head, (number + 1) * head), slice(width + number * head, width + (number + 1) * head))
        for number in range(HEADS)
    ]
    scores = [
        jnp.concatenate(
            [contract_cols(query[here, columns], padded[window, columns]) for here, window in spots],
            axis=0,
        )
        for columns, _ in heads
    ]
    probs = [normalized_exp(jnp.where(mask[...] > 0.5, values * scale, NEG)) for values in scores]
    attended = []
    for number, (_, value_columns) in enumerate(heads):
        probs_ref[number] = probs[number]
        low = probs[number].astype(BF)
        attended.append(
            jnp.concatenate(
                [product(low[here, :], padded[window, value_columns]) for here, window in spots], axis=0
            )
        )
    attended = jnp.concatenate(attended, axis=1).astype(BF)
    attended_ref[...] = attended
    hidden = jnp.concatenate([line[own_unit(spot, half), :] for spot in range(blocks)], axis=0)
    ffn_forward(
        hidden.astype(F32), attended, gains[0, 1:2, :], w_out[0], w_up.at[0], w_down.at[0], saved
    )


def one_forward_kernel(
    mask,
    hidden_ref,
    w_qkv,
    w_out,
    w_up,
    w_down,
    gains,
    normal_ref,
    inverse_ref,
    normed_ref,
    packed,
    probs_ref,
    attended_ref,
    *saved,
):
    section = my_section()
    rows, width = hidden_ref.shape
    half = rows // 4
    block = 2 * half
    head = width // HEADS
    scale = float(head) ** (-0.5)
    hidden = hidden_ref[...].astype(F32)
    normal, inverse = unit(hidden)
    normal_ref[...] = normal
    inverse_ref[...] = widened(inverse, inverse_ref.shape[1])
    normed = (normal * gains[1, 0:1, :]).astype(BF)
    normed_ref[...] = normed
    packed[...] = product(normed, w_qkv[1]).astype(BF)
    heads = [
        tuple(
            slice(part * width + number * head, part * width + (number + 1) * head) for part in range(3)
        )
        for number in range(HEADS)
    ]
    scores = [contract_cols(packed[:, near], packed[:, far]) for near, far, _ in heads]
    probs = [normalized_exp(jnp.where(mask[...] > 0.5, values * scale, NEG)) for values in scores]
    parts = []
    for number, (_, _, value_columns) in enumerate(heads):
        probs_ref[number] = probs[number]
        parts.append(product(probs[number].astype(BF), packed[:, value_columns]))
    attended = jnp.concatenate(parts, axis=1).astype(BF)
    attended_ref[...] = attended
    ffn_forward(hidden, attended, gains[1, 1:2, :], w_out[1], w_up.at[1], w_down.at[1], saved)


def store_block(terms, number, value):
    width = value.shape[1]
    unit_rows = width // 2
    core, number = divmod(number, 6)
    side, flip = my_section() ^ core, my_flip(core)
    value = value.astype(BF)
    for part in range(2):
        quarter, place = divmod(2 * number + part, 3)
        terms[side, flip ^ quarter, place * unit_rows : (place + 1) * unit_rows, :] = value[
            part * unit_rows : (part + 1) * unit_rows, :
        ]


def store_gains(terms, attn_term, ffn_term):
    spare, width = terms.shape[2] - GAIN_ROWS, terms.shape[3]
    value = jnp.concatenate(
        [attn_term, ffn_term, jnp.zeros((GAIN_ROWS - 2, width), F32)], axis=0
    ).astype(BF)
    for side in range(2):
        for quarter in range(4):
            terms[side, quarter, spare:, :] = value


def ffn_input_grad(grad_out, saved, gain, w_out, w_up, w_down, grad_pre_ref):
    middle_unit, middle_inverse, slope = saved
    width = grad_out.shape[1]
    grad_second = None
    for index in range(w_up.shape[1] // width):
        columns = slice(index * width, (index + 1) * width)
        grad_active = contract_cols(grad_out, w_down[columns, :])
        grad_pre = (grad_active * slope[:, columns]).astype(BF)
        grad_pre_ref[:, columns] = grad_pre
        term = contract_cols(grad_pre, w_up[:, columns])
        grad_second = term if grad_second is None else grad_second + term
    normal = middle_unit[...]
    gain_term = jnp.sum(grad_second * normal, axis=0, keepdims=True)
    grad_middle = grad_out.astype(F32) + unit_back(
        grad_second * gain, normal, middle_inverse[:, 0:1]
    )
    return grad_middle, contract_cols(grad_middle.astype(BF), w_out).astype(BF), gain_term


def ffn_weight_grads(terms, grad_out, grad_middle, second, active, attended, grad_pre):
    width = grad_out.shape[1]
    store_block(terms, 3, contract_rows(attended[...], grad_middle.astype(BF)))
    for index in range(active.shape[1] // width):
        columns = slice(index * width, (index + 1) * width)
        store_block(terms, 4 + index, contract_rows(second[...], grad_pre[:, columns]))
        store_block(terms, 8 + index, contract_rows(active[:, columns], grad_out))


def one_backward_kernel(
    grad_ref,
    w_qkv,
    w_out,
    w_up,
    w_down,
    gains,
    normal_ref,
    inverse_ref,
    normed_ref,
    packed,
    probs_ref,
    *rest,
):
    middle_unit, middle_inverse, second, active, slope, attended, grad_in, terms, grad_pre = rest
    width = grad_ref.shape[1]
    head = width // HEADS
    scale = float(head) ** (-0.5)
    grad_out = grad_ref[...]
    grad_middle, grad_att, ffn_term = ffn_input_grad(
        grad_out,
        (middle_unit, middle_inverse, slope),
        gains[1, 1:2, :],
        w_out[1],
        w_up.at[1],
        w_down.at[1],
        grad_pre,
    )
    ffn_weight_grads(terms, grad_out, grad_middle, second, active, attended, grad_pre)
    heads = [
        tuple(
            slice(part * width + number * head, part * width + (number + 1) * head) for part in range(3)
        )
        for number in range(HEADS)
    ]
    probs = [probs_ref[number] for number in range(HEADS)]
    grad_probs = [
        contract_cols(grad_att[:, near], packed[:, value_columns]) for near, _, value_columns in heads
    ]
    grad_scores = [
        (prob * (grad - jnp.sum(prob * grad, axis=-1, keepdims=True))).astype(BF)
        for prob, grad in zip(probs, grad_probs)
    ]
    grad_parts = [
        [product(grad, packed[:, far]) * scale for grad, (_, far, _) in zip(grad_scores, heads)],
        [contract_rows(grad, packed[:, near]) * scale for grad, (near, _, _) in zip(grad_scores, heads)],
        [contract_rows(prob.astype(BF), grad_att[:, near]) for prob, (near, _, _) in zip(probs, heads)],
    ]
    grad_normed = None
    for index in range(3):
        columns = slice(index * width, (index + 1) * width)
        grad_block = jnp.concatenate(grad_parts[index], axis=1).astype(BF)
        term = contract_cols(grad_block, w_qkv[1, :, columns])
        grad_normed = term if grad_normed is None else grad_normed + term
        store_block(terms, index, contract_rows(normed_ref[...], grad_block))
    normal = normal_ref[...]
    store_gains(terms, jnp.sum(grad_normed * normal, axis=0, keepdims=True), ffn_term)
    grad_in[...] = (
        grad_middle + unit_back(grad_normed * gains[1, 0:1, :], normal, inverse_ref[:, 0:1])
    ).astype(BF)


def one_kernel(mask, hidden_ref, cotangent, *rest):
    weights, rest = rest[:5], rest[5:]
    result_one, grad_one, terms, *held = rest
    normal, inverse, normed, packed, probs, attended = held[:6]
    middle, mid_inverse, second, active, slope, grad_pre = held[6:]
    one_forward_kernel(
        mask,
        hidden_ref,
        *weights,
        *held[:6],
        result_one,
        middle,
        mid_inverse,
        second,
        active,
        slope,
    )
    one_backward_kernel(
        cotangent,
        *weights,
        normal,
        inverse,
        normed,
        packed,
        probs,
        middle,
        mid_inverse,
        second,
        active,
        slope,
        attended,
        grad_one,
        terms,
        grad_pre,
    )


def zero_ffn_kernel(
    grad_ref,
    w_out,
    w_up,
    w_down,
    gains,
    middle_unit,
    middle_inverse,
    slope,
    grad_middle_ref,
    grad_att_ref,
    grad_pre,
    gain_term,
):
    grad_middle, grad_att, term = ffn_input_grad(
        grad_ref[...],
        (middle_unit, middle_inverse, slope),
        gains[0, 1:2, :],
        w_out[0],
        w_up.at[0],
        w_down.at[0],
        grad_pre,
    )
    grad_middle_ref[...] = grad_middle
    grad_att_ref[...] = grad_att
    gain_term[...] = term


def zero_backward_kernel(
    grad_ref,
    w_qkv,
    gains,
    normal_all,
    inverse_all,
    normed_all,
    query,
    padded,
    probs_ref,
    result_zero,
    result_one,
    second,
    active,
    attended,
    grad_middle_ref,
    grad_att_ref,
    grad_pre,
    ffn_term,
    result_keep,
    grad_line,
    swap,
    terms,
):
    section = my_section()
    rows, width = grad_ref.shape
    reached = normal_all.shape[0]
    half = rows // 4
    blocks = 4
    head = width // HEADS
    scale = float(head) ** (-0.5)
    grad_out = grad_ref[...]

    @pl.when(section == 0)
    def _():
        result_keep[...] = result_zero[...]
        swap[:rows, :] = result_one[...]

    @pl.when(section == 1)
    def _():
        result_keep[...] = result_one[...]
        swap[:rows, :] = result_zero[...]

    grad_middle = grad_middle_ref[...]
    grad_att = grad_att_ref[...]
    ffn_weight_grads(terms, grad_out, grad_middle, second, active, attended, grad_pre)
    spots = [(slice(spot * half, (spot + 1) * half), key_units(spot, half)) for spot in range(blocks)]
    heads = [
        (slice(number * head, (number + 1) * head), slice(width + number * head, width + (number + 1) * head))
        for number in range(HEADS)
    ]
    probs = [probs_ref[number] for number in range(HEADS)]
    grad_probs = [
        jnp.concatenate(
            [
                contract_cols(grad_att[here, columns], padded[window, value_columns])
                for here, window in spots
            ],
            axis=0,
        )
        for columns, value_columns in heads
    ]
    grad_scores = [
        (prob * (grad - jnp.sum(prob * grad, axis=-1, keepdims=True))).astype(BF)
        for prob, grad in zip(probs, grad_probs)
    ]
    grad_query = [
        jnp.concatenate(
            [product(grad[here, :], padded[window, columns]) for here, window in spots], axis=0
        )
        * scale
        for grad, (columns, _) in zip(grad_scores, heads)
    ]
    grad_query = jnp.concatenate(grad_query, axis=1).astype(BF)

    def gathered(lefts, right):
        parts = []
        for left, (columns, _) in zip(lefts, heads):
            terms_of = [contract_rows(left[here, :], right[here, columns]) for here, _ in spots]
            units = []
            for index in range(reached // half):
                spot, place = divmod(index, 2)
                held = None
                if spot < blocks:
                    held = terms_of[spot][place * half : (place + 1) * half, :]
                if place == 0 and spot > 0:
                    last = terms_of[spot - 1][2 * half :, :]
                    held = last if held is None else held + last
                units.append(held)
            parts.append(jnp.concatenate(units, axis=0))
        return jnp.concatenate(parts, axis=1)

    grad_keys = (gathered(grad_scores, query) * scale).astype(BF)
    grad_values = gathered([prob.astype(BF) for prob in probs], grad_att).astype(BF)
    normed = normed_all[...]
    normed_mine = jnp.concatenate(
        [normed[own_unit(spot, half), :] for spot in range(blocks)], axis=0
    )
    store_block(terms, 0, contract_rows(normed_mine, grad_query))
    store_block(terms, 1, contract_rows(normed, grad_keys))
    store_block(terms, 2, contract_rows(normed, grad_values))
    from_query = contract_cols(grad_query, w_qkv[0, :, :width])
    grad_line[:reached, :] = contract_cols(
        grad_keys, w_qkv[0, :, width : 2 * width]
    ) + contract_cols(grad_values, w_qkv[0, :, 2 * width :])
    for spot in range(blocks):
        grad_line[own_unit(spot, half), :] += from_query[spot * half : (spot + 1) * half, :]
    grad_normed = grad_line[:reached, :]
    normal = normal_all[...]
    store_gains(terms, jnp.sum(grad_normed * normal, axis=0, keepdims=True), ffn_term[...])
    grad_line[:reached, :] = unit_back(grad_normed * gains[0, 0:1, :], normal, inverse_all[:, 0:1])
    for spot in range(blocks):
        grad_line[own_unit(spot, half), :] += grad_middle[spot * half : (spot + 1) * half, :]
    grad_line[reached:, :] = jnp.zeros((grad_line.shape[0] - reached, width), F32)

    @pl.when(section == 0)
    def _():
        swap[rows : 2 * rows, :] = grad_out

    @pl.when(section == 1)
    def _():
        swap[rows:, :] = grad_line[:reached, :].astype(BF)


def zero_both_kernel(
    grad_ref,
    w_qkv,
    w_out,
    w_up,
    w_down,
    gains,
    middle_unit,
    middle_inverse,
    slope,
    *rest,
):
    *rest, grad_middle, grad_att, grad_pre, gain_term = rest
    zero_ffn_kernel(
        grad_ref,
        w_out,
        w_up,
        w_down,
        gains,
        middle_unit,
        middle_inverse,
        slope,
        grad_middle,
        grad_att,
        grad_pre,
        gain_term,
    )
    inputs, outputs = rest[:-4], rest[-4:]
    zero_backward_kernel(
        grad_ref, w_qkv, gains, *inputs, grad_middle, grad_att, grad_pre, gain_term, *outputs
    )


def share_kernel(keep, one_near, zero_near, came, *pieces):
    rows = keep.shape[0]
    half = rows // 4
    block = 2 * half
    section = my_section()
    near_rows = rows_at(section * half, half)
    far_rows = rows_at(half - section * half, half)
    for step, piece in enumerate(pieces):
        spot = my_line() ^ step
        mine = rows_at(spot * half, half)
        piece[near_rows, :] = keep[mine, :]
        piece[far_rows, :] = came[mine, :]

    @pl.when(section == 0)
    def _():
        for step, piece in enumerate(pieces):
            base = (my_line() ^ step) * block
            near, far = rows_at(base + block, block), rows_at(rows + base + half, half)
            far = pl.ds(far.start, block)
            piece[block:, :] = (zero_near[near, :] + came[far, :].astype(F32)).astype(BF)

    @pl.when(section == 1)
    def _():
        for step, piece in enumerate(pieces):
            spot = my_line() ^ step
            piece[block : block + half, :] = came[rows_at(rows + spot * half, half), :]
            piece[block + half :, :] = one_near[rows_at(spot * half, half), :]


def settle_kernel(piece0, piece1, piece2, piece3, results, input_grads):
    block = piece0.shape[0] // 2
    for step, piece in enumerate((piece0, piece1, piece2, piece3)):
        micro = my_line() ^ step
        results[0, micro, 0] = piece[:block, :]
        input_grads[0, micro, 0] = piece[block:, :]


def write_half(core, terms, targets, held, sems):
    width = terms.shape[2]
    unit_rows = width // 2
    copies = []
    for place in range(6):
        number = 6 * core + place
        for part in range(2):
            quarter, spot = divmod(2 * place + part, 3)
            value = terms[my_flip(core) ^ quarter, spot * unit_rows : (spot + 1) * unit_rows, :]
            held[place, part * unit_rows : (part + 1) * unit_rows, :] = value.astype(F32)
        which = 0 if number < 3 else 1 if number == 3 else 2 if number < 8 else 3
        first = (number, 0, number - 4, number - 8)[which] * width
        rows = pl.ds(first if which == 3 else 0, width)
        columns = pl.ds(0 if which in (1, 3) else first, width)
        copies.append(
            pltpu.make_async_copy(
                held.at[place], targets[which].at[0, rows, columns], sems.at[place]
            )
        )
        copies[-1].start()
    for copy in copies:
        copy.wait()


def by_section(body):
    for core in range(2):
        pl.when(my_section() == core)(partial(body, core))


def near_kernel(zero, one, gain_attn, qkv, out, gain_ffn, up, down, held, sems):
    spare = zero.shape[1] - GAIN_ROWS

    def body(core):
        terms = (zero, one)[core]
        gains = terms[0, spare:, :].astype(F32)
        gain_attn[...] = gains[0:1, :]
        gain_ffn[...] = gains[1:2, :]
        write_half(core, terms, (qkv, out, up, down), held, sems)

    by_section(body)


def far_kernel(qkv_in, out_in, up_in, down_in, zero, one, qkv, out, up, down, held, sems):
    by_section(
        lambda core: write_half(1 - core, (zero, one)[core], (qkv, out, up, down), held, sems)
    )


SWAP = [(0, 1), (1, 0)]
PLANE = ("section", "rep")


def crossed(flips):
    return [(4 * s + g, 4 * s + (g ^ flips[s])) for s in range(2) for g in range(4)]


FIRST = crossed((1, 2))
SECOND = crossed((2, 1))


def along_line(value, step):
    return lax.ppermute(value, "dp", [(z, z ^ step) for z in range(4)])


def reduce_terms(terms, came, zed, home, before, between=None):
    bar = lax.optimization_barrier
    first = lax.ppermute(terms[0, 2:4] + came[2:4], PLANE, FIRST)
    second = lax.ppermute(terms[0, 1] + came[1] + first[1], PLANE, SECOND)
    total = bar(terms[0, 0] + came[0] + first[0] + second)
    total, home[before] = bar((total, home[before]))
    total = bar(total + along_line(total, 1))
    if between is not None:
        total, home[between] = bar((total, home[between]))
    half = total.shape[0] // 2
    odd = zed & 1
    mine = lax.dynamic_slice_in_dim(total, odd * half, half, 0)
    mine = bar(mine + along_line(mine, 2))
    other = along_line(mine, 1)
    total = bar(
        jnp.where(
            odd == 0, jnp.concatenate([mine, other]), jnp.concatenate([other, mine])
        )
    )
    pair = jnp.stack([total, lax.ppermute(total, PLANE, SECOND)])
    return pair, lax.ppermute(pair, PLANE, FIRST)


def lines(
    block_input,
    output_grad,
    seq_lengths,
    attn_gain,
    qkv_proj,
    out_proj,
    ffn_gain,
    up_proj,
    down_proj,
):
    section = lax.axis_index("section")
    zed = lax.axis_index("dp")
    micro_count, _, block, width = block_input.shape
    hidden_units = up_proj.shape[2]
    half = block // 2
    rows, reach = micro_count * half, block + half
    reached = rows + rows + half
    term_rows = 6 * width // 4 + GAIN_ROWS

    *packed, window_mask, strided_mask = call(
        pack_kernel,
        (),
        (block_input, output_grad, attn_gain, ffn_gain, seq_lengths),
        (
            ((block + 16, width), BF),
            *((((block, width), BF),) * (micro_count - 1)),
            ((rows, reach), F32),
            ((rows, rows), F32),
        ),
        8,
        scratch=(
            pltpu.VMEM((2, 1, width), BF),
            pltpu.SMEM(seq_lengths.shape, jnp.int32),
            pltpu.SemaphoreType.DMA((2 * micro_count,)),
            pltpu.SemaphoreType.DMA((3,)),
        ),
        held=5,
    )
    near = [packed[0]] + [along_line(packed[step], step) for step in range(1, micro_count)]
    far = [lax.ppermute(piece, "section", SWAP) for piece in near]
    own = (qkv_proj[0], out_proj[0], up_proj[0], down_proj[0])
    near[1], *own = lax.optimization_barrier((near[1], *own))
    swapped = [lax.ppermute(weight, "section", SWAP) for weight in own]
    weights = tuple(
        jnp.stack([jnp.where(section == 0, a, b), jnp.where(section == 0, b, a)])
        for a, b in zip(own, swapped)
    )
    gains_near, gains_far = near[0][block:].astype(F32), far[0][block:].astype(F32)
    weights += (
        jnp.stack(
            [
                jnp.where(section == 0, gains_near, gains_far),
                jnp.where(section == 0, gains_far, gains_near),
            ]
        ),
    )
    ffn_saved = (
        ((rows, width), BF),
        ((rows, width), F32),
        ((rows, 128), F32),
        ((rows, width), BF),
        ((rows, hidden_units), BF),
        ((rows, hidden_units), F32),
    )
    (
        _,
        normal_all,
        inverse_all,
        normed_all,
        query,
        padded,
        probs_zero,
        attended_zero,
        cotangent,
        result_zero,
        *saved_zero,
    ) = call(
        zero_forward_kernel,
        (),
        (window_mask, *near, *far, *weights),
        (
            ((reached + half, width), BF),
            ((reached, width), F32),
            ((reached, 128), F32),
            ((reached, width), BF),
            ((rows, width), BF),
            ((reached, 2 * width), BF),
            ((HEADS, rows, reach), F32),
            ((rows, width), BF),
            ((rows, width), BF),
            *ffn_saved,
        ),
    )
    result_one, grad_one, terms_one = call(
        one_kernel,
        (),
        (strided_mask, result_zero, cotangent, *weights),
        (((rows, width), BF), ((rows, width), BF), ((2, 4, term_rows, width), BF)),
        micros=4.0,
        scratch=(
            pltpu.VMEM((rows, width), F32),
            pltpu.VMEM((rows, 128), F32),
            pltpu.VMEM((rows, width), BF),
            pltpu.VMEM((rows, 3 * width), BF),
            pltpu.VMEM((HEADS, rows, rows), F32),
            pltpu.VMEM((rows, width), BF),
            *(pltpu.VMEM(*shape) for shape in ffn_saved[1:]),
            pltpu.VMEM((rows, hidden_units), BF),
        ),
    )
    middle_zero, mid_inverse_zero, second_zero, active_zero, slope_zero = saved_zero
    came_one = lax.ppermute(terms_one[1], "section", SWAP)
    result_keep, grad_line, swap, terms_zero = call(
        zero_both_kernel,
        (),
        (
            grad_one,
            *weights,
            middle_zero,
            mid_inverse_zero,
            slope_zero,
            normal_all,
            inverse_all,
            normed_all,
            query,
            padded,
            probs_zero,
            result_zero,
            result_one,
            second_zero,
            active_zero,
            attended_zero,
        ),
        (
            ((rows, width), BF),
            ((reached + half, width), F32),
            ((rows + reached, width), BF),
            ((2, 4, term_rows, width), BF),
        ),
        micros=4.0,
        scratch=(
            pltpu.VMEM((rows, width), F32),
            pltpu.VMEM((rows, width), BF),
            pltpu.VMEM((rows, hidden_units), BF),
            pltpu.VMEM((1, width), F32),
        ),
    )
    came = lax.ppermute(swap, "section", SWAP)
    shared = call(
        share_kernel,
        (),
        (result_keep, grad_one, grad_line, came),
        (((2 * block, width), BF),) * micro_count,
        8,
    )
    home = [shared[0]] + [along_line(shared[step], step) for step in range(1, micro_count)]
    came_zero = lax.ppermute(terms_zero[1], "section", SWAP)
    one_pair, one_first = reduce_terms(terms_one, came_one, zed, home, 1, 3)
    zero_pair, zero_first = reduce_terms(terms_zero, came_zero, zed, home, 2)
    results, input_grads = call(
        settle_kernel,
        (),
        home,
        (((1, micro_count, 1, block, width), BF),) * 2,
        8,
    )

    def both_cores(parts):
        near = jnp.concatenate(parts)
        return near, jnp.concatenate([lax.ppermute(part, "section", SWAP) for part in parts])

    zero_near, zero_far = both_cores((zero_pair, zero_first))
    one_near, one_far = both_cores((one_pair, one_first))
    sums = (
        ((1, width, 3 * width), F32),
        ((1, width, width), F32),
        ((1, width, hidden_units), F32),
        ((1, hidden_units, width), F32),
    )
    held = (pltpu.VMEM((6, width, width), F32), pltpu.SemaphoreType.DMA((6,)))
    gain_attn_sum, qkv_half, out_half, gain_ffn_sum, up_half, down_half = call(
        near_kernel,
        (),
        (zero_near, one_near),
        (((1, width), F32), *sums[:2], ((1, width), F32), *sums[2:]),
        16,
        scratch=held,
        out_held=(1, 2, 4, 5),
    )
    qkv_sum, out_sum, up_sum, down_sum = call(
        far_kernel,
        (),
        (qkv_half, out_half, up_half, down_half, zero_far, one_far),
        sums,
        16,
        scratch=held,
        held=4,
        out_held=(0, 1, 2, 3),
        aliases={0: 0, 1: 1, 2: 2, 3: 3},
    )
    return (
        results,
        input_grads,
        gain_attn_sum,
        qkv_sum,
        out_sum,
        gain_ffn_sum,
        up_sum,
        down_sum,
    )


def local(*arrays):
    micro_count, _, tok_rows, model_width = arrays[0].shape
    one_line_per_chip = (
        lax.axis_size("section") == 2
        and lax.axis_size("dp") == 4
        and lax.axis_size("rep") == 4
        and micro_count == 4
        and tok_rows == STRIDE
        and model_width == 256
        and arrays[7].shape[2] == 4 * model_width
    )
    return lines(*arrays) if one_line_per_chip else general(*arrays)


def solution(mesh):
    placed = (
        P(None, "rep", "dp", None),
        P(None, "rep", "dp", None),
        P(),
        P("section", None),
        P("section", None, None),
        P("section", None, None),
        P("section", None),
        P("section", None, None),
        P("section", None, None),
    )
    return jax.shard_map(
        local,
        mesh=mesh,
        in_specs=placed,
        out_specs=(
            P("section", None, "rep", "dp", None),
            P("section", None, "rep", "dp", None),
            P("section", None),
            P("section", None, None),
            P("section", None, None),
            P("section", None),
            P("section", None, None),
            P("section", None, None),
        ),
        check_vma=False,
    )
```

```python
from functools import partial

import jax
import jax.numpy as jnp
from jax import lax
from jax.experimental import pallas as pl
from jax.experimental.pallas import tpu as pltpu
from jax.sharding import PartitionSpec as P

HEADS = 2
STRIDE = 128


NEG = -1e30


def from_behind(shard, axis, by):
    length = lax.axis_size(axis)
    pairs = [(i, i + by) for i in range(length) if 0 <= i + by < length]
    return lax.ppermute(shard, axis, pairs)


def normalize(values):
    centered = values - jnp.mean(values, axis=-1, keepdims=True)
    spread = jnp.mean(centered * centered, axis=-1, keepdims=True)
    return centered * lax.rsqrt(spread + 1e-05)


def gained(values, gain):
    return normalize(values) * gain


def allowed(query_pos, query_seg, key_pos, key_seg, strided, seq_slots):
    offset = query_pos - key_pos
    same_seq = (query_seg == key_seg) & (query_seg < seq_slots)
    nearby = (offset >= 0) & (offset < STRIDE)
    spaced = (offset >= 0) & (offset % STRIDE == 0)
    pattern = jnp.where(strided, spaced, nearby)
    return same_seq & pattern | (offset == 0)


def product(left, right):
    return jnp.dot(left, right, preferred_element_type=jnp.float32)


def contract_rows(left, right):
    return lax.dot_general(
        left, right, (((0,), (0,)), ((), ())), preferred_element_type=jnp.float32
    )


def contract_cols(left, right):
    return lax.dot_general(
        left, right, (((1,), (1,)), ((), ())), preferred_element_type=jnp.float32
    )


def put_row(buffer, value, slot_index, is_valid):
    current = lax.dynamic_index_in_dim(buffer, slot_index, 0, keepdims=False)
    return lax.dynamic_update_index_in_dim(
        buffer, jnp.where(is_valid, value, current), slot_index, 0
    )


def softmax_parts(scores):
    row_max = jnp.max(scores, axis=-1, keepdims=True)
    shifted = jnp.exp(scores - row_max)
    row_total = jnp.sum(shifted, axis=-1, keepdims=True)
    return ((shifted / row_total).astype(jnp.bfloat16), (row_max + jnp.log(row_total))[..., 0])


def general(
    block_input,
    output_grad,
    seq_lengths,
    attn_gain,
    qkv_proj,
    out_proj,
    ffn_gain,
    up_proj,
    down_proj,
):
    section_index = lax.axis_index("section")
    line_row = lax.axis_index("dp")
    group_index = lax.axis_index("rep")
    strided = section_index == 1
    micro_count, _, tok_rows, model_width = block_input.shape
    line_count = lax.axis_size("dp")
    line_span = tok_rows * line_count
    head_size = model_width // HEADS
    score_scale = float(head_size) ** (-0.5)
    seq_slots = seq_lengths.shape[-1]
    block_count = line_span // STRIDE
    residues = STRIDE // line_count
    line_lengths = lax.dynamic_index_in_dim(seq_lengths, group_index, 1, keepdims=False)
    all_pos = jnp.arange(line_span, dtype=jnp.int32)
    my_pos = line_row * tok_rows + jnp.arange(tok_rows, dtype=jnp.int32)
    win_pos = line_row * tok_rows - tok_rows + jnp.arange(2 * tok_rows, dtype=jnp.int32)
    res_pos = (
        jnp.arange(block_count, dtype=jnp.int32)[None, :] * STRIDE
        + line_row * residues
        + jnp.arange(residues, dtype=jnp.int32)[:, None]
    )
    gain_attn = attn_gain[0].astype(jnp.float32)
    gain_ffn = ffn_gain[0].astype(jnp.float32)
    w_qkv = qkv_proj[0]
    w_out = out_proj[0]
    w_up = up_proj[0]
    w_down = down_proj[0]

    def segments_of(slot_index):
        seq_ends = jnp.cumsum(lax.dynamic_index_in_dim(line_lengths, slot_index, 0, keepdims=False))
        all_seg = jnp.sum((all_pos[:, None] >= seq_ends[None, :]).astype(jnp.int32), axis=1)
        my_seg = lax.dynamic_slice_in_dim(all_seg, line_row * tok_rows, tok_rows)
        padded = jnp.concatenate([jnp.full((tok_rows,), seq_slots, jnp.int32), all_seg])
        win_seg = lax.dynamic_slice_in_dim(padded, line_row * tok_rows, 2 * tok_rows)
        res_seg = lax.dynamic_slice_in_dim(
            all_seg.reshape(block_count, STRIDE), line_row * residues, residues, 1
        ).T
        dense_mask = allowed(
            my_pos[:, None], my_seg[:, None], all_pos[None, :], all_seg[None, :], strided, seq_slots
        )
        win_mask = allowed(
            my_pos[:, None], my_seg[:, None], win_pos[None, :], win_seg[None, :], False, seq_slots
        )
        res_mask = allowed(
            res_pos[:, :, None],
            res_seg[:, :, None],
            res_pos[:, None, :],
            res_seg[:, None, :],
            True,
            seq_slots,
        )
        return (all_seg, my_seg, dense_mask, win_mask, res_mask)

    def project(hidden):
        normed = gained(hidden, gain_attn).astype(jnp.bfloat16)
        packed = product(normed, w_qkv).astype(jnp.bfloat16)
        return (normed, packed)

    def finish(hidden, attended):
        middle = hidden + product(attended, w_out)
        second = gained(middle, gain_ffn).astype(jnp.bfloat16)
        pre_act = product(second, w_up)
        active = jax.nn.gelu(pre_act, approximate=False).astype(jnp.bfloat16)
        return (middle, second, pre_act, active, middle + product(active, w_down))

    def dense_backward(packed, grad_att, lse_now, masks):
        all_seg, my_seg, dense_mask = (masks[0], masks[1], masks[2])
        queries = packed[:, :model_width]
        key_rows = packed[:, model_width : 2 * model_width]
        values = packed[:, 2 * model_width :]
        keys_all, values_all = (
            lax.all_gather(key_rows, "dp", axis=0, tiled=True),
            lax.all_gather(values, "dp", axis=0, tiled=True),
        )
        grad_q_heads = []
        grad_k_heads = []
        grad_v_heads = []
        delta_heads = []
        for head_index in range(HEADS):
            columns = slice(head_index * head_size, (head_index + 1) * head_size)
            query_head = queries[:, columns]
            out_head = grad_att[:, columns]
            scores = jnp.where(
                dense_mask, contract_cols(query_head, keys_all[:, columns]) * score_scale, NEG
            )
            attn_probs = jnp.exp(scores - lse_now[head_index][:, None])
            grad_probs = contract_cols(out_head, values_all[:, columns])
            delta_row = jnp.sum(attn_probs * grad_probs, axis=1)
            grad_scores = (attn_probs * (grad_probs - delta_row[:, None])).astype(jnp.bfloat16)
            grad_q_heads.append(product(grad_scores, keys_all[:, columns]) * score_scale)
            delta_heads.append(delta_row)
            key_part = contract_rows(grad_scores, query_head) * score_scale
            value_part = contract_rows(attn_probs.astype(jnp.bfloat16), out_head)
            key_mine, value_mine = (
                lax.psum_scatter(
                    key_part.astype(jnp.bfloat16), "dp", scatter_dimension=0, tiled=True
                ).astype(jnp.float32),
                lax.psum_scatter(
                    value_part.astype(jnp.bfloat16), "dp", scatter_dimension=0, tiled=True
                ).astype(jnp.float32),
            )
            grad_k_heads.append(key_mine)
            grad_v_heads.append(value_mine)
        return jnp.concatenate(
            [
                jnp.concatenate(grad_q_heads, axis=1).astype(jnp.bfloat16),
                jnp.concatenate(grad_k_heads, axis=1).astype(jnp.bfloat16),
                jnp.concatenate(grad_v_heads, axis=1).astype(jnp.bfloat16),
            ],
            axis=1,
        )

    received = jnp.zeros((tok_rows, model_width), jnp.bfloat16)
    saved_in = jnp.zeros((micro_count, tok_rows, model_width), jnp.bfloat16)
    saved_att = jnp.zeros((micro_count, tok_rows, model_width), jnp.bfloat16)
    saved_lse = jnp.zeros((micro_count, HEADS, tok_rows), jnp.float32)
    results = jnp.zeros((micro_count, tok_rows, model_width), jnp.bfloat16)
    for tick_index in range(micro_count + 1):
        slot_raw = tick_index - section_index
        is_valid = (slot_raw >= 0) & (slot_raw < micro_count)
        slot_index = jnp.clip(slot_raw, 0, micro_count - 1)
        hidden_low = jnp.where(
            section_index == 0, block_input[min(tick_index, micro_count - 1), 0], received
        )
        hidden = hidden_low.astype(jnp.float32)
        normed, packed = project(hidden)
        masks = segments_of(slot_index)
        dense_dense_mask = masks[2]
        dense_keys_all = lax.all_gather(
            packed[:, model_width : 2 * model_width], "dp", axis=0, tiled=True
        )
        dense_values_all = lax.all_gather(packed[:, 2 * model_width :], "dp", axis=0, tiled=True)
        head_outs = []
        head_lse = []
        for dense_head_index in range(HEADS):
            dense_columns = slice(dense_head_index * head_size, (dense_head_index + 1) * head_size)
            dense_scores = jnp.where(
                dense_dense_mask,
                contract_cols(packed[:, dense_columns], dense_keys_all[:, dense_columns])
                * score_scale,
                NEG,
            )
            dense_attn_probs, lse_row = softmax_parts(dense_scores)
            head_outs.append(product(dense_attn_probs, dense_values_all[:, dense_columns]))
            head_lse.append(lse_row)
        attended = jnp.concatenate(head_outs, axis=1).astype(jnp.bfloat16)
        lse_rows = jnp.stack(head_lse)
        output = finish(hidden, attended)[4].astype(jnp.bfloat16)
        saved_in = put_row(saved_in, hidden_low, slot_index, is_valid)
        saved_att = put_row(saved_att, attended, slot_index, is_valid)
        saved_lse = put_row(saved_lse, lse_rows, slot_index, is_valid)
        results = put_row(results, output, slot_index, is_valid)
        if tick_index < micro_count:
            received = from_behind(output, "section", 1)
    totals = (
        jnp.zeros((model_width,), jnp.float32),
        jnp.zeros(w_qkv.shape, jnp.float32),
        jnp.zeros(w_out.shape, jnp.float32),
        jnp.zeros((model_width,), jnp.float32),
        jnp.zeros(w_up.shape, jnp.float32),
        jnp.zeros(w_down.shape, jnp.float32),
    )
    sent_back = jnp.zeros((tok_rows, model_width), jnp.bfloat16)
    input_grads = jnp.zeros((micro_count, tok_rows, model_width), jnp.bfloat16)
    for tick_index in range(micro_count + 1):
        slot_raw = tick_index - (1 - section_index)
        is_valid = (slot_raw >= 0) & (slot_raw < micro_count)
        slot_index = jnp.clip(slot_raw, 0, micro_count - 1)
        grad_out = jnp.where(
            section_index == 1, output_grad[min(tick_index, micro_count - 1), 0], sent_back
        )
        hidden = lax.dynamic_index_in_dim(saved_in, slot_index, 0, keepdims=False).astype(
            jnp.float32
        )
        attended = lax.dynamic_index_in_dim(saved_att, slot_index, 0, keepdims=False)
        lse_now = lax.dynamic_index_in_dim(saved_lse, slot_index, 0, keepdims=False)
        normed, packed = project(hidden)
        middle, second, pre_act, active, _ = finish(hidden, attended)
        grad_down = contract_rows(active, grad_out)
        grad_active = contract_cols(grad_out, w_down)
        gelu_back = jax.vjp(partial(jax.nn.gelu, approximate=False), pre_act)[1]
        grad_pre = gelu_back(grad_active)[0].astype(jnp.bfloat16)
        grad_up = contract_rows(second, grad_pre)
        ffn_back = jax.vjp(gained, middle, gain_ffn)[1]
        grad_mid_norm, grad_gain_ffn = ffn_back(contract_cols(grad_pre, w_up))
        grad_middle = grad_out.astype(jnp.float32) + grad_mid_norm
        grad_branch = grad_middle.astype(jnp.bfloat16)
        grad_outproj = contract_rows(attended, grad_branch)
        grad_att = contract_cols(grad_branch, w_out).astype(jnp.bfloat16)
        masks = segments_of(slot_index)
        grad_packed = dense_backward(packed, grad_att, lse_now, masks)
        grad_qkv = contract_rows(normed, grad_packed)
        attn_back = jax.vjp(gained, hidden, gain_attn)[1]
        grad_hid_norm, grad_gain_attn = attn_back(contract_cols(grad_packed, w_qkv))
        grad_hidden = (grad_middle + grad_hid_norm).astype(jnp.bfloat16)
        terms = (grad_gain_attn, grad_qkv, grad_outproj, grad_gain_ffn, grad_up, grad_down)
        totals = tuple(
            (
                running + jnp.where(is_valid, term_now, 0.0)
                for running, term_now in zip(totals, terms)
            )
        )
        input_grads = put_row(input_grads, grad_hidden, slot_index, is_valid)
        if tick_index < micro_count:
            sent_back = from_behind(grad_hidden, "section", -1)
    summed = lax.psum(
        (totals[0], totals[1], totals[2], totals[3], totals[4], totals[5]), ("dp", "rep")
    )
    return (
        results[None, :, None],
        input_grads[None, :, None],
        summed[0][None],
        summed[1][None],
        summed[2][None],
        summed[3][None],
        summed[4][None],
        summed[5][None],
    )


BF = jnp.bfloat16
F32 = jnp.float32
MIB = 1024 * 1024
GAIN_ROWS = 16


def in_hbm(array):
    return pltpu.with_memory_space_constraint(array, pltpu.HBM)


def call(body, scalars, arrays, shapes, mib=16, micros=1.0, scratch=(), held=0, out_held=(), aliases=None):
    in_specs = [pl.BlockSpec(memory_space=pltpu.SMEM)] * len(scalars)
    in_specs += [pl.BlockSpec(memory_space=pl.ANY)] * held
    in_specs += [pl.BlockSpec(memory_space=pltpu.VMEM)] * (len(arrays) - held)
    return pl.pallas_call(
        body,
        out_shape=tuple(jax.ShapeDtypeStruct(*shape) for shape in shapes),
        in_specs=in_specs,
        out_specs=tuple(
            pl.BlockSpec(memory_space=pl.ANY if index in out_held else pltpu.VMEM)
            for index in range(len(shapes))
        ),
        scratch_shapes=list(scratch),
        input_output_aliases=aliases or {},
        compiler_params=pltpu.CompilerParams(vmem_limit_bytes=mib * MIB),
        cost_estimate=pl.CostEstimate(
            flops=int(micros * 1.1e9), bytes_accessed=int(micros * 3.4e6), transcendentals=0
        ),
    )(
        *scalars,
        *(array if aliases else in_hbm(array) for array in arrays[:held]),
        *arrays[held:],
    )


def my_section():
    return lax.axis_index("section")


def my_line():
    return lax.axis_index("dp")


def my_flip(core):
    rep = lax.axis_index("rep")
    low, high = rep & 1, rep >> 1
    return 2 * low + high if core == 0 else 2 * high + low


def rows_at(start, count):
    return pl.ds(pl.multiple_of(start, count), count)


def segment_at(ends, position):
    total = jnp.zeros(position.shape, jnp.int32)
    for end in ends:
        total = total + (position >= end).astype(jnp.int32)
    return total


def ends_of(lengths):
    ends = []
    so_far = jnp.int32(0)
    for slot in range(lengths.shape[2]):
        so_far = so_far + lengths[my_line(), lax.axis_index("rep"), slot]
        ends.append(so_far)
    return ends


def write_masks(lengths, window_mask, strided_mask):
    section = my_section()
    rows, reach = window_mask.shape
    half = rows // 4
    block = 2 * half
    ends = ends_of(lengths)
    slots = len(ends)
    query_index = lax.broadcasted_iota(jnp.int32, (half, 1), 0)
    key_index = lax.broadcasted_iota(jnp.int32, (1, reach), 1)
    offset = block + query_index - key_index
    near = (offset >= 0) & (offset < STRIDE)
    for spot in range(4):
        first = block * spot + section * half
        key_pos = first - block + key_index
        query_segment = segment_at(ends, first + query_index)
        key_segment = jnp.where(key_pos >= 0, segment_at(ends, key_pos), slots)
        same = (query_segment == key_segment) & (query_segment < slots)
        window_mask[spot * half : (spot + 1) * half, :] = (same & near | (offset == 0)).astype(F32)

    def place(axis):
        shape = (rows, 1) if axis == 0 else (1, rows)
        index = lax.broadcasted_iota(jnp.int32, shape, axis)
        return block * (index // half) + section * half + (index & (half - 1))

    query_pos, key_pos = place(0), place(1)
    offset = query_pos - key_pos
    segment = segment_at(ends, query_pos)
    same = (segment == segment_at(ends, key_pos)) & (segment < slots)
    allow = same & (offset >= 0) & ((offset & (STRIDE - 1)) == 0) | (offset == 0)
    strided_mask[...] = allow.astype(F32)


def pack_kernel(tokens, grads, gain_attn, gain_ffn, lengths, *rest):
    *pieces, window_mask, strided_mask, gains, lengths_held, sems, side_sems = rest
    block = tokens.shape[2]
    half = block // 2
    rows = rows_at(my_section() * half, half)
    side = [
        pltpu.make_async_copy(lengths, lengths_held, side_sems.at[2]),
        pltpu.make_async_copy(gain_attn, gains.at[0], side_sems.at[0]),
        pltpu.make_async_copy(gain_ffn, gains.at[1], side_sems.at[1]),
    ]
    copies = []
    for step, piece in enumerate(pieces):
        micro = my_line() ^ step
        for part, source in enumerate((tokens, grads)):
            copies.append(
                pltpu.make_async_copy(
                    source.at[micro, 0, rows],
                    piece.at[part * half : (part + 1) * half],
                    sems.at[2 * step + part],
                )
            )
    for copy in (*side, *copies):
        copy.start()
    for copy in side:
        copy.wait()
    write_masks(lengths_held, window_mask, strided_mask)
    pieces[0][block:, :] = jnp.concatenate(
        [
            gains[0].astype(F32),
            gains[1].astype(F32),
            jnp.zeros((pieces[0].shape[0] - block - 2, gains.shape[2]), F32),
        ],
        axis=0,
    ).astype(BF)
    for copy in copies:
        copy.wait()


def unit(values):
    centered = values - jnp.mean(values, axis=-1, keepdims=True)
    inverse = lax.rsqrt(jnp.mean(centered * centered, axis=-1, keepdims=True) + 1e-05)
    return centered * inverse, inverse


def unit_back(grad, normal, inverse):
    return inverse * (
        grad
        - jnp.mean(grad, axis=-1, keepdims=True)
        - normal * jnp.mean(grad * normal, axis=-1, keepdims=True)
    )


def widened(column, width):
    return jnp.broadcast_to(column, (column.shape[0], width))


def normalized_exp(scores):
    shifted = jnp.exp(scores - jnp.max(scores, axis=-1, keepdims=True))
    return shifted * (1.0 / jnp.sum(shifted, axis=-1, keepdims=True))


def ffn_forward(hidden, attended, gain, w_out, w_up, w_down, saved):
    result, middle_unit, middle_inverse, second_ref, active, slope = saved
    middle = hidden + product(attended, w_out)
    normal, inverse = unit(middle)
    middle_unit[...] = normal
    middle_inverse[...] = widened(inverse, middle_inverse.shape[1])
    second = (normal * gain).astype(BF)
    second_ref[...] = second
    chunk = middle.shape[1]
    total = middle
    for index in range(w_up.shape[1] // chunk):
        columns = slice(index * chunk, (index + 1) * chunk)
        pre_act = product(second, w_up[:, columns])
        below = 0.5 + 0.5 * lax.erf(pre_act * (0.5**0.5))
        now = (pre_act * below).astype(BF)
        active[:, columns] = now
        slope[:, columns] = below + pre_act * (
            jnp.exp(-0.5 * pre_act * pre_act) * 0.3989422804014327
        )
        total = total + product(now, w_down[columns, :])
    result[...] = total.astype(BF)


def own_unit(spot, half):
    return slice((2 * spot + 2) * half, (2 * spot + 3) * half)


def key_units(spot, half):
    return slice(2 * spot * half, (2 * spot + 3) * half)


def zero_forward_kernel(
    mask,
    own0,
    own1,
    own2,
    own3,
    far0,
    far1,
    far2,
    far3,
    w_qkv,
    w_out,
    w_up,
    w_down,
    gains,
    line,
    normal_all,
    inverse_all,
    normed_all,
    query,
    padded,
    probs_ref,
    attended_ref,
    cotangent,
    *saved,
):
    section = my_section()
    reached, width = normal_all.shape
    half = line.shape[0] // 10
    block = 2 * half
    blocks = 4
    rows = blocks * half
    head = width // HEADS
    scale = float(head) ** (-0.5)
    reach = block + half
    line[:block, :] = jnp.zeros((block, width), BF)
    for step, (near, far) in enumerate(((own0, far0), (own1, far1), (own2, far2), (own3, far3))):
        spot = my_line() ^ step
        line[rows_at(spot * block + block, half), :] = near[:half, :]
        line[rows_at(spot * block + block + half - section * block, half), :] = far[:half, :]
        cotangent[rows_at(spot * half, half), :] = near[half:block, :]
    normal, inverse = unit(line[:reached, :].astype(F32))
    normal_all[...] = normal
    inverse_all[...] = widened(inverse, inverse_all.shape[1])
    normed = (normal * gains[0, 0:1, :]).astype(BF)
    normed_all[...] = normed
    padded[...] = product(normed, w_qkv[0, :, width:]).astype(BF)
    normed_mine = jnp.concatenate(
        [normed[own_unit(spot, half), :] for spot in range(blocks)], axis=0
    )
    query[...] = product(normed_mine, w_qkv[0, :, :width]).astype(BF)
    spots = [(slice(spot * half, (spot + 1) * half), key_units(spot, half)) for spot in range(blocks)]
    heads = [
        (slice(number * head, (number + 1) * head), slice(width + number * head, width + (number + 1) * head))
        for number in range(HEADS)
    ]
    scores = [
        jnp.concatenate(
            [contract_cols(query[here, columns], padded[window, columns]) for here, window in spots],
            axis=0,
        )
        for columns, _ in heads
    ]
    probs = [normalized_exp(jnp.where(mask[...] > 0.5, values * scale, NEG)) for values in scores]
    attended = []
    for number, (_, value_columns) in enumerate(heads):
        probs_ref[number] = probs[number]
        low = probs[number].astype(BF)
        attended.append(
            jnp.concatenate(
                [product(low[here, :], padded[window, value_columns]) for here, window in spots], axis=0
            )
        )
    attended = jnp.concatenate(attended, axis=1).astype(BF)
    attended_ref[...] = attended
    hidden = jnp.concatenate([line[own_unit(spot, half), :] for spot in range(blocks)], axis=0)
    ffn_forward(
        hidden.astype(F32), attended, gains[0, 1:2, :], w_out[0], w_up.at[0], w_down.at[0], saved
    )


def one_forward_kernel(
    mask,
    hidden_ref,
    w_qkv,
    w_out,
    w_up,
    w_down,
    gains,
    normal_ref,
    inverse_ref,
    normed_ref,
    packed,
    probs_ref,
    attended_ref,
    *saved,
):
    section = my_section()
    rows, width = hidden_ref.shape
    half = rows // 4
    block = 2 * half
    head = width // HEADS
    scale = float(head) ** (-0.5)
    hidden = hidden_ref[...].astype(F32)
    normal, inverse = unit(hidden)
    normal_ref[...] = normal
    inverse_ref[...] = widened(inverse, inverse_ref.shape[1])
    normed = (normal * gains[1, 0:1, :]).astype(BF)
    normed_ref[...] = normed
    packed[...] = product(normed, w_qkv[1]).astype(BF)
    heads = [
        tuple(
            slice(part * width + number * head, part * width + (number + 1) * head) for part in range(3)
        )
        for number in range(HEADS)
    ]
    scores = [contract_cols(packed[:, near], packed[:, far]) for near, far, _ in heads]
    probs = [normalized_exp(jnp.where(mask[...] > 0.5, values * scale, NEG)) for values in scores]
    parts = []
    for number, (_, _, value_columns) in enumerate(heads):
        probs_ref[number] = probs[number]
        parts.append(product(probs[number].astype(BF), packed[:, value_columns]))
    attended = jnp.concatenate(parts, axis=1).astype(BF)
    attended_ref[...] = attended
    ffn_forward(hidden, attended, gains[1, 1:2, :], w_out[1], w_up.at[1], w_down.at[1], saved)


def store_block(terms, number, value):
    width = value.shape[1]
    unit_rows = width // 2
    core, number = divmod(number, 6)
    side, flip = my_section() ^ core, my_flip(core)
    value = value.astype(BF)
    for part in range(2):
        quarter, place = divmod(2 * number + part, 3)
        terms[side, flip ^ quarter, place * unit_rows : (place + 1) * unit_rows, :] = value[
            part * unit_rows : (part + 1) * unit_rows, :
        ]


def store_gains(terms, attn_term, ffn_term):
    spare, width = terms.shape[2] - GAIN_ROWS, terms.shape[3]
    value = jnp.concatenate(
        [attn_term, ffn_term, jnp.zeros((GAIN_ROWS - 2, width), F32)], axis=0
    ).astype(BF)
    for side in range(2):
        for quarter in range(4):
            terms[side, quarter, spare:, :] = value


def ffn_input_grad(grad_out, saved, gain, w_out, w_up, w_down, grad_pre_ref):
    middle_unit, middle_inverse, slope = saved
    width = grad_out.shape[1]
    grad_second = None
    for index in range(w_up.shape[1] // width):
        columns = slice(index * width, (index + 1) * width)
        grad_active = contract_cols(grad_out, w_down[columns, :])
        grad_pre = (grad_active * slope[:, columns]).astype(BF)
        grad_pre_ref[:, columns] = grad_pre
        term = contract_cols(grad_pre, w_up[:, columns])
        grad_second = term if grad_second is None else grad_second + term
    normal = middle_unit[...]
    gain_term = jnp.sum(grad_second * normal, axis=0, keepdims=True)
    grad_middle = grad_out.astype(F32) + unit_back(
        grad_second * gain, normal, middle_inverse[:, 0:1]
    )
    return grad_middle, contract_cols(grad_middle.astype(BF), w_out).astype(BF), gain_term


def ffn_weight_grads(terms, grad_out, grad_middle, second, active, attended, grad_pre):
    width = grad_out.shape[1]
    store_block(terms, 3, contract_rows(attended[...], grad_middle.astype(BF)))
    for index in range(active.shape[1] // width):
        columns = slice(index * width, (index + 1) * width)
        store_block(terms, 4 + index, contract_rows(second[...], grad_pre[:, columns]))
        store_block(terms, 8 + index, contract_rows(active[:, columns], grad_out))


def one_backward_kernel(
    grad_ref,
    w_qkv,
    w_out,
    w_up,
    w_down,
    gains,
    normal_ref,
    inverse_ref,
    normed_ref,
    packed,
    probs_ref,
    *rest,
):
    middle_unit, middle_inverse, second, active, slope, attended, grad_in, terms, grad_pre = rest
    width = grad_ref.shape[1]
    head = width // HEADS
    scale = float(head) ** (-0.5)
    grad_out = grad_ref[...]
    grad_middle, grad_att, ffn_term = ffn_input_grad(
        grad_out,
        (middle_unit, middle_inverse, slope),
        gains[1, 1:2, :],
        w_out[1],
        w_up.at[1],
        w_down.at[1],
        grad_pre,
    )
    ffn_weight_grads(terms, grad_out, grad_middle, second, active, attended, grad_pre)
    heads = [
        tuple(
            slice(part * width + number * head, part * width + (number + 1) * head) for part in range(3)
        )
        for number in range(HEADS)
    ]
    probs = [probs_ref[number] for number in range(HEADS)]
    grad_probs = [
        contract_cols(grad_att[:, near], packed[:, value_columns]) for near, _, value_columns in heads
    ]
    grad_scores = [
        (prob * (grad - jnp.sum(prob * grad, axis=-1, keepdims=True))).astype(BF)
        for prob, grad in zip(probs, grad_probs)
    ]
    grad_parts = [
        [product(grad, packed[:, far]) * scale for grad, (_, far, _) in zip(grad_scores, heads)],
        [contract_rows(grad, packed[:, near]) * scale for grad, (near, _, _) in zip(grad_scores, heads)],
        [contract_rows(prob.astype(BF), grad_att[:, near]) for prob, (near, _, _) in zip(probs, heads)],
    ]
    grad_normed = None
    for index in range(3):
        columns = slice(index * width, (index + 1) * width)
        grad_block = jnp.concatenate(grad_parts[index], axis=1).astype(BF)
        term = contract_cols(grad_block, w_qkv[1, :, columns])
        grad_normed = term if grad_normed is None else grad_normed + term
        store_block(terms, index, contract_rows(normed_ref[...], grad_block))
    normal = normal_ref[...]
    store_gains(terms, jnp.sum(grad_normed * normal, axis=0, keepdims=True), ffn_term)
    grad_in[...] = (
        grad_middle + unit_back(grad_normed * gains[1, 0:1, :], normal, inverse_ref[:, 0:1])
    ).astype(BF)


def one_kernel(mask, hidden_ref, cotangent, *rest):
    weights, rest = rest[:5], rest[5:]
    result_one, grad_one, keep, send, *held, terms = rest
    normal, inverse, normed, packed, probs, attended = held[:6]
    middle, mid_inverse, second, active, slope, grad_pre = held[6:]
    one_forward_kernel(
        mask,
        hidden_ref,
        *weights,
        *held[:6],
        result_one,
        middle,
        mid_inverse,
        second,
        active,
        slope,
    )
    one_backward_kernel(
        cotangent,
        *weights,
        normal,
        inverse,
        normed,
        packed,
        probs,
        middle,
        mid_inverse,
        second,
        active,
        slope,
        attended,
        grad_one,
        terms,
        grad_pre,
    )
    keep[...] = terms[0]
    send[...] = terms[1]


def zero_ffn_kernel(
    grad_ref,
    w_out,
    w_up,
    w_down,
    gains,
    middle_unit,
    middle_inverse,
    slope,
    grad_middle_ref,
    grad_att_ref,
    grad_pre,
    gain_term,
):
    grad_middle, grad_att, term = ffn_input_grad(
        grad_ref[...],
        (middle_unit, middle_inverse, slope),
        gains[0, 1:2, :],
        w_out[0],
        w_up.at[0],
        w_down.at[0],
        grad_pre,
    )
    grad_middle_ref[...] = grad_middle
    grad_att_ref[...] = grad_att
    gain_term[...] = term


def zero_backward_kernel(
    grad_ref,
    w_qkv,
    gains,
    normal_all,
    inverse_all,
    normed_all,
    query,
    padded,
    probs_ref,
    result_zero,
    result_one,
    second,
    active,
    attended,
    grad_middle_ref,
    grad_att_ref,
    grad_pre,
    ffn_term,
    result_keep,
    grad_line,
    swap,
    terms,
):
    section = my_section()
    rows, width = grad_ref.shape
    reached = normal_all.shape[0]
    half = rows // 4
    blocks = 4
    head = width // HEADS
    scale = float(head) ** (-0.5)
    grad_out = grad_ref[...]

    @pl.when(section == 0)
    def _():
        result_keep[...] = result_zero[...]
        swap[:rows, :] = result_one[...]

    @pl.when(section == 1)
    def _():
        result_keep[...] = result_one[...]
        swap[:rows, :] = result_zero[...]

    grad_middle = grad_middle_ref[...]
    grad_att = grad_att_ref[...]
    ffn_weight_grads(terms, grad_out, grad_middle, second, active, attended, grad_pre)
    spots = [(slice(spot * half, (spot + 1) * half), key_units(spot, half)) for spot in range(blocks)]
    heads = [
        (slice(number * head, (number + 1) * head), slice(width + number * head, width + (number + 1) * head))
        for number in range(HEADS)
    ]
    probs = [probs_ref[number] for number in range(HEADS)]
    grad_probs = [
        jnp.concatenate(
            [
                contract_cols(grad_att[here, columns], padded[window, value_columns])
                for here, window in spots
            ],
            axis=0,
        )
        for columns, value_columns in heads
    ]
    grad_scores = [
        (prob * (grad - jnp.sum(prob * grad, axis=-1, keepdims=True))).astype(BF)
        for prob, grad in zip(probs, grad_probs)
    ]
    grad_query = [
        jnp.concatenate(
            [product(grad[here, :], padded[window, columns]) for here, window in spots], axis=0
        )
        * scale
        for grad, (columns, _) in zip(grad_scores, heads)
    ]
    grad_query = jnp.concatenate(grad_query, axis=1).astype(BF)

    def gathered(lefts, right):
        parts = []
        for left, (columns, _) in zip(lefts, heads):
            terms_of = [contract_rows(left[here, :], right[here, columns]) for here, _ in spots]
            units = []
            for index in range(reached // half):
                spot, place = divmod(index, 2)
                held = None
                if spot < blocks:
                    held = terms_of[spot][place * half : (place + 1) * half, :]
                if place == 0 and spot > 0:
                    last = terms_of[spot - 1][2 * half :, :]
                    held = last if held is None else held + last
                units.append(held)
            parts.append(jnp.concatenate(units, axis=0))
        return jnp.concatenate(parts, axis=1)

    grad_keys = (gathered(grad_scores, query) * scale).astype(BF)
    grad_values = gathered([prob.astype(BF) for prob in probs], grad_att).astype(BF)
    normed = normed_all[...]
    normed_mine = jnp.concatenate(
        [normed[own_unit(spot, half), :] for spot in range(blocks)], axis=0
    )
    store_block(terms, 0, contract_rows(normed_mine, grad_query))
    store_block(terms, 1, contract_rows(normed, grad_keys))
    store_block(terms, 2, contract_rows(normed, grad_values))
    from_query = contract_cols(grad_query, w_qkv[0, :, :width])
    grad_line[:reached, :] = contract_cols(
        grad_keys, w_qkv[0, :, width : 2 * width]
    ) + contract_cols(grad_values, w_qkv[0, :, 2 * width :])
    for spot in range(blocks):
        grad_line[own_unit(spot, half), :] += from_query[spot * half : (spot + 1) * half, :]
    grad_normed = grad_line[:reached, :]
    normal = normal_all[...]
    store_gains(terms, jnp.sum(grad_normed * normal, axis=0, keepdims=True), ffn_term[...])
    grad_line[:reached, :] = unit_back(grad_normed * gains[0, 0:1, :], normal, inverse_all[:, 0:1])
    for spot in range(blocks):
        grad_line[own_unit(spot, half), :] += grad_middle[spot * half : (spot + 1) * half, :]
    grad_line[reached:, :] = jnp.zeros((grad_line.shape[0] - reached, width), F32)

    @pl.when(section == 0)
    def _():
        swap[rows : 2 * rows, :] = grad_out

    @pl.when(section == 1)
    def _():
        swap[rows:, :] = grad_line[:reached, :].astype(BF)


def zero_both_kernel(
    grad_ref,
    w_qkv,
    w_out,
    w_up,
    w_down,
    gains,
    middle_unit,
    middle_inverse,
    slope,
    *rest,
):
    *rest, grad_middle, grad_att, grad_pre, gain_term, terms = rest
    zero_ffn_kernel(
        grad_ref,
        w_out,
        w_up,
        w_down,
        gains,
        middle_unit,
        middle_inverse,
        slope,
        grad_middle,
        grad_att,
        grad_pre,
        gain_term,
    )
    inputs, outputs, (keep, send) = rest[:-5], rest[-5:-2], rest[-2:]
    zero_backward_kernel(
        grad_ref, w_qkv, gains, *inputs, grad_middle, grad_att, grad_pre, gain_term, *outputs, terms
    )
    keep[...] = terms[0]
    send[...] = terms[1]


def share_kernel(keep, one_near, zero_near, came, *pieces):
    rows = keep.shape[0]
    half = rows // 4
    block = 2 * half
    section = my_section()
    near_rows = rows_at(section * half, half)
    far_rows = rows_at(half - section * half, half)
    for step, piece in enumerate(pieces):
        spot = my_line() ^ step
        mine = rows_at(spot * half, half)
        piece[near_rows, :] = keep[mine, :]
        piece[far_rows, :] = came[mine, :]

    @pl.when(section == 0)
    def _():
        for step, piece in enumerate(pieces):
            base = (my_line() ^ step) * block
            near, far = rows_at(base + block, block), rows_at(rows + base + half, half)
            far = pl.ds(far.start, block)
            piece[block:, :] = (zero_near[near, :] + came[far, :].astype(F32)).astype(BF)

    @pl.when(section == 1)
    def _():
        for step, piece in enumerate(pieces):
            spot = my_line() ^ step
            piece[block : block + half, :] = came[rows_at(rows + spot * half, half), :]
            piece[block + half :, :] = one_near[rows_at(spot * half, half), :]


def settle_kernel(piece0, piece1, piece2, piece3, results, input_grads):
    block = piece0.shape[0] // 2
    for step, piece in enumerate((piece0, piece1, piece2, piece3)):
        micro = my_line() ^ step
        results[0, micro, 0] = piece[:block, :]
        input_grads[0, micro, 0] = piece[block:, :]


def write_half(core, terms, targets, held, sems):
    width = terms.shape[2]
    unit_rows = width // 2
    copies = []
    for place in range(6):
        number = 6 * core + place
        for part in range(2):
            quarter, spot = divmod(2 * place + part, 3)
            value = terms[my_flip(core) ^ quarter, spot * unit_rows : (spot + 1) * unit_rows, :]
            held[place, part * unit_rows : (part + 1) * unit_rows, :] = value.astype(F32)
        which = 0 if number < 3 else 1 if number == 3 else 2 if number < 8 else 3
        first = (number, 0, number - 4, number - 8)[which] * width
        rows = pl.ds(first if which == 3 else 0, width)
        columns = pl.ds(0 if which in (1, 3) else first, width)
        copies.append(
            pltpu.make_async_copy(
                held.at[place], targets[which].at[0, rows, columns], sems.at[place]
            )
        )
        copies[-1].start()
    for copy in copies:
        copy.wait()


def by_section(body):
    for core in range(2):
        pl.when(my_section() == core)(partial(body, core))


def near_kernel(zero, one, gain_attn, qkv, out, gain_ffn, up, down, held, sems):
    spare = zero.shape[1] - GAIN_ROWS

    def body(core):
        terms = (zero, one)[core]
        gains = terms[0, spare:, :].astype(F32)
        gain_attn[...] = gains[0:1, :]
        gain_ffn[...] = gains[1:2, :]
        write_half(core, terms, (qkv, out, up, down), held, sems)

    by_section(body)


def far_kernel(qkv_in, out_in, up_in, down_in, zero, one, qkv, out, up, down, held, sems):
    by_section(
        lambda core: write_half(1 - core, (zero, one)[core], (qkv, out, up, down), held, sems)
    )


SWAP = [(0, 1), (1, 0)]
PLANE = ("section", "rep")


def crossed(flips):
    return [(4 * s + g, 4 * s + (g ^ flips[s])) for s in range(2) for g in range(4)]


FIRST = crossed((1, 2))
SECOND = crossed((2, 1))


def along_line(value, step):
    return lax.ppermute(value, "dp", [(z, z ^ step) for z in range(4)])


def reduce_terms(keep, came, home, steps, before, between=None):
    bar = lax.optimization_barrier
    first = lax.ppermute(keep[2:4] + came[2:4], PLANE, FIRST)
    second = lax.ppermute(keep[1] + came[1] + first[1], PLANE, SECOND)
    total = bar(keep[0] + came[0] + first[0] + second)
    total, home[before] = bar((total, home[before]))
    total = bar(total + along_line(total, steps[0]))
    if between is not None:
        total, home[between] = bar((total, home[between]))
    total = bar(total + along_line(total, steps[1]))
    pair = jnp.stack([total, lax.ppermute(total, PLANE, SECOND)])
    return pair, lax.ppermute(pair, PLANE, FIRST)


def lines(
    block_input,
    output_grad,
    seq_lengths,
    attn_gain,
    qkv_proj,
    out_proj,
    ffn_gain,
    up_proj,
    down_proj,
):
    section = lax.axis_index("section")
    micro_count, _, block, width = block_input.shape
    hidden_units = up_proj.shape[2]
    half = block // 2
    rows, reach = micro_count * half, block + half
    reached = rows + rows + half
    term_rows = 6 * width // 4 + GAIN_ROWS

    *packed, window_mask, strided_mask = call(
        pack_kernel,
        (),
        (block_input, output_grad, attn_gain, ffn_gain, seq_lengths),
        (
            ((block + 16, width), BF),
            *((((block, width), BF),) * (micro_count - 1)),
            ((rows, reach), F32),
            ((rows, rows), F32),
        ),
        8,
        scratch=(
            pltpu.VMEM((2, 1, width), BF),
            pltpu.SMEM(seq_lengths.shape, jnp.int32),
            pltpu.SemaphoreType.DMA((2 * micro_count,)),
            pltpu.SemaphoreType.DMA((3,)),
        ),
        held=5,
    )
    near = [packed[0]] + [along_line(packed[step], step) for step in range(1, micro_count)]
    far = [lax.ppermute(piece, "section", SWAP) for piece in near]
    own = (qkv_proj[0], out_proj[0], up_proj[0], down_proj[0])
    near[1], *own = lax.optimization_barrier((near[1], *own))
    swapped = [lax.ppermute(weight, "section", SWAP) for weight in own]
    weights = tuple(
        jnp.stack([jnp.where(section == 0, a, b), jnp.where(section == 0, b, a)])
        for a, b in zip(own, swapped)
    )
    gains_near, gains_far = near[0][block:].astype(F32), far[0][block:].astype(F32)
    weights += (
        jnp.stack(
            [
                jnp.where(section == 0, gains_near, gains_far),
                jnp.where(section == 0, gains_far, gains_near),
            ]
        ),
    )
    ffn_saved = (
        ((rows, width), BF),
        ((rows, width), F32),
        ((rows, 128), F32),
        ((rows, width), BF),
        ((rows, hidden_units), BF),
        ((rows, hidden_units), F32),
    )
    (
        _,
        normal_all,
        inverse_all,
        normed_all,
        query,
        padded,
        probs_zero,
        attended_zero,
        cotangent,
        result_zero,
        *saved_zero,
    ) = call(
        zero_forward_kernel,
        (),
        (window_mask, *near, *far, *weights),
        (
            ((reached + half, width), BF),
            ((reached, width), F32),
            ((reached, 128), F32),
            ((reached, width), BF),
            ((rows, width), BF),
            ((reached, 2 * width), BF),
            ((HEADS, rows, reach), F32),
            ((rows, width), BF),
            ((rows, width), BF),
            *ffn_saved,
        ),
    )
    result_one, grad_one, keep_one, send_one = call(
        one_kernel,
        (),
        (strided_mask, result_zero, cotangent, *weights),
        (((rows, width), BF), ((rows, width), BF), *(((4, term_rows, width), BF),) * 2),
        micros=4.0,
        scratch=(
            pltpu.VMEM((rows, width), F32),
            pltpu.VMEM((rows, 128), F32),
            pltpu.VMEM((rows, width), BF),
            pltpu.VMEM((rows, 3 * width), BF),
            pltpu.VMEM((HEADS, rows, rows), F32),
            pltpu.VMEM((rows, width), BF),
            *(pltpu.VMEM(*shape) for shape in ffn_saved[1:]),
            pltpu.VMEM((rows, hidden_units), BF),
            pltpu.VMEM((2, 4, term_rows, width), BF),
        ),
    )
    middle_zero, mid_inverse_zero, second_zero, active_zero, slope_zero = saved_zero
    came_one = lax.ppermute(send_one, "section", SWAP)
    result_keep, grad_line, swap, keep_zero, send_zero = call(
        zero_both_kernel,
        (),
        (
            grad_one,
            *weights,
            middle_zero,
            mid_inverse_zero,
            slope_zero,
            normal_all,
            inverse_all,
            normed_all,
            query,
            padded,
            probs_zero,
            result_zero,
            result_one,
            second_zero,
            active_zero,
            attended_zero,
        ),
        (
            ((rows, width), BF),
            ((reached + half, width), F32),
            ((rows + reached, width), BF),
            *(((4, term_rows, width), BF),) * 2,
        ),
        micros=4.0,
        scratch=(
            pltpu.VMEM((rows, width), F32),
            pltpu.VMEM((rows, width), BF),
            pltpu.VMEM((rows, hidden_units), BF),
            pltpu.VMEM((1, width), F32),
            pltpu.VMEM((2, 4, term_rows, width), BF),
        ),
    )
    came = lax.ppermute(swap, "section", SWAP)
    shared = call(
        share_kernel,
        (),
        (result_keep, grad_one, grad_line, came),
        (((2 * block, width), BF),) * micro_count,
        8,
    )
    home = [shared[0]] + [along_line(shared[step], step) for step in range(1, micro_count)]
    came_zero = lax.ppermute(send_zero, "section", SWAP)
    one_pair, one_first = reduce_terms(keep_one, came_one, home, (2, 1), 3, 2)
    zero_pair, zero_first = reduce_terms(keep_zero, came_zero, home, (1, 2), 1)
    results, input_grads = call(
        settle_kernel,
        (),
        home,
        (((1, micro_count, 1, block, width), BF),) * 2,
        8,
    )

    def both_cores(parts):
        near = jnp.concatenate(parts)
        return near, jnp.concatenate([lax.ppermute(part, "section", SWAP) for part in parts])

    zero_near, zero_far = both_cores((zero_pair, zero_first))
    one_near, one_far = both_cores((one_pair, one_first))
    sums = (
        ((1, width, 3 * width), F32),
        ((1, width, width), F32),
        ((1, width, hidden_units), F32),
        ((1, hidden_units, width), F32),
    )
    held = (pltpu.VMEM((6, width, width), F32), pltpu.SemaphoreType.DMA((6,)))
    gain_attn_sum, qkv_half, out_half, gain_ffn_sum, up_half, down_half = call(
        near_kernel,
        (),
        (zero_near, one_near),
        (((1, width), F32), *sums[:2], ((1, width), F32), *sums[2:]),
        16,
        scratch=held,
        out_held=(1, 2, 4, 5),
    )
    qkv_sum, out_sum, up_sum, down_sum = call(
        far_kernel,
        (),
        (qkv_half, out_half, up_half, down_half, zero_far, one_far),
        sums,
        16,
        scratch=held,
        held=4,
        out_held=(0, 1, 2, 3),
        aliases={0: 0, 1: 1, 2: 2, 3: 3},
    )
    return (
        results,
        input_grads,
        gain_attn_sum,
        qkv_sum,
        out_sum,
        gain_ffn_sum,
        up_sum,
        down_sum,
    )


def local(*arrays):
    micro_count, _, tok_rows, model_width = arrays[0].shape
    one_line_per_chip = (
        lax.axis_size("section") == 2
        and lax.axis_size("dp") == 4
        and lax.axis_size("rep") == 4
        and micro_count == 4
        and tok_rows == STRIDE
        and model_width == 256
        and arrays[7].shape[2] == 4 * model_width
    )
    return lines(*arrays) if one_line_per_chip else general(*arrays)


def solution(mesh):
    placed = (
        P(None, "rep", "dp", None),
        P(None, "rep", "dp", None),
        P(),
        P("section", None),
        P("section", None, None),
        P("section", None, None),
        P("section", None),
        P("section", None, None),
        P("section", None, None),
    )
    return jax.shard_map(
        local,
        mesh=mesh,
        in_specs=placed,
        out_specs=(
            P("section", None, "rep", "dp", None),
            P("section", None, "rep", "dp", None),
            P("section", None),
            P("section", None, None),
            P("section", None, None),
            P("section", None),
            P("section", None, None),
            P("section", None, None),
        ),
        check_vma=False,
    )
```

```python
from functools import partial

import jax
import jax.numpy as jnp
from jax import lax
from jax.experimental import pallas as pl
from jax.experimental.pallas import tpu as pltpu
from jax.sharding import PartitionSpec as P

HEADS = 2
STRIDE = 128


NEG = -1e30


def from_behind(shard, axis, by):
    length = lax.axis_size(axis)
    pairs = [(i, i + by) for i in range(length) if 0 <= i + by < length]
    return lax.ppermute(shard, axis, pairs)


def normalize(values):
    centered = values - jnp.mean(values, axis=-1, keepdims=True)
    spread = jnp.mean(centered * centered, axis=-1, keepdims=True)
    return centered * lax.rsqrt(spread + 1e-05)


def gained(values, gain):
    return normalize(values) * gain


def allowed(query_pos, query_seg, key_pos, key_seg, strided, seq_slots):
    offset = query_pos - key_pos
    same_seq = (query_seg == key_seg) & (query_seg < seq_slots)
    nearby = (offset >= 0) & (offset < STRIDE)
    spaced = (offset >= 0) & (offset % STRIDE == 0)
    pattern = jnp.where(strided, spaced, nearby)
    return same_seq & pattern | (offset == 0)


def product(left, right):
    return jnp.dot(left, right, preferred_element_type=jnp.float32)


def contract_rows(left, right):
    return lax.dot_general(
        left, right, (((0,), (0,)), ((), ())), preferred_element_type=jnp.float32
    )


def contract_cols(left, right):
    return lax.dot_general(
        left, right, (((1,), (1,)), ((), ())), preferred_element_type=jnp.float32
    )


def put_row(buffer, value, slot_index, is_valid):
    current = lax.dynamic_index_in_dim(buffer, slot_index, 0, keepdims=False)
    return lax.dynamic_update_index_in_dim(
        buffer, jnp.where(is_valid, value, current), slot_index, 0
    )


def softmax_parts(scores):
    row_max = jnp.max(scores, axis=-1, keepdims=True)
    shifted = jnp.exp(scores - row_max)
    row_total = jnp.sum(shifted, axis=-1, keepdims=True)
    return ((shifted / row_total).astype(jnp.bfloat16), (row_max + jnp.log(row_total))[..., 0])


def general(
    block_input,
    output_grad,
    seq_lengths,
    attn_gain,
    qkv_proj,
    out_proj,
    ffn_gain,
    up_proj,
    down_proj,
):
    section_index = lax.axis_index("section")
    line_row = lax.axis_index("dp")
    group_index = lax.axis_index("rep")
    strided = section_index == 1
    micro_count, _, tok_rows, model_width = block_input.shape
    line_count = lax.axis_size("dp")
    line_span = tok_rows * line_count
    head_size = model_width // HEADS
    score_scale = float(head_size) ** (-0.5)
    seq_slots = seq_lengths.shape[-1]
    block_count = line_span // STRIDE
    residues = STRIDE // line_count
    line_lengths = lax.dynamic_index_in_dim(seq_lengths, group_index, 1, keepdims=False)
    all_pos = jnp.arange(line_span, dtype=jnp.int32)
    my_pos = line_row * tok_rows + jnp.arange(tok_rows, dtype=jnp.int32)
    win_pos = line_row * tok_rows - tok_rows + jnp.arange(2 * tok_rows, dtype=jnp.int32)
    res_pos = (
        jnp.arange(block_count, dtype=jnp.int32)[None, :] * STRIDE
        + line_row * residues
        + jnp.arange(residues, dtype=jnp.int32)[:, None]
    )
    gain_attn = attn_gain[0].astype(jnp.float32)
    gain_ffn = ffn_gain[0].astype(jnp.float32)
    w_qkv = qkv_proj[0]
    w_out = out_proj[0]
    w_up = up_proj[0]
    w_down = down_proj[0]

    def segments_of(slot_index):
        seq_ends = jnp.cumsum(lax.dynamic_index_in_dim(line_lengths, slot_index, 0, keepdims=False))
        all_seg = jnp.sum((all_pos[:, None] >= seq_ends[None, :]).astype(jnp.int32), axis=1)
        my_seg = lax.dynamic_slice_in_dim(all_seg, line_row * tok_rows, tok_rows)
        padded = jnp.concatenate([jnp.full((tok_rows,), seq_slots, jnp.int32), all_seg])
        win_seg = lax.dynamic_slice_in_dim(padded, line_row * tok_rows, 2 * tok_rows)
        res_seg = lax.dynamic_slice_in_dim(
            all_seg.reshape(block_count, STRIDE), line_row * residues, residues, 1
        ).T
        dense_mask = allowed(
            my_pos[:, None], my_seg[:, None], all_pos[None, :], all_seg[None, :], strided, seq_slots
        )
        win_mask = allowed(
            my_pos[:, None], my_seg[:, None], win_pos[None, :], win_seg[None, :], False, seq_slots
        )
        res_mask = allowed(
            res_pos[:, :, None],
            res_seg[:, :, None],
            res_pos[:, None, :],
            res_seg[:, None, :],
            True,
            seq_slots,
        )
        return (all_seg, my_seg, dense_mask, win_mask, res_mask)

    def project(hidden):
        normed = gained(hidden, gain_attn).astype(jnp.bfloat16)
        packed = product(normed, w_qkv).astype(jnp.bfloat16)
        return (normed, packed)

    def finish(hidden, attended):
        middle = hidden + product(attended, w_out)
        second = gained(middle, gain_ffn).astype(jnp.bfloat16)
        pre_act = product(second, w_up)
        active = jax.nn.gelu(pre_act, approximate=False).astype(jnp.bfloat16)
        return (middle, second, pre_act, active, middle + product(active, w_down))

    def dense_backward(packed, grad_att, lse_now, masks):
        all_seg, my_seg, dense_mask = (masks[0], masks[1], masks[2])
        queries = packed[:, :model_width]
        key_rows = packed[:, model_width : 2 * model_width]
        values = packed[:, 2 * model_width :]
        keys_all, values_all = (
            lax.all_gather(key_rows, "dp", axis=0, tiled=True),
            lax.all_gather(values, "dp", axis=0, tiled=True),
        )
        grad_q_heads = []
        grad_k_heads = []
        grad_v_heads = []
        delta_heads = []
        for head_index in range(HEADS):
            columns = slice(head_index * head_size, (head_index + 1) * head_size)
            query_head = queries[:, columns]
            out_head = grad_att[:, columns]
            scores = jnp.where(
                dense_mask, contract_cols(query_head, keys_all[:, columns]) * score_scale, NEG
            )
            attn_probs = jnp.exp(scores - lse_now[head_index][:, None])
            grad_probs = contract_cols(out_head, values_all[:, columns])
            delta_row = jnp.sum(attn_probs * grad_probs, axis=1)
            grad_scores = (attn_probs * (grad_probs - delta_row[:, None])).astype(jnp.bfloat16)
            grad_q_heads.append(product(grad_scores, keys_all[:, columns]) * score_scale)
            delta_heads.append(delta_row)
            key_part = contract_rows(grad_scores, query_head) * score_scale
            value_part = contract_rows(attn_probs.astype(jnp.bfloat16), out_head)
            key_mine, value_mine = (
                lax.psum_scatter(
                    key_part.astype(jnp.bfloat16), "dp", scatter_dimension=0, tiled=True
                ).astype(jnp.float32),
                lax.psum_scatter(
                    value_part.astype(jnp.bfloat16), "dp", scatter_dimension=0, tiled=True
                ).astype(jnp.float32),
            )
            grad_k_heads.append(key_mine)
            grad_v_heads.append(value_mine)
        return jnp.concatenate(
            [
                jnp.concatenate(grad_q_heads, axis=1).astype(jnp.bfloat16),
                jnp.concatenate(grad_k_heads, axis=1).astype(jnp.bfloat16),
                jnp.concatenate(grad_v_heads, axis=1).astype(jnp.bfloat16),
            ],
            axis=1,
        )

    received = jnp.zeros((tok_rows, model_width), jnp.bfloat16)
    saved_in = jnp.zeros((micro_count, tok_rows, model_width), jnp.bfloat16)
    saved_att = jnp.zeros((micro_count, tok_rows, model_width), jnp.bfloat16)
    saved_lse = jnp.zeros((micro_count, HEADS, tok_rows), jnp.float32)
    results = jnp.zeros((micro_count, tok_rows, model_width), jnp.bfloat16)
    for tick_index in range(micro_count + 1):
        slot_raw = tick_index - section_index
        is_valid = (slot_raw >= 0) & (slot_raw < micro_count)
        slot_index = jnp.clip(slot_raw, 0, micro_count - 1)
        hidden_low = jnp.where(
            section_index == 0, block_input[min(tick_index, micro_count - 1), 0], received
        )
        hidden = hidden_low.astype(jnp.float32)
        normed, packed = project(hidden)
        masks = segments_of(slot_index)
        dense_dense_mask = masks[2]
        dense_keys_all = lax.all_gather(
            packed[:, model_width : 2 * model_width], "dp", axis=0, tiled=True
        )
        dense_values_all = lax.all_gather(packed[:, 2 * model_width :], "dp", axis=0, tiled=True)
        head_outs = []
        head_lse = []
        for dense_head_index in range(HEADS):
            dense_columns = slice(dense_head_index * head_size, (dense_head_index + 1) * head_size)
            dense_scores = jnp.where(
                dense_dense_mask,
                contract_cols(packed[:, dense_columns], dense_keys_all[:, dense_columns])
                * score_scale,
                NEG,
            )
            dense_attn_probs, lse_row = softmax_parts(dense_scores)
            head_outs.append(product(dense_attn_probs, dense_values_all[:, dense_columns]))
            head_lse.append(lse_row)
        attended = jnp.concatenate(head_outs, axis=1).astype(jnp.bfloat16)
        lse_rows = jnp.stack(head_lse)
        output = finish(hidden, attended)[4].astype(jnp.bfloat16)
        saved_in = put_row(saved_in, hidden_low, slot_index, is_valid)
        saved_att = put_row(saved_att, attended, slot_index, is_valid)
        saved_lse = put_row(saved_lse, lse_rows, slot_index, is_valid)
        results = put_row(results, output, slot_index, is_valid)
        if tick_index < micro_count:
            received = from_behind(output, "section", 1)
    totals = (
        jnp.zeros((model_width,), jnp.float32),
        jnp.zeros(w_qkv.shape, jnp.float32),
        jnp.zeros(w_out.shape, jnp.float32),
        jnp.zeros((model_width,), jnp.float32),
        jnp.zeros(w_up.shape, jnp.float32),
        jnp.zeros(w_down.shape, jnp.float32),
    )
    sent_back = jnp.zeros((tok_rows, model_width), jnp.bfloat16)
    input_grads = jnp.zeros((micro_count, tok_rows, model_width), jnp.bfloat16)
    for tick_index in range(micro_count + 1):
        slot_raw = tick_index - (1 - section_index)
        is_valid = (slot_raw >= 0) & (slot_raw < micro_count)
        slot_index = jnp.clip(slot_raw, 0, micro_count - 1)
        grad_out = jnp.where(
            section_index == 1, output_grad[min(tick_index, micro_count - 1), 0], sent_back
        )
        hidden = lax.dynamic_index_in_dim(saved_in, slot_index, 0, keepdims=False).astype(
            jnp.float32
        )
        attended = lax.dynamic_index_in_dim(saved_att, slot_index, 0, keepdims=False)
        lse_now = lax.dynamic_index_in_dim(saved_lse, slot_index, 0, keepdims=False)
        normed, packed = project(hidden)
        middle, second, pre_act, active, _ = finish(hidden, attended)
        grad_down = contract_rows(active, grad_out)
        grad_active = contract_cols(grad_out, w_down)
        gelu_back = jax.vjp(partial(jax.nn.gelu, approximate=False), pre_act)[1]
        grad_pre = gelu_back(grad_active)[0].astype(jnp.bfloat16)
        grad_up = contract_rows(second, grad_pre)
        ffn_back = jax.vjp(gained, middle, gain_ffn)[1]
        grad_mid_norm, grad_gain_ffn = ffn_back(contract_cols(grad_pre, w_up))
        grad_middle = grad_out.astype(jnp.float32) + grad_mid_norm
        grad_branch = grad_middle.astype(jnp.bfloat16)
        grad_outproj = contract_rows(attended, grad_branch)
        grad_att = contract_cols(grad_branch, w_out).astype(jnp.bfloat16)
        masks = segments_of(slot_index)
        grad_packed = dense_backward(packed, grad_att, lse_now, masks)
        grad_qkv = contract_rows(normed, grad_packed)
        attn_back = jax.vjp(gained, hidden, gain_attn)[1]
        grad_hid_norm, grad_gain_attn = attn_back(contract_cols(grad_packed, w_qkv))
        grad_hidden = (grad_middle + grad_hid_norm).astype(jnp.bfloat16)
        terms = (grad_gain_attn, grad_qkv, grad_outproj, grad_gain_ffn, grad_up, grad_down)
        totals = tuple(
            (
                running + jnp.where(is_valid, term_now, 0.0)
                for running, term_now in zip(totals, terms)
            )
        )
        input_grads = put_row(input_grads, grad_hidden, slot_index, is_valid)
        if tick_index < micro_count:
            sent_back = from_behind(grad_hidden, "section", -1)
    summed = lax.psum(
        (totals[0], totals[1], totals[2], totals[3], totals[4], totals[5]), ("dp", "rep")
    )
    return (
        results[None, :, None],
        input_grads[None, :, None],
        summed[0][None],
        summed[1][None],
        summed[2][None],
        summed[3][None],
        summed[4][None],
        summed[5][None],
    )


BF = jnp.bfloat16
F32 = jnp.float32
MIB = 1024 * 1024
GAIN_ROWS = 16


def in_hbm(array):
    return pltpu.with_memory_space_constraint(array, pltpu.HBM)


def call(body, scalars, arrays, shapes, mib=16, micros=1.0, scratch=(), held=0, out_held=(), aliases=None):
    in_specs = [pl.BlockSpec(memory_space=pltpu.SMEM)] * len(scalars)
    in_specs += [pl.BlockSpec(memory_space=pl.ANY)] * held
    in_specs += [pl.BlockSpec(memory_space=pltpu.VMEM)] * (len(arrays) - held)
    return pl.pallas_call(
        body,
        out_shape=tuple(jax.ShapeDtypeStruct(*shape) for shape in shapes),
        in_specs=in_specs,
        out_specs=tuple(
            pl.BlockSpec(memory_space=pl.ANY if index in out_held else pltpu.VMEM)
            for index in range(len(shapes))
        ),
        scratch_shapes=list(scratch),
        input_output_aliases=aliases or {},
        compiler_params=pltpu.CompilerParams(vmem_limit_bytes=mib * MIB),
        cost_estimate=pl.CostEstimate(
            flops=int(micros * 1.1e9), bytes_accessed=int(micros * 3.4e6), transcendentals=0
        ),
    )(
        *scalars,
        *(array if aliases else in_hbm(array) for array in arrays[:held]),
        *arrays[held:],
    )


def my_section():
    return lax.axis_index("section")


def my_line():
    return lax.axis_index("dp")


def my_flip(core):
    rep = lax.axis_index("rep")
    low, high = rep & 1, rep >> 1
    return 2 * low + high if core == 0 else 2 * high + low


def rows_at(start, count):
    return pl.ds(pl.multiple_of(start, count), count)


def segment_at(ends, position):
    total = jnp.zeros(position.shape, jnp.int32)
    for end in ends:
        total = total + (position >= end).astype(jnp.int32)
    return total


def ends_of(lengths):
    ends = []
    so_far = jnp.int32(0)
    for slot in range(lengths.shape[2]):
        so_far = so_far + lengths[my_line(), lax.axis_index("rep"), slot]
        ends.append(so_far)
    return ends


def write_masks(lengths, window_mask, strided_mask):
    section = my_section()
    rows, reach = window_mask.shape
    half = rows // 4
    block = 2 * half
    ends = ends_of(lengths)
    slots = len(ends)
    query_index = lax.broadcasted_iota(jnp.int32, (half, 1), 0)
    key_index = lax.broadcasted_iota(jnp.int32, (1, reach), 1)
    offset = block + query_index - key_index
    near = (offset >= 0) & (offset < STRIDE)
    for spot in range(4):
        first = block * spot + section * half
        key_pos = first - block + key_index
        query_segment = segment_at(ends, first + query_index)
        key_segment = jnp.where(key_pos >= 0, segment_at(ends, key_pos), slots)
        same = (query_segment == key_segment) & (query_segment < slots)
        window_mask[spot * half : (spot + 1) * half, :] = (same & near | (offset == 0)).astype(F32)

    def place(axis):
        shape = (rows, 1) if axis == 0 else (1, rows)
        index = lax.broadcasted_iota(jnp.int32, shape, axis)
        return block * (index // half) + section * half + (index & (half - 1))

    query_pos, key_pos = place(0), place(1)
    offset = query_pos - key_pos
    segment = segment_at(ends, query_pos)
    same = (segment == segment_at(ends, key_pos)) & (segment < slots)
    allow = same & (offset >= 0) & ((offset & (STRIDE - 1)) == 0) | (offset == 0)
    strided_mask[...] = allow.astype(F32)


def pack_kernel(tokens, grads, gain_attn, gain_ffn, lengths, *rest):
    *pieces, window_mask, strided_mask, gains, lengths_held, sems, side_sems = rest
    block = tokens.shape[2]
    half = block // 2
    rows = rows_at(my_section() * half, half)
    side = [
        pltpu.make_async_copy(lengths, lengths_held, side_sems.at[2]),
        pltpu.make_async_copy(gain_attn, gains.at[0], side_sems.at[0]),
        pltpu.make_async_copy(gain_ffn, gains.at[1], side_sems.at[1]),
    ]
    copies = []
    for step, piece in enumerate(pieces):
        micro = my_line() ^ step
        for part, source in enumerate((tokens, grads)):
            copies.append(
                pltpu.make_async_copy(
                    source.at[micro, 0, rows],
                    piece.at[part * half : (part + 1) * half],
                    sems.at[2 * step + part],
                )
            )
    for copy in (*side, *copies):
        copy.start()
    for copy in side:
        copy.wait()
    write_masks(lengths_held, window_mask, strided_mask)
    pieces[0][block:, :] = jnp.concatenate(
        [
            gains[0].astype(F32),
            gains[1].astype(F32),
            jnp.zeros((pieces[0].shape[0] - block - 2, gains.shape[2]), F32),
        ],
        axis=0,
    ).astype(BF)
    for copy in copies:
        copy.wait()


def unit(values):
    centered = values - jnp.mean(values, axis=-1, keepdims=True)
    inverse = lax.rsqrt(jnp.mean(centered * centered, axis=-1, keepdims=True) + 1e-05)
    return centered * inverse, inverse


def unit_back(grad, normal, inverse):
    return inverse * (
        grad
        - jnp.mean(grad, axis=-1, keepdims=True)
        - normal * jnp.mean(grad * normal, axis=-1, keepdims=True)
    )


def widened(column, width):
    return jnp.broadcast_to(column, (column.shape[0], width))


def normalized_exp(scores):
    shifted = jnp.exp(scores - jnp.max(scores, axis=-1, keepdims=True))
    return shifted * (1.0 / jnp.sum(shifted, axis=-1, keepdims=True))


def ffn_forward(hidden, attended, gain, w_out, w_up, w_down, saved):
    result, middle_unit, middle_inverse, second_ref, active, slope = saved
    middle = hidden + product(attended, w_out)
    normal, inverse = unit(middle)
    middle_unit[...] = normal
    middle_inverse[...] = widened(inverse, middle_inverse.shape[1])
    second = (normal * gain).astype(BF)
    second_ref[...] = second
    chunk = middle.shape[1]
    total = middle
    for index in range(w_up.shape[1] // chunk):
        columns = slice(index * chunk, (index + 1) * chunk)
        pre_act = product(second, w_up[:, columns])
        below = 0.5 + 0.5 * lax.erf(pre_act * (0.5**0.5))
        now = (pre_act * below).astype(BF)
        active[:, columns] = now
        slope[:, columns] = below + pre_act * (
            jnp.exp(-0.5 * pre_act * pre_act) * 0.3989422804014327
        )
        total = total + product(now, w_down[columns, :])
    result[...] = total.astype(BF)


def own_unit(spot, half):
    return slice((2 * spot + 2) * half, (2 * spot + 3) * half)


def key_units(spot, half):
    return slice(2 * spot * half, (2 * spot + 3) * half)


def zero_forward_kernel(
    mask,
    own0,
    own1,
    own2,
    own3,
    far0,
    far1,
    far2,
    far3,
    w_qkv,
    w_out,
    w_up,
    w_down,
    gains,
    line,
    normal_all,
    inverse_all,
    normed_all,
    query,
    padded,
    probs_ref,
    attended_ref,
    cotangent,
    *saved,
):
    section = my_section()
    reached, width = normal_all.shape
    half = line.shape[0] // 10
    block = 2 * half
    blocks = 4
    rows = blocks * half
    head = width // HEADS
    scale = float(head) ** (-0.5)
    reach = block + half
    line[:block, :] = jnp.zeros((block, width), BF)
    for step, (near, far) in enumerate(((own0, far0), (own1, far1), (own2, far2), (own3, far3))):
        spot = my_line() ^ step
        line[rows_at(spot * block + block, half), :] = near[:half, :]
        line[rows_at(spot * block + block + half - section * block, half), :] = far[:half, :]
        cotangent[rows_at(spot * half, half), :] = near[half:block, :]
    normal, inverse = unit(line[:reached, :].astype(F32))
    normal_all[...] = normal
    inverse_all[...] = widened(inverse, inverse_all.shape[1])
    normed = (normal * gains[0, 0:1, :]).astype(BF)
    normed_all[...] = normed
    padded[...] = product(normed, w_qkv[0, :, width:]).astype(BF)
    normed_mine = jnp.concatenate(
        [normed[own_unit(spot, half), :] for spot in range(blocks)], axis=0
    )
    query[...] = product(normed_mine, w_qkv[0, :, :width]).astype(BF)
    spots = [(slice(spot * half, (spot + 1) * half), key_units(spot, half)) for spot in range(blocks)]
    heads = [
        (slice(number * head, (number + 1) * head), slice(width + number * head, width + (number + 1) * head))
        for number in range(HEADS)
    ]
    scores = [
        jnp.concatenate(
            [contract_cols(query[here, columns], padded[window, columns]) for here, window in spots],
            axis=0,
        )
        for columns, _ in heads
    ]
    probs = [normalized_exp(jnp.where(mask[...] > 0.5, values * scale, NEG)) for values in scores]
    attended = []
    for number, (_, value_columns) in enumerate(heads):
        probs_ref[number] = probs[number]
        low = probs[number].astype(BF)
        attended.append(
            jnp.concatenate(
                [product(low[here, :], padded[window, value_columns]) for here, window in spots], axis=0
            )
        )
    attended = jnp.concatenate(attended, axis=1).astype(BF)
    attended_ref[...] = attended
    hidden = jnp.concatenate([line[own_unit(spot, half), :] for spot in range(blocks)], axis=0)
    ffn_forward(
        hidden.astype(F32), attended, gains[0, 1:2, :], w_out[0], w_up.at[0], w_down.at[0], saved
    )


def one_forward_kernel(
    mask,
    hidden_ref,
    w_qkv,
    w_out,
    w_up,
    w_down,
    gains,
    normal_ref,
    inverse_ref,
    normed_ref,
    packed,
    probs_ref,
    attended_ref,
    *saved,
):
    section = my_section()
    rows, width = hidden_ref.shape
    half = rows // 4
    block = 2 * half
    head = width // HEADS
    scale = float(head) ** (-0.5)
    hidden = hidden_ref[...].astype(F32)
    normal, inverse = unit(hidden)
    normal_ref[...] = normal
    inverse_ref[...] = widened(inverse, inverse_ref.shape[1])
    normed = (normal * gains[1, 0:1, :]).astype(BF)
    normed_ref[...] = normed
    packed[...] = product(normed, w_qkv[1]).astype(BF)
    heads = [
        tuple(
            slice(part * width + number * head, part * width + (number + 1) * head) for part in range(3)
        )
        for number in range(HEADS)
    ]
    scores = [contract_cols(packed[:, near], packed[:, far]) for near, far, _ in heads]
    probs = [normalized_exp(jnp.where(mask[...] > 0.5, values * scale, NEG)) for values in scores]
    parts = []
    for number, (_, _, value_columns) in enumerate(heads):
        probs_ref[number] = probs[number]
        parts.append(product(probs[number].astype(BF), packed[:, value_columns]))
    attended = jnp.concatenate(parts, axis=1).astype(BF)
    attended_ref[...] = attended
    ffn_forward(hidden, attended, gains[1, 1:2, :], w_out[1], w_up.at[1], w_down.at[1], saved)


def store_block(terms, number, value):
    width = value.shape[1]
    unit_rows = width // 2
    core, number = divmod(number, 6)
    side, flip = my_section() ^ core, my_flip(core)
    value = value.astype(BF)
    for part in range(2):
        quarter, place = divmod(2 * number + part, 3)
        terms[side, flip ^ quarter, place * unit_rows : (place + 1) * unit_rows, :] = value[
            part * unit_rows : (part + 1) * unit_rows, :
        ]


def store_gains(terms, attn_term, ffn_term):
    spare, width = terms.shape[2] - GAIN_ROWS, terms.shape[3]
    value = jnp.concatenate(
        [attn_term, ffn_term, jnp.zeros((GAIN_ROWS - 2, width), F32)], axis=0
    ).astype(BF)
    for side in range(2):
        for quarter in range(4):
            terms[side, quarter, spare:, :] = value


def ffn_input_grad(grad_out, saved, gain, w_out, w_up, w_down, grad_pre_ref):
    middle_unit, middle_inverse, slope = saved
    width = grad_out.shape[1]
    grad_second = None
    for index in range(w_up.shape[1] // width):
        columns = slice(index * width, (index + 1) * width)
        grad_active = contract_cols(grad_out, w_down[columns, :])
        grad_pre = (grad_active * slope[:, columns]).astype(BF)
        grad_pre_ref[:, columns] = grad_pre
        term = contract_cols(grad_pre, w_up[:, columns])
        grad_second = term if grad_second is None else grad_second + term
    normal = middle_unit[...]
    gain_term = jnp.sum(grad_second * normal, axis=0, keepdims=True)
    grad_middle = grad_out.astype(F32) + unit_back(
        grad_second * gain, normal, middle_inverse[:, 0:1]
    )
    return grad_middle, contract_cols(grad_middle.astype(BF), w_out).astype(BF), gain_term


def ffn_weight_grads(terms, grad_out, grad_middle, second, active, attended, grad_pre):
    width = grad_out.shape[1]
    store_block(terms, 3, contract_rows(attended[...], grad_middle.astype(BF)))
    for index in range(active.shape[1] // width):
        columns = slice(index * width, (index + 1) * width)
        store_block(terms, 4 + index, contract_rows(second[...], grad_pre[:, columns]))
        store_block(terms, 8 + index, contract_rows(active[:, columns], grad_out))


def one_backward_kernel(
    grad_ref,
    w_qkv,
    w_out,
    w_up,
    w_down,
    gains,
    normal_ref,
    inverse_ref,
    normed_ref,
    packed,
    probs_ref,
    *rest,
):
    middle_unit, middle_inverse, second, active, slope, attended, grad_in, terms, grad_pre = rest
    width = grad_ref.shape[1]
    head = width // HEADS
    scale = float(head) ** (-0.5)
    grad_out = grad_ref[...]
    grad_middle, grad_att, ffn_term = ffn_input_grad(
        grad_out,
        (middle_unit, middle_inverse, slope),
        gains[1, 1:2, :],
        w_out[1],
        w_up.at[1],
        w_down.at[1],
        grad_pre,
    )
    ffn_weight_grads(terms, grad_out, grad_middle, second, active, attended, grad_pre)
    heads = [
        tuple(
            slice(part * width + number * head, part * width + (number + 1) * head) for part in range(3)
        )
        for number in range(HEADS)
    ]
    probs = [probs_ref[number] for number in range(HEADS)]
    grad_probs = [
        contract_cols(grad_att[:, near], packed[:, value_columns]) for near, _, value_columns in heads
    ]
    grad_scores = [
        (prob * (grad - jnp.sum(prob * grad, axis=-1, keepdims=True))).astype(BF)
        for prob, grad in zip(probs, grad_probs)
    ]
    grad_parts = [
        [product(grad, packed[:, far]) * scale for grad, (_, far, _) in zip(grad_scores, heads)],
        [contract_rows(grad, packed[:, near]) * scale for grad, (near, _, _) in zip(grad_scores, heads)],
        [contract_rows(prob.astype(BF), grad_att[:, near]) for prob, (near, _, _) in zip(probs, heads)],
    ]
    grad_normed = None
    for index in range(3):
        columns = slice(index * width, (index + 1) * width)
        grad_block = jnp.concatenate(grad_parts[index], axis=1).astype(BF)
        term = contract_cols(grad_block, w_qkv[1, :, columns])
        grad_normed = term if grad_normed is None else grad_normed + term
        store_block(terms, index, contract_rows(normed_ref[...], grad_block))
    normal = normal_ref[...]
    store_gains(terms, jnp.sum(grad_normed * normal, axis=0, keepdims=True), ffn_term)
    grad_in[...] = (
        grad_middle + unit_back(grad_normed * gains[1, 0:1, :], normal, inverse_ref[:, 0:1])
    ).astype(BF)


def one_kernel(mask, hidden_ref, cotangent, *rest):
    weights, rest = rest[:5], rest[5:]
    result_one, grad_one, keep, send, *held, terms = rest
    normal, inverse, normed, packed, probs, attended = held[:6]
    middle, mid_inverse, second, active, slope, grad_pre = held[6:]
    one_forward_kernel(
        mask,
        hidden_ref,
        *weights,
        *held[:6],
        result_one,
        middle,
        mid_inverse,
        second,
        active,
        slope,
    )
    one_backward_kernel(
        cotangent,
        *weights,
        normal,
        inverse,
        normed,
        packed,
        probs,
        middle,
        mid_inverse,
        second,
        active,
        slope,
        attended,
        grad_one,
        terms,
        grad_pre,
    )
    keep[...] = terms[0]
    send[...] = terms[1]


def zero_ffn_kernel(
    grad_ref,
    w_out,
    w_up,
    w_down,
    gains,
    middle_unit,
    middle_inverse,
    slope,
    grad_middle_ref,
    grad_att_ref,
    grad_pre,
    gain_term,
):
    grad_middle, grad_att, term = ffn_input_grad(
        grad_ref[...],
        (middle_unit, middle_inverse, slope),
        gains[0, 1:2, :],
        w_out[0],
        w_up.at[0],
        w_down.at[0],
        grad_pre,
    )
    grad_middle_ref[...] = grad_middle
    grad_att_ref[...] = grad_att
    gain_term[...] = term


def zero_backward_kernel(
    grad_ref,
    w_qkv,
    gains,
    normal_all,
    inverse_all,
    normed_all,
    query,
    padded,
    probs_ref,
    result_zero,
    result_one,
    second,
    active,
    attended,
    grad_middle_ref,
    grad_att_ref,
    grad_pre,
    ffn_term,
    result_keep,
    grad_line,
    swap,
    terms,
):
    section = my_section()
    rows, width = grad_ref.shape
    reached = normal_all.shape[0]
    half = rows // 4
    blocks = 4
    head = width // HEADS
    scale = float(head) ** (-0.5)
    grad_out = grad_ref[...]

    @pl.when(section == 0)
    def _():
        result_keep[...] = result_zero[...]
        swap[:rows, :] = result_one[...]

    @pl.when(section == 1)
    def _():
        result_keep[...] = result_one[...]
        swap[:rows, :] = result_zero[...]

    grad_middle = grad_middle_ref[...]
    grad_att = grad_att_ref[...]
    ffn_weight_grads(terms, grad_out, grad_middle, second, active, attended, grad_pre)
    spots = [(slice(spot * half, (spot + 1) * half), key_units(spot, half)) for spot in range(blocks)]
    heads = [
        (slice(number * head, (number + 1) * head), slice(width + number * head, width + (number + 1) * head))
        for number in range(HEADS)
    ]
    probs = [probs_ref[number] for number in range(HEADS)]
    grad_probs = [
        jnp.concatenate(
            [
                contract_cols(grad_att[here, columns], padded[window, value_columns])
                for here, window in spots
            ],
            axis=0,
        )
        for columns, value_columns in heads
    ]
    grad_scores = [
        (prob * (grad - jnp.sum(prob * grad, axis=-1, keepdims=True))).astype(BF)
        for prob, grad in zip(probs, grad_probs)
    ]
    grad_query = [
        jnp.concatenate(
            [product(grad[here, :], padded[window, columns]) for here, window in spots], axis=0
        )
        * scale
        for grad, (columns, _) in zip(grad_scores, heads)
    ]
    grad_query = jnp.concatenate(grad_query, axis=1).astype(BF)

    def gathered(lefts, right):
        parts = []
        for left, (columns, _) in zip(lefts, heads):
            terms_of = [contract_rows(left[here, :], right[here, columns]) for here, _ in spots]
            units = []
            for index in range(reached // half):
                spot, place = divmod(index, 2)
                held = None
                if spot < blocks:
                    held = terms_of[spot][place * half : (place + 1) * half, :]
                if place == 0 and spot > 0:
                    last = terms_of[spot - 1][2 * half :, :]
                    held = last if held is None else held + last
                units.append(held)
            parts.append(jnp.concatenate(units, axis=0))
        return jnp.concatenate(parts, axis=1)

    grad_keys = (gathered(grad_scores, query) * scale).astype(BF)
    grad_values = gathered([prob.astype(BF) for prob in probs], grad_att).astype(BF)
    normed = normed_all[...]
    normed_mine = jnp.concatenate(
        [normed[own_unit(spot, half), :] for spot in range(blocks)], axis=0
    )
    store_block(terms, 0, contract_rows(normed_mine, grad_query))
    store_block(terms, 1, contract_rows(normed, grad_keys))
    store_block(terms, 2, contract_rows(normed, grad_values))
    from_query = contract_cols(grad_query, w_qkv[0, :, :width])
    grad_line[:reached, :] = contract_cols(
        grad_keys, w_qkv[0, :, width : 2 * width]
    ) + contract_cols(grad_values, w_qkv[0, :, 2 * width :])
    for spot in range(blocks):
        grad_line[own_unit(spot, half), :] += from_query[spot * half : (spot + 1) * half, :]
    grad_normed = grad_line[:reached, :]
    normal = normal_all[...]
    store_gains(terms, jnp.sum(grad_normed * normal, axis=0, keepdims=True), ffn_term[...])
    grad_line[:reached, :] = unit_back(grad_normed * gains[0, 0:1, :], normal, inverse_all[:, 0:1])
    for spot in range(blocks):
        grad_line[own_unit(spot, half), :] += grad_middle[spot * half : (spot + 1) * half, :]
    grad_line[reached:, :] = jnp.zeros((grad_line.shape[0] - reached, width), F32)

    @pl.when(section == 0)
    def _():
        swap[rows : 2 * rows, :] = grad_out

    @pl.when(section == 1)
    def _():
        swap[rows:, :] = grad_line[:reached, :].astype(BF)


def zero_both_kernel(
    grad_ref,
    w_qkv,
    w_out,
    w_up,
    w_down,
    gains,
    middle_unit,
    middle_inverse,
    slope,
    *rest,
):
    *rest, grad_middle, grad_att, grad_pre, gain_term, terms = rest
    zero_ffn_kernel(
        grad_ref,
        w_out,
        w_up,
        w_down,
        gains,
        middle_unit,
        middle_inverse,
        slope,
        grad_middle,
        grad_att,
        grad_pre,
        gain_term,
    )
    inputs, outputs, (keep, send) = rest[:-5], rest[-5:-2], rest[-2:]
    zero_backward_kernel(
        grad_ref, w_qkv, gains, *inputs, grad_middle, grad_att, grad_pre, gain_term, *outputs, terms
    )
    keep[...] = terms[0]
    send[...] = terms[1]


def share_kernel(keep, one_near, zero_near, came, *pieces):
    rows = keep.shape[0]
    half = rows // 4
    block = 2 * half
    section = my_section()
    near_rows = rows_at(section * half, half)
    far_rows = rows_at(half - section * half, half)
    for step, piece in enumerate(pieces):
        spot = my_line() ^ step
        mine = rows_at(spot * half, half)
        piece[near_rows, :] = keep[mine, :]
        piece[far_rows, :] = came[mine, :]

    @pl.when(section == 0)
    def _():
        for step, piece in enumerate(pieces):
            base = (my_line() ^ step) * block
            near, far = rows_at(base + block, block), rows_at(rows + base + half, half)
            far = pl.ds(far.start, block)
            piece[block:, :] = (zero_near[near, :] + came[far, :].astype(F32)).astype(BF)

    @pl.when(section == 1)
    def _():
        for step, piece in enumerate(pieces):
            spot = my_line() ^ step
            piece[block : block + half, :] = came[rows_at(rows + spot * half, half), :]
            piece[block + half :, :] = one_near[rows_at(spot * half, half), :]


def settle_kernel(piece0, piece1, piece2, piece3, results, input_grads):
    block = piece0.shape[0] // 2
    for step, piece in enumerate((piece0, piece1, piece2, piece3)):
        micro = my_line() ^ step
        results[0, micro, 0] = piece[:block, :]
        input_grads[0, micro, 0] = piece[block:, :]


def write_half(core, terms, targets, held, sems):
    width = terms.shape[2]
    unit_rows = width // 2
    copies = []
    for place in range(6):
        number = 6 * core + place
        for part in range(2):
            quarter, spot = divmod(2 * place + part, 3)
            value = terms[my_flip(core) ^ quarter, spot * unit_rows : (spot + 1) * unit_rows, :]
            held[place, part * unit_rows : (part + 1) * unit_rows, :] = value.astype(F32)
        which = 0 if number < 3 else 1 if number == 3 else 2 if number < 8 else 3
        first = (number, 0, number - 4, number - 8)[which] * width
        rows = pl.ds(first if which == 3 else 0, width)
        columns = pl.ds(0 if which in (1, 3) else first, width)
        copies.append(
            pltpu.make_async_copy(
                held.at[place], targets[which].at[0, rows, columns], sems.at[place]
            )
        )
        copies[-1].start()
    for copy in copies:
        copy.wait()


def by_section(body):
    for core in range(2):
        pl.when(my_section() == core)(partial(body, core))


def near_kernel(zero, one, gain_attn, qkv, out, gain_ffn, up, down, held, sems, gains, gain_sems):
    spare = zero.shape[1] - GAIN_ROWS

    def body(core):
        terms = (zero, one)[core]
        sums = terms[0, spare:, :].astype(F32)
        copies = []
        for index, target in enumerate((gain_attn, gain_ffn)):
            gains[index] = sums[index : index + 1, :]
            copies.append(pltpu.make_async_copy(gains.at[index], target, gain_sems.at[index]))
            copies[-1].start()
        write_half(core, terms, (qkv, out, up, down), held, sems)
        for copy in copies:
            copy.wait()

    by_section(body)


def far_kernel(qkv_in, out_in, up_in, down_in, zero, one, qkv, out, up, down, held, sems):
    by_section(
        lambda core: write_half(1 - core, (zero, one)[core], (qkv, out, up, down), held, sems)
    )


SWAP = [(0, 1), (1, 0)]
PLANE = ("section", "rep")


def crossed(flips):
    return [(4 * s + g, 4 * s + (g ^ flips[s])) for s in range(2) for g in range(4)]


FIRST = crossed((1, 2))
SECOND = crossed((2, 1))


def along_line(value, step):
    return lax.ppermute(value, "dp", [(z, z ^ step) for z in range(4)])


def reduce_terms(keep, came, home, steps, before, between=None):
    bar = lax.optimization_barrier
    first = lax.ppermute(keep[2:4] + came[2:4], PLANE, FIRST)
    second = lax.ppermute(keep[1] + came[1] + first[1], PLANE, SECOND)
    total = bar(keep[0] + came[0] + first[0] + second)
    total, home[before] = bar((total, home[before]))
    total = bar(total + along_line(total, steps[0]))
    if between is not None:
        total, home[between] = bar((total, home[between]))
    total = bar(total + along_line(total, steps[1]))
    pair = jnp.stack([total, lax.ppermute(total, PLANE, SECOND)])
    return pair, lax.ppermute(pair, PLANE, FIRST)


def lines(
    block_input,
    output_grad,
    seq_lengths,
    attn_gain,
    qkv_proj,
    out_proj,
    ffn_gain,
    up_proj,
    down_proj,
):
    section = lax.axis_index("section")
    micro_count, _, block, width = block_input.shape
    hidden_units = up_proj.shape[2]
    half = block // 2
    rows, reach = micro_count * half, block + half
    reached = rows + rows + half
    term_rows = 6 * width // 4 + GAIN_ROWS

    *packed, window_mask, strided_mask = call(
        pack_kernel,
        (),
        (block_input, output_grad, attn_gain, ffn_gain, seq_lengths),
        (
            ((block + 16, width), BF),
            *((((block, width), BF),) * (micro_count - 1)),
            ((rows, reach), F32),
            ((rows, rows), F32),
        ),
        8,
        scratch=(
            pltpu.VMEM((2, 1, width), BF),
            pltpu.SMEM(seq_lengths.shape, jnp.int32),
            pltpu.SemaphoreType.DMA((2 * micro_count,)),
            pltpu.SemaphoreType.DMA((3,)),
        ),
        held=5,
    )
    near = [packed[0]] + [along_line(packed[step], step) for step in range(1, micro_count)]
    far = [lax.ppermute(piece, "section", SWAP) for piece in near]
    own = (qkv_proj[0], out_proj[0], up_proj[0], down_proj[0])
    near[1], *own = lax.optimization_barrier((near[1], *own))
    swapped = [lax.ppermute(weight, "section", SWAP) for weight in own]
    weights = tuple(
        jnp.stack([jnp.where(section == 0, a, b), jnp.where(section == 0, b, a)])
        for a, b in zip(own, swapped)
    )
    gains_near, gains_far = near[0][block:].astype(F32), far[0][block:].astype(F32)
    weights += (
        jnp.stack(
            [
                jnp.where(section == 0, gains_near, gains_far),
                jnp.where(section == 0, gains_far, gains_near),
            ]
        ),
    )
    ffn_saved = (
        ((rows, width), BF),
        ((rows, width), F32),
        ((rows, 128), F32),
        ((rows, width), BF),
        ((rows, hidden_units), BF),
        ((rows, hidden_units), F32),
    )
    (
        _,
        normal_all,
        inverse_all,
        normed_all,
        query,
        padded,
        probs_zero,
        attended_zero,
        cotangent,
        result_zero,
        *saved_zero,
    ) = call(
        zero_forward_kernel,
        (),
        (window_mask, *near, *far, *weights),
        (
            ((reached + half, width), BF),
            ((reached, width), F32),
            ((reached, 128), F32),
            ((reached, width), BF),
            ((rows, width), BF),
            ((reached, 2 * width), BF),
            ((HEADS, rows, reach), F32),
            ((rows, width), BF),
            ((rows, width), BF),
            *ffn_saved,
        ),
    )
    result_one, grad_one, keep_one, send_one = call(
        one_kernel,
        (),
        (strided_mask, result_zero, cotangent, *weights),
        (((rows, width), BF), ((rows, width), BF), *(((4, term_rows, width), BF),) * 2),
        micros=4.0,
        scratch=(
            pltpu.VMEM((rows, width), F32),
            pltpu.VMEM((rows, 128), F32),
            pltpu.VMEM((rows, width), BF),
            pltpu.VMEM((rows, 3 * width), BF),
            pltpu.VMEM((HEADS, rows, rows), F32),
            pltpu.VMEM((rows, width), BF),
            *(pltpu.VMEM(*shape) for shape in ffn_saved[1:]),
            pltpu.VMEM((rows, hidden_units), BF),
            pltpu.VMEM((2, 4, term_rows, width), BF),
        ),
    )
    middle_zero, mid_inverse_zero, second_zero, active_zero, slope_zero = saved_zero
    came_one = lax.ppermute(send_one, "section", SWAP)
    result_keep, grad_line, swap, keep_zero, send_zero = call(
        zero_both_kernel,
        (),
        (
            grad_one,
            *weights,
            middle_zero,
            mid_inverse_zero,
            slope_zero,
            normal_all,
            inverse_all,
            normed_all,
            query,
            padded,
            probs_zero,
            result_zero,
            result_one,
            second_zero,
            active_zero,
            attended_zero,
        ),
        (
            ((rows, width), BF),
            ((reached + half, width), F32),
            ((rows + reached, width), BF),
            *(((4, term_rows, width), BF),) * 2,
        ),
        micros=4.0,
        scratch=(
            pltpu.VMEM((rows, width), F32),
            pltpu.VMEM((rows, width), BF),
            pltpu.VMEM((rows, hidden_units), BF),
            pltpu.VMEM((1, width), F32),
            pltpu.VMEM((2, 4, term_rows, width), BF),
        ),
    )
    came = lax.ppermute(swap, "section", SWAP)
    shared = call(
        share_kernel,
        (),
        (result_keep, grad_one, grad_line, came),
        (((2 * block, width), BF),) * micro_count,
        8,
    )
    home = [shared[0]] + [along_line(shared[step], step) for step in range(1, micro_count)]
    came_zero = lax.ppermute(send_zero, "section", SWAP)
    one_pair, one_first = reduce_terms(keep_one, came_one, home, (2, 1), 3, 2)
    zero_pair, zero_first = reduce_terms(keep_zero, came_zero, home, (1, 2), 1)
    results, input_grads = call(
        settle_kernel,
        (),
        home,
        (((1, micro_count, 1, block, width), BF),) * 2,
        8,
    )

    def both_cores(parts):
        near = jnp.concatenate(parts)
        return near, jnp.concatenate([lax.ppermute(part, "section", SWAP) for part in parts])

    zero_near, zero_far = both_cores((zero_pair, zero_first))
    one_near, one_far = both_cores((one_pair, one_first))
    sums = (
        ((1, width, 3 * width), F32),
        ((1, width, width), F32),
        ((1, width, hidden_units), F32),
        ((1, hidden_units, width), F32),
    )
    held = (pltpu.VMEM((6, width, width), F32), pltpu.SemaphoreType.DMA((6,)))
    gain_attn_sum, qkv_half, out_half, gain_ffn_sum, up_half, down_half = call(
        near_kernel,
        (),
        (zero_near, one_near),
        (((1, width), F32), *sums[:2], ((1, width), F32), *sums[2:]),
        16,
        scratch=(*held, pltpu.VMEM((2, 1, width), F32), pltpu.SemaphoreType.DMA((2,))),
        out_held=(0, 1, 2, 3, 4, 5),
    )
    qkv_sum, out_sum, up_sum, down_sum = call(
        far_kernel,
        (),
        (qkv_half, out_half, up_half, down_half, zero_far, one_far),
        sums,
        16,
        scratch=held,
        held=4,
        out_held=(0, 1, 2, 3),
        aliases={0: 0, 1: 1, 2: 2, 3: 3},
    )
    return (
        results,
        input_grads,
        gain_attn_sum,
        qkv_sum,
        out_sum,
        gain_ffn_sum,
        up_sum,
        down_sum,
    )


def local(*arrays):
    micro_count, _, tok_rows, model_width = arrays[0].shape
    one_line_per_chip = (
        lax.axis_size("section") == 2
        and lax.axis_size("dp") == 4
        and lax.axis_size("rep") == 4
        and micro_count == 4
        and tok_rows == STRIDE
        and model_width == 256
        and arrays[7].shape[2] == 4 * model_width
    )
    return lines(*arrays) if one_line_per_chip else general(*arrays)


def solution(mesh):
    placed = (
        P(None, "rep", "dp", None),
        P(None, "rep", "dp", None),
        P(),
        P("section", None),
        P("section", None, None),
        P("section", None, None),
        P("section", None),
        P("section", None, None),
        P("section", None, None),
    )
    return jax.shard_map(
        local,
        mesh=mesh,
        in_specs=placed,
        out_specs=(
            P("section", None, "rep", "dp", None),
            P("section", None, "rep", "dp", None),
            P("section", None),
            P("section", None, None),
            P("section", None, None),
            P("section", None),
            P("section", None, None),
            P("section", None, None),
        ),
        check_vma=False,
    )
```

```python
from functools import partial

import jax
import jax.numpy as jnp
from jax import lax
from jax.experimental import pallas as pl
from jax.experimental.pallas import tpu as pltpu
from jax.sharding import PartitionSpec as P

HEADS = 2
STRIDE = 128


NEG = -1e30


def from_behind(shard, axis, by):
    length = lax.axis_size(axis)
    pairs = [(i, i + by) for i in range(length) if 0 <= i + by < length]
    return lax.ppermute(shard, axis, pairs)


def normalize(values):
    centered = values - jnp.mean(values, axis=-1, keepdims=True)
    spread = jnp.mean(centered * centered, axis=-1, keepdims=True)
    return centered * lax.rsqrt(spread + 1e-05)


def gained(values, gain):
    return normalize(values) * gain


def allowed(query_pos, query_seg, key_pos, key_seg, strided, seq_slots):
    offset = query_pos - key_pos
    same_seq = (query_seg == key_seg) & (query_seg < seq_slots)
    nearby = (offset >= 0) & (offset < STRIDE)
    spaced = (offset >= 0) & (offset % STRIDE == 0)
    pattern = jnp.where(strided, spaced, nearby)
    return same_seq & pattern | (offset == 0)


def product(left, right):
    return jnp.dot(left, right, preferred_element_type=jnp.float32)


def contract_rows(left, right):
    return lax.dot_general(
        left, right, (((0,), (0,)), ((), ())), preferred_element_type=jnp.float32
    )


def contract_cols(left, right):
    return lax.dot_general(
        left, right, (((1,), (1,)), ((), ())), preferred_element_type=jnp.float32
    )


def put_row(buffer, value, slot_index, is_valid):
    current = lax.dynamic_index_in_dim(buffer, slot_index, 0, keepdims=False)
    return lax.dynamic_update_index_in_dim(
        buffer, jnp.where(is_valid, value, current), slot_index, 0
    )


def softmax_parts(scores):
    row_max = jnp.max(scores, axis=-1, keepdims=True)
    shifted = jnp.exp(scores - row_max)
    row_total = jnp.sum(shifted, axis=-1, keepdims=True)
    return ((shifted / row_total).astype(jnp.bfloat16), (row_max + jnp.log(row_total))[..., 0])


def general(
    block_input,
    output_grad,
    seq_lengths,
    attn_gain,
    qkv_proj,
    out_proj,
    ffn_gain,
    up_proj,
    down_proj,
):
    section_index = lax.axis_index("section")
    line_row = lax.axis_index("dp")
    group_index = lax.axis_index("rep")
    strided = section_index == 1
    micro_count, _, tok_rows, model_width = block_input.shape
    line_count = lax.axis_size("dp")
    line_span = tok_rows * line_count
    head_size = model_width // HEADS
    score_scale = float(head_size) ** (-0.5)
    seq_slots = seq_lengths.shape[-1]
    block_count = line_span // STRIDE
    residues = STRIDE // line_count
    line_lengths = lax.dynamic_index_in_dim(seq_lengths, group_index, 1, keepdims=False)
    all_pos = jnp.arange(line_span, dtype=jnp.int32)
    my_pos = line_row * tok_rows + jnp.arange(tok_rows, dtype=jnp.int32)
    win_pos = line_row * tok_rows - tok_rows + jnp.arange(2 * tok_rows, dtype=jnp.int32)
    res_pos = (
        jnp.arange(block_count, dtype=jnp.int32)[None, :] * STRIDE
        + line_row * residues
        + jnp.arange(residues, dtype=jnp.int32)[:, None]
    )
    gain_attn = attn_gain[0].astype(jnp.float32)
    gain_ffn = ffn_gain[0].astype(jnp.float32)
    w_qkv = qkv_proj[0]
    w_out = out_proj[0]
    w_up = up_proj[0]
    w_down = down_proj[0]

    def segments_of(slot_index):
        seq_ends = jnp.cumsum(lax.dynamic_index_in_dim(line_lengths, slot_index, 0, keepdims=False))
        all_seg = jnp.sum((all_pos[:, None] >= seq_ends[None, :]).astype(jnp.int32), axis=1)
        my_seg = lax.dynamic_slice_in_dim(all_seg, line_row * tok_rows, tok_rows)
        padded = jnp.concatenate([jnp.full((tok_rows,), seq_slots, jnp.int32), all_seg])
        win_seg = lax.dynamic_slice_in_dim(padded, line_row * tok_rows, 2 * tok_rows)
        res_seg = lax.dynamic_slice_in_dim(
            all_seg.reshape(block_count, STRIDE), line_row * residues, residues, 1
        ).T
        dense_mask = allowed(
            my_pos[:, None], my_seg[:, None], all_pos[None, :], all_seg[None, :], strided, seq_slots
        )
        win_mask = allowed(
            my_pos[:, None], my_seg[:, None], win_pos[None, :], win_seg[None, :], False, seq_slots
        )
        res_mask = allowed(
            res_pos[:, :, None],
            res_seg[:, :, None],
            res_pos[:, None, :],
            res_seg[:, None, :],
            True,
            seq_slots,
        )
        return (all_seg, my_seg, dense_mask, win_mask, res_mask)

    def project(hidden):
        normed = gained(hidden, gain_attn).astype(jnp.bfloat16)
        packed = product(normed, w_qkv).astype(jnp.bfloat16)
        return (normed, packed)

    def finish(hidden, attended):
        middle = hidden + product(attended, w_out)
        second = gained(middle, gain_ffn).astype(jnp.bfloat16)
        pre_act = product(second, w_up)
        active = jax.nn.gelu(pre_act, approximate=False).astype(jnp.bfloat16)
        return (middle, second, pre_act, active, middle + product(active, w_down))

    def dense_backward(packed, grad_att, lse_now, masks):
        all_seg, my_seg, dense_mask = (masks[0], masks[1], masks[2])
        queries = packed[:, :model_width]
        key_rows = packed[:, model_width : 2 * model_width]
        values = packed[:, 2 * model_width :]
        keys_all, values_all = (
            lax.all_gather(key_rows, "dp", axis=0, tiled=True),
            lax.all_gather(values, "dp", axis=0, tiled=True),
        )
        grad_q_heads = []
        grad_k_heads = []
        grad_v_heads = []
        delta_heads = []
        for head_index in range(HEADS):
            columns = slice(head_index * head_size, (head_index + 1) * head_size)
            query_head = queries[:, columns]
            out_head = grad_att[:, columns]
            scores = jnp.where(
                dense_mask, contract_cols(query_head, keys_all[:, columns]) * score_scale, NEG
            )
            attn_probs = jnp.exp(scores - lse_now[head_index][:, None])
            grad_probs = contract_cols(out_head, values_all[:, columns])
            delta_row = jnp.sum(attn_probs * grad_probs, axis=1)
            grad_scores = (attn_probs * (grad_probs - delta_row[:, None])).astype(jnp.bfloat16)
            grad_q_heads.append(product(grad_scores, keys_all[:, columns]) * score_scale)
            delta_heads.append(delta_row)
            key_part = contract_rows(grad_scores, query_head) * score_scale
            value_part = contract_rows(attn_probs.astype(jnp.bfloat16), out_head)
            key_mine, value_mine = (
                lax.psum_scatter(
                    key_part.astype(jnp.bfloat16), "dp", scatter_dimension=0, tiled=True
                ).astype(jnp.float32),
                lax.psum_scatter(
                    value_part.astype(jnp.bfloat16), "dp", scatter_dimension=0, tiled=True
                ).astype(jnp.float32),
            )
            grad_k_heads.append(key_mine)
            grad_v_heads.append(value_mine)
        return jnp.concatenate(
            [
                jnp.concatenate(grad_q_heads, axis=1).astype(jnp.bfloat16),
                jnp.concatenate(grad_k_heads, axis=1).astype(jnp.bfloat16),
                jnp.concatenate(grad_v_heads, axis=1).astype(jnp.bfloat16),
            ],
            axis=1,
        )

    received = jnp.zeros((tok_rows, model_width), jnp.bfloat16)
    saved_in = jnp.zeros((micro_count, tok_rows, model_width), jnp.bfloat16)
    saved_att = jnp.zeros((micro_count, tok_rows, model_width), jnp.bfloat16)
    saved_lse = jnp.zeros((micro_count, HEADS, tok_rows), jnp.float32)
    results = jnp.zeros((micro_count, tok_rows, model_width), jnp.bfloat16)
    for tick_index in range(micro_count + 1):
        slot_raw = tick_index - section_index
        is_valid = (slot_raw >= 0) & (slot_raw < micro_count)
        slot_index = jnp.clip(slot_raw, 0, micro_count - 1)
        hidden_low = jnp.where(
            section_index == 0, block_input[min(tick_index, micro_count - 1), 0], received
        )
        hidden = hidden_low.astype(jnp.float32)
        normed, packed = project(hidden)
        masks = segments_of(slot_index)
        dense_dense_mask = masks[2]
        dense_keys_all = lax.all_gather(
            packed[:, model_width : 2 * model_width], "dp", axis=0, tiled=True
        )
        dense_values_all = lax.all_gather(packed[:, 2 * model_width :], "dp", axis=0, tiled=True)
        head_outs = []
        head_lse = []
        for dense_head_index in range(HEADS):
            dense_columns = slice(dense_head_index * head_size, (dense_head_index + 1) * head_size)
            dense_scores = jnp.where(
                dense_dense_mask,
                contract_cols(packed[:, dense_columns], dense_keys_all[:, dense_columns])
                * score_scale,
                NEG,
            )
            dense_attn_probs, lse_row = softmax_parts(dense_scores)
            head_outs.append(product(dense_attn_probs, dense_values_all[:, dense_columns]))
            head_lse.append(lse_row)
        attended = jnp.concatenate(head_outs, axis=1).astype(jnp.bfloat16)
        lse_rows = jnp.stack(head_lse)
        output = finish(hidden, attended)[4].astype(jnp.bfloat16)
        saved_in = put_row(saved_in, hidden_low, slot_index, is_valid)
        saved_att = put_row(saved_att, attended, slot_index, is_valid)
        saved_lse = put_row(saved_lse, lse_rows, slot_index, is_valid)
        results = put_row(results, output, slot_index, is_valid)
        if tick_index < micro_count:
            received = from_behind(output, "section", 1)
    totals = (
        jnp.zeros((model_width,), jnp.float32),
        jnp.zeros(w_qkv.shape, jnp.float32),
        jnp.zeros(w_out.shape, jnp.float32),
        jnp.zeros((model_width,), jnp.float32),
        jnp.zeros(w_up.shape, jnp.float32),
        jnp.zeros(w_down.shape, jnp.float32),
    )
    sent_back = jnp.zeros((tok_rows, model_width), jnp.bfloat16)
    input_grads = jnp.zeros((micro_count, tok_rows, model_width), jnp.bfloat16)
    for tick_index in range(micro_count + 1):
        slot_raw = tick_index - (1 - section_index)
        is_valid = (slot_raw >= 0) & (slot_raw < micro_count)
        slot_index = jnp.clip(slot_raw, 0, micro_count - 1)
        grad_out = jnp.where(
            section_index == 1, output_grad[min(tick_index, micro_count - 1), 0], sent_back
        )
        hidden = lax.dynamic_index_in_dim(saved_in, slot_index, 0, keepdims=False).astype(
            jnp.float32
        )
        attended = lax.dynamic_index_in_dim(saved_att, slot_index, 0, keepdims=False)
        lse_now = lax.dynamic_index_in_dim(saved_lse, slot_index, 0, keepdims=False)
        normed, packed = project(hidden)
        middle, second, pre_act, active, _ = finish(hidden, attended)
        grad_down = contract_rows(active, grad_out)
        grad_active = contract_cols(grad_out, w_down)
        gelu_back = jax.vjp(partial(jax.nn.gelu, approximate=False), pre_act)[1]
        grad_pre = gelu_back(grad_active)[0].astype(jnp.bfloat16)
        grad_up = contract_rows(second, grad_pre)
        ffn_back = jax.vjp(gained, middle, gain_ffn)[1]
        grad_mid_norm, grad_gain_ffn = ffn_back(contract_cols(grad_pre, w_up))
        grad_middle = grad_out.astype(jnp.float32) + grad_mid_norm
        grad_branch = grad_middle.astype(jnp.bfloat16)
        grad_outproj = contract_rows(attended, grad_branch)
        grad_att = contract_cols(grad_branch, w_out).astype(jnp.bfloat16)
        masks = segments_of(slot_index)
        grad_packed = dense_backward(packed, grad_att, lse_now, masks)
        grad_qkv = contract_rows(normed, grad_packed)
        attn_back = jax.vjp(gained, hidden, gain_attn)[1]
        grad_hid_norm, grad_gain_attn = attn_back(contract_cols(grad_packed, w_qkv))
        grad_hidden = (grad_middle + grad_hid_norm).astype(jnp.bfloat16)
        terms = (grad_gain_attn, grad_qkv, grad_outproj, grad_gain_ffn, grad_up, grad_down)
        totals = tuple(
            (
                running + jnp.where(is_valid, term_now, 0.0)
                for running, term_now in zip(totals, terms)
            )
        )
        input_grads = put_row(input_grads, grad_hidden, slot_index, is_valid)
        if tick_index < micro_count:
            sent_back = from_behind(grad_hidden, "section", -1)
    summed = lax.psum(
        (totals[0], totals[1], totals[2], totals[3], totals[4], totals[5]), ("dp", "rep")
    )
    return (
        results[None, :, None],
        input_grads[None, :, None],
        summed[0][None],
        summed[1][None],
        summed[2][None],
        summed[3][None],
        summed[4][None],
        summed[5][None],
    )


BF = jnp.bfloat16
F32 = jnp.float32
MIB = 1024 * 1024
GAIN_ROWS = 16


def in_hbm(array):
    return pltpu.with_memory_space_constraint(array, pltpu.HBM)


def call(body, scalars, arrays, shapes, mib=16, micros=1.0, scratch=(), held=0, out_held=(), aliases=None):
    in_specs = [pl.BlockSpec(memory_space=pltpu.SMEM)] * len(scalars)
    in_specs += [pl.BlockSpec(memory_space=pl.ANY)] * held
    in_specs += [pl.BlockSpec(memory_space=pltpu.VMEM)] * (len(arrays) - held)
    return pl.pallas_call(
        body,
        out_shape=tuple(jax.ShapeDtypeStruct(*shape) for shape in shapes),
        in_specs=in_specs,
        out_specs=tuple(
            pl.BlockSpec(memory_space=pl.ANY if index in out_held else pltpu.VMEM)
            for index in range(len(shapes))
        ),
        scratch_shapes=list(scratch),
        input_output_aliases=aliases or {},
        compiler_params=pltpu.CompilerParams(vmem_limit_bytes=mib * MIB),
        cost_estimate=pl.CostEstimate(
            flops=int(micros * 1.1e9), bytes_accessed=int(micros * 3.4e6), transcendentals=0
        ),
    )(
        *scalars,
        *(array if aliases else in_hbm(array) for array in arrays[:held]),
        *arrays[held:],
    )


def my_section():
    return lax.axis_index("section")


def my_line():
    return lax.axis_index("dp")


def my_flip(core):
    rep = lax.axis_index("rep")
    low, high = rep & 1, rep >> 1
    return 2 * low + high if core == 0 else 2 * high + low


def rows_at(start, count):
    return pl.ds(pl.multiple_of(start, count), count)


def segment_at(ends, position):
    total = jnp.zeros(position.shape, jnp.int32)
    for end in ends:
        total = total + (position >= end).astype(jnp.int32)
    return total


def ends_of(lengths):
    ends = []
    so_far = jnp.int32(0)
    for slot in range(lengths.shape[2]):
        so_far = so_far + lengths[my_line(), lax.axis_index("rep"), slot]
        ends.append(so_far)
    return ends


def write_masks(lengths, window_mask, strided_mask):
    section = my_section()
    rows, reach = window_mask.shape
    half = rows // 4
    block = 2 * half
    ends = ends_of(lengths)
    slots = len(ends)
    query_index = lax.broadcasted_iota(jnp.int32, (half, 1), 0)
    key_index = lax.broadcasted_iota(jnp.int32, (1, reach), 1)
    offset = block + query_index - key_index
    near = (offset >= 0) & (offset < STRIDE)
    for spot in range(4):
        first = block * spot + section * half
        key_pos = first - block + key_index
        query_segment = segment_at(ends, first + query_index)
        key_segment = jnp.where(key_pos >= 0, segment_at(ends, key_pos), slots)
        same = (query_segment == key_segment) & (query_segment < slots)
        window_mask[spot * half : (spot + 1) * half, :] = (same & near | (offset == 0)).astype(F32)

    def place(axis):
        shape = (rows, 1) if axis == 0 else (1, rows)
        index = lax.broadcasted_iota(jnp.int32, shape, axis)
        return block * (index // half) + section * half + (index & (half - 1))

    query_pos, key_pos = place(0), place(1)
    offset = query_pos - key_pos
    segment = segment_at(ends, query_pos)
    same = (segment == segment_at(ends, key_pos)) & (segment < slots)
    allow = same & (offset >= 0) & ((offset & (STRIDE - 1)) == 0) | (offset == 0)
    strided_mask[...] = allow.astype(F32)


def pack_kernel(tokens, grads, gain_attn, gain_ffn, lengths, *rest):
    *pieces, window_mask, strided_mask, gains, lengths_held, sems, side_sems = rest
    block = tokens.shape[2]
    half = block // 2
    rows = rows_at(my_section() * half, half)
    side = [
        pltpu.make_async_copy(lengths, lengths_held, side_sems.at[2]),
        pltpu.make_async_copy(gain_attn, gains.at[0], side_sems.at[0]),
        pltpu.make_async_copy(gain_ffn, gains.at[1], side_sems.at[1]),
    ]
    copies = []
    for step, piece in enumerate(pieces):
        micro = my_line() ^ step
        for part, source in enumerate((tokens, grads)):
            copies.append(
                pltpu.make_async_copy(
                    source.at[micro, 0, rows],
                    piece.at[part * half : (part + 1) * half],
                    sems.at[2 * step + part],
                )
            )
    for copy in (*side, *copies):
        copy.start()
    for copy in side:
        copy.wait()
    write_masks(lengths_held, window_mask, strided_mask)
    pieces[0][block:, :] = jnp.concatenate(
        [
            gains[0].astype(F32),
            gains[1].astype(F32),
            jnp.zeros((pieces[0].shape[0] - block - 2, gains.shape[2]), F32),
        ],
        axis=0,
    ).astype(BF)
    for copy in copies:
        copy.wait()


def unit(values):
    centered = values - jnp.mean(values, axis=-1, keepdims=True)
    inverse = lax.rsqrt(jnp.mean(centered * centered, axis=-1, keepdims=True) + 1e-05)
    return centered * inverse, inverse


def unit_back(grad, normal, inverse):
    return inverse * (
        grad
        - jnp.mean(grad, axis=-1, keepdims=True)
        - normal * jnp.mean(grad * normal, axis=-1, keepdims=True)
    )


def widened(column, width):
    return jnp.broadcast_to(column, (column.shape[0], width))


def normalized_exp(scores):
    shifted = jnp.exp(scores - jnp.max(scores, axis=-1, keepdims=True))
    return shifted * (1.0 / jnp.sum(shifted, axis=-1, keepdims=True))


def ffn_forward(hidden, attended, gain, w_out, w_up, w_down, saved):
    result, middle_unit, middle_inverse, second_ref, active, slope = saved
    middle = hidden + product(attended, w_out)
    normal, inverse = unit(middle)
    middle_unit[...] = normal
    middle_inverse[...] = widened(inverse, middle_inverse.shape[1])
    second = (normal * gain).astype(BF)
    second_ref[...] = second
    chunk = middle.shape[1]
    total = middle
    for index in range(w_up.shape[1] // chunk):
        columns = slice(index * chunk, (index + 1) * chunk)
        pre_act = product(second, w_up[:, columns])
        below = 0.5 + 0.5 * lax.erf(pre_act * (0.5**0.5))
        now = (pre_act * below).astype(BF)
        active[:, columns] = now
        slope[:, columns] = below + pre_act * (
            jnp.exp(-0.5 * pre_act * pre_act) * 0.3989422804014327
        )
        total = total + product(now, w_down[columns, :])
    result[...] = total.astype(BF)


def own_unit(spot, half):
    return slice((2 * spot + 2) * half, (2 * spot + 3) * half)


def key_units(spot, half):
    return slice(2 * spot * half, (2 * spot + 3) * half)


def zero_forward_kernel(
    mask,
    own0,
    own1,
    own2,
    own3,
    far0,
    far1,
    far2,
    far3,
    w_qkv,
    w_out,
    w_up,
    w_down,
    gains,
    line,
    normal_all,
    inverse_all,
    normed_all,
    query,
    padded,
    probs_ref,
    attended_ref,
    cotangent,
    *saved,
):
    section = my_section()
    reached, width = normal_all.shape
    half = line.shape[0] // 10
    block = 2 * half
    blocks = 4
    rows = blocks * half
    head = width // HEADS
    scale = float(head) ** (-0.5)
    reach = block + half
    line[:block, :] = jnp.zeros((block, width), BF)
    for step, (near, far) in enumerate(((own0, far0), (own1, far1), (own2, far2), (own3, far3))):
        spot = my_line() ^ step
        line[rows_at(spot * block + block, half), :] = near[:half, :]
        line[rows_at(spot * block + block + half - section * block, half), :] = far[:half, :]
        cotangent[rows_at(spot * half, half), :] = near[half:block, :]
    normal, inverse = unit(line[:reached, :].astype(F32))
    normal_all[...] = normal
    inverse_all[...] = widened(inverse, inverse_all.shape[1])
    normed = (normal * gains[0, 0:1, :]).astype(BF)
    normed_all[...] = normed
    padded[...] = product(normed, w_qkv[0, :, width:]).astype(BF)
    normed_mine = jnp.concatenate(
        [normed[own_unit(spot, half), :] for spot in range(blocks)], axis=0
    )
    query[...] = product(normed_mine, w_qkv[0, :, :width]).astype(BF)
    spots = [(slice(spot * half, (spot + 1) * half), key_units(spot, half)) for spot in range(blocks)]
    heads = [
        (slice(number * head, (number + 1) * head), slice(width + number * head, width + (number + 1) * head))
        for number in range(HEADS)
    ]
    scores = [
        jnp.concatenate(
            [contract_cols(query[here, columns], padded[window, columns]) for here, window in spots],
            axis=0,
        )
        for columns, _ in heads
    ]
    probs = [normalized_exp(jnp.where(mask[...] > 0.5, values * scale, NEG)) for values in scores]
    attended = []
    for number, (_, value_columns) in enumerate(heads):
        probs_ref[number] = probs[number]
        low = probs[number].astype(BF)
        attended.append(
            jnp.concatenate(
                [product(low[here, :], padded[window, value_columns]) for here, window in spots], axis=0
            )
        )
    attended = jnp.concatenate(attended, axis=1).astype(BF)
    attended_ref[...] = attended
    hidden = jnp.concatenate([line[own_unit(spot, half), :] for spot in range(blocks)], axis=0)
    ffn_forward(
        hidden.astype(F32), attended, gains[0, 1:2, :], w_out[0], w_up.at[0], w_down.at[0], saved
    )


def one_forward_kernel(
    mask,
    hidden_ref,
    w_qkv,
    w_out,
    w_up,
    w_down,
    gains,
    normal_ref,
    inverse_ref,
    normed_ref,
    packed,
    probs_ref,
    attended_ref,
    *saved,
):
    section = my_section()
    rows, width = hidden_ref.shape
    half = rows // 4
    block = 2 * half
    head = width // HEADS
    scale = float(head) ** (-0.5)
    hidden = hidden_ref[...].astype(F32)
    normal, inverse = unit(hidden)
    normal_ref[...] = normal
    inverse_ref[...] = widened(inverse, inverse_ref.shape[1])
    normed = (normal * gains[1, 0:1, :]).astype(BF)
    normed_ref[...] = normed
    packed[...] = product(normed, w_qkv[1]).astype(BF)
    heads = [
        tuple(
            slice(part * width + number * head, part * width + (number + 1) * head) for part in range(3)
        )
        for number in range(HEADS)
    ]
    scores = [contract_cols(packed[:, near], packed[:, far]) for near, far, _ in heads]
    probs = [normalized_exp(jnp.where(mask[...] > 0.5, values * scale, NEG)) for values in scores]
    parts = []
    for number, (_, _, value_columns) in enumerate(heads):
        probs_ref[number] = probs[number]
        parts.append(product(probs[number].astype(BF), packed[:, value_columns]))
    attended = jnp.concatenate(parts, axis=1).astype(BF)
    attended_ref[...] = attended
    ffn_forward(hidden, attended, gains[1, 1:2, :], w_out[1], w_up.at[1], w_down.at[1], saved)


def store_block(terms, number, value):
    width = value.shape[1]
    unit_rows = width // 2
    core, number = divmod(number, 6)
    side, flip = my_section() ^ core, my_flip(core)
    value = value.astype(BF)
    for part in range(2):
        quarter, place = divmod(2 * number + part, 3)
        terms[side, flip ^ quarter, place * unit_rows : (place + 1) * unit_rows, :] = value[
            part * unit_rows : (part + 1) * unit_rows, :
        ]


def store_gains(terms, attn_term, ffn_term):
    spare, width = terms.shape[2] - GAIN_ROWS, terms.shape[3]
    value = jnp.concatenate(
        [attn_term, ffn_term, jnp.zeros((GAIN_ROWS - 2, width), F32)], axis=0
    ).astype(BF)
    for side in range(2):
        for quarter in range(4):
            terms[side, quarter, spare:, :] = value


def ffn_input_grad(grad_out, saved, gain, w_out, w_up, w_down, grad_pre_ref):
    middle_unit, middle_inverse, slope = saved
    width = grad_out.shape[1]
    grad_second = None
    for index in range(w_up.shape[1] // width):
        columns = slice(index * width, (index + 1) * width)
        grad_active = contract_cols(grad_out, w_down[columns, :])
        grad_pre = (grad_active * slope[:, columns]).astype(BF)
        grad_pre_ref[:, columns] = grad_pre
        term = contract_cols(grad_pre, w_up[:, columns])
        grad_second = term if grad_second is None else grad_second + term
    normal = middle_unit[...]
    gain_term = jnp.sum(grad_second * normal, axis=0, keepdims=True)
    grad_middle = grad_out.astype(F32) + unit_back(
        grad_second * gain, normal, middle_inverse[:, 0:1]
    )
    return grad_middle, contract_cols(grad_middle.astype(BF), w_out).astype(BF), gain_term


def ffn_weight_grads(terms, grad_out, grad_middle, second, active, attended, grad_pre):
    width = grad_out.shape[1]
    store_block(terms, 3, contract_rows(attended[...], grad_middle.astype(BF)))
    for index in range(active.shape[1] // width):
        columns = slice(index * width, (index + 1) * width)
        store_block(terms, 4 + index, contract_rows(second[...], grad_pre[:, columns]))
        store_block(terms, 8 + index, contract_rows(active[:, columns], grad_out))


def one_backward_kernel(
    grad_ref,
    w_qkv,
    w_out,
    w_up,
    w_down,
    gains,
    normal_ref,
    inverse_ref,
    normed_ref,
    packed,
    probs_ref,
    *rest,
):
    middle_unit, middle_inverse, second, active, slope, attended, grad_in, terms, grad_pre = rest
    width = grad_ref.shape[1]
    head = width // HEADS
    scale = float(head) ** (-0.5)
    grad_out = grad_ref[...]
    grad_middle, grad_att, ffn_term = ffn_input_grad(
        grad_out,
        (middle_unit, middle_inverse, slope),
        gains[1, 1:2, :],
        w_out[1],
        w_up.at[1],
        w_down.at[1],
        grad_pre,
    )
    ffn_weight_grads(terms, grad_out, grad_middle, second, active, attended, grad_pre)
    heads = [
        tuple(
            slice(part * width + number * head, part * width + (number + 1) * head) for part in range(3)
        )
        for number in range(HEADS)
    ]
    probs = [probs_ref[number] for number in range(HEADS)]
    grad_probs = [
        contract_cols(grad_att[:, near], packed[:, value_columns]) for near, _, value_columns in heads
    ]
    grad_scores = [
        (prob * (grad - jnp.sum(prob * grad, axis=-1, keepdims=True))).astype(BF)
        for prob, grad in zip(probs, grad_probs)
    ]
    grad_parts = [
        [product(grad, packed[:, far]) * scale for grad, (_, far, _) in zip(grad_scores, heads)],
        [contract_rows(grad, packed[:, near]) * scale for grad, (near, _, _) in zip(grad_scores, heads)],
        [contract_rows(prob.astype(BF), grad_att[:, near]) for prob, (near, _, _) in zip(probs, heads)],
    ]
    grad_normed = None
    for index in range(3):
        columns = slice(index * width, (index + 1) * width)
        grad_block = jnp.concatenate(grad_parts[index], axis=1).astype(BF)
        term = contract_cols(grad_block, w_qkv[1, :, columns])
        grad_normed = term if grad_normed is None else grad_normed + term
        store_block(terms, index, contract_rows(normed_ref[...], grad_block))
    normal = normal_ref[...]
    store_gains(terms, jnp.sum(grad_normed * normal, axis=0, keepdims=True), ffn_term)
    grad_in[...] = (
        grad_middle + unit_back(grad_normed * gains[1, 0:1, :], normal, inverse_ref[:, 0:1])
    ).astype(BF)


def one_kernel(mask, hidden_ref, cotangent, *rest):
    weights, rest = rest[:5], rest[5:]
    result_one, grad_one, keep, send, *held, terms = rest
    normal, inverse, normed, packed, probs, attended = held[:6]
    middle, mid_inverse, second, active, slope, grad_pre = held[6:]
    one_forward_kernel(
        mask,
        hidden_ref,
        *weights,
        *held[:6],
        result_one,
        middle,
        mid_inverse,
        second,
        active,
        slope,
    )
    one_backward_kernel(
        cotangent,
        *weights,
        normal,
        inverse,
        normed,
        packed,
        probs,
        middle,
        mid_inverse,
        second,
        active,
        slope,
        attended,
        grad_one,
        terms,
        grad_pre,
    )
    keep[...] = terms[0]
    send[...] = terms[1]


def zero_ffn_kernel(
    grad_ref,
    w_out,
    w_up,
    w_down,
    gains,
    middle_unit,
    middle_inverse,
    slope,
    grad_middle_ref,
    grad_att_ref,
    grad_pre,
    gain_term,
):
    grad_middle, grad_att, term = ffn_input_grad(
        grad_ref[...],
        (middle_unit, middle_inverse, slope),
        gains[0, 1:2, :],
        w_out[0],
        w_up.at[0],
        w_down.at[0],
        grad_pre,
    )
    grad_middle_ref[...] = grad_middle
    grad_att_ref[...] = grad_att
    gain_term[...] = term


def zero_backward_kernel(
    grad_ref,
    w_qkv,
    gains,
    normal_all,
    inverse_all,
    normed_all,
    query,
    padded,
    probs_ref,
    result_zero,
    result_one,
    second,
    active,
    attended,
    grad_middle_ref,
    grad_att_ref,
    grad_pre,
    ffn_term,
    result_keep,
    grad_line,
    swap,
    terms,
):
    section = my_section()
    rows, width = grad_ref.shape
    reached = normal_all.shape[0]
    half = rows // 4
    blocks = 4
    head = width // HEADS
    scale = float(head) ** (-0.5)
    grad_out = grad_ref[...]

    @pl.when(section == 0)
    def _():
        result_keep[...] = result_zero[...]
        swap[:rows, :] = result_one[...]

    @pl.when(section == 1)
    def _():
        result_keep[...] = result_one[...]
        swap[:rows, :] = result_zero[...]

    grad_middle = grad_middle_ref[...]
    grad_att = grad_att_ref[...]
    ffn_weight_grads(terms, grad_out, grad_middle, second, active, attended, grad_pre)
    spots = [(slice(spot * half, (spot + 1) * half), key_units(spot, half)) for spot in range(blocks)]
    heads = [
        (slice(number * head, (number + 1) * head), slice(width + number * head, width + (number + 1) * head))
        for number in range(HEADS)
    ]
    probs = [probs_ref[number] for number in range(HEADS)]
    grad_probs = [
        jnp.concatenate(
            [
                contract_cols(grad_att[here, columns], padded[window, value_columns])
                for here, window in spots
            ],
            axis=0,
        )
        for columns, value_columns in heads
    ]
    grad_scores = [
        (prob * (grad - jnp.sum(prob * grad, axis=-1, keepdims=True))).astype(BF)
        for prob, grad in zip(probs, grad_probs)
    ]
    grad_query = [
        jnp.concatenate(
            [product(grad[here, :], padded[window, columns]) for here, window in spots], axis=0
        )
        * scale
        for grad, (columns, _) in zip(grad_scores, heads)
    ]
    grad_query = jnp.concatenate(grad_query, axis=1).astype(BF)

    def gathered(lefts, right):
        parts = []
        for left, (columns, _) in zip(lefts, heads):
            terms_of = [contract_rows(left[here, :], right[here, columns]) for here, _ in spots]
            units = []
            for index in range(reached // half):
                spot, place = divmod(index, 2)
                held = None
                if spot < blocks:
                    held = terms_of[spot][place * half : (place + 1) * half, :]
                if place == 0 and spot > 0:
                    last = terms_of[spot - 1][2 * half :, :]
                    held = last if held is None else held + last
                units.append(held)
            parts.append(jnp.concatenate(units, axis=0))
        return jnp.concatenate(parts, axis=1)

    grad_keys = (gathered(grad_scores, query) * scale).astype(BF)
    grad_values = gathered([prob.astype(BF) for prob in probs], grad_att).astype(BF)
    normed = normed_all[...]
    normed_mine = jnp.concatenate(
        [normed[own_unit(spot, half), :] for spot in range(blocks)], axis=0
    )
    store_block(terms, 0, contract_rows(normed_mine, grad_query))
    store_block(terms, 1, contract_rows(normed, grad_keys))
    store_block(terms, 2, contract_rows(normed, grad_values))
    from_query = contract_cols(grad_query, w_qkv[0, :, :width])
    grad_line[:reached, :] = contract_cols(
        grad_keys, w_qkv[0, :, width : 2 * width]
    ) + contract_cols(grad_values, w_qkv[0, :, 2 * width :])
    for spot in range(blocks):
        grad_line[own_unit(spot, half), :] += from_query[spot * half : (spot + 1) * half, :]
    grad_normed = grad_line[:reached, :]
    normal = normal_all[...]
    store_gains(terms, jnp.sum(grad_normed * normal, axis=0, keepdims=True), ffn_term[...])
    grad_line[:reached, :] = unit_back(grad_normed * gains[0, 0:1, :], normal, inverse_all[:, 0:1])
    for spot in range(blocks):
        grad_line[own_unit(spot, half), :] += grad_middle[spot * half : (spot + 1) * half, :]
    grad_line[reached:, :] = jnp.zeros((grad_line.shape[0] - reached, width), F32)

    @pl.when(section == 0)
    def _():
        swap[rows : 2 * rows, :] = grad_out

    @pl.when(section == 1)
    def _():
        swap[rows:, :] = grad_line[:reached, :].astype(BF)


def zero_both_kernel(
    grad_ref,
    w_qkv,
    w_out,
    w_up,
    w_down,
    gains,
    middle_unit,
    middle_inverse,
    slope,
    *rest,
):
    *rest, grad_middle, grad_att, grad_pre, gain_term, terms = rest
    zero_ffn_kernel(
        grad_ref,
        w_out,
        w_up,
        w_down,
        gains,
        middle_unit,
        middle_inverse,
        slope,
        grad_middle,
        grad_att,
        grad_pre,
        gain_term,
    )
    inputs, outputs, (keep, send) = rest[:-5], rest[-5:-2], rest[-2:]
    zero_backward_kernel(
        grad_ref, w_qkv, gains, *inputs, grad_middle, grad_att, grad_pre, gain_term, *outputs, terms
    )
    keep[...] = terms[0]
    send[...] = terms[1]


def share_kernel(keep, one_near, zero_near, came, *pieces):
    rows = keep.shape[0]
    half = rows // 4
    block = 2 * half
    section = my_section()
    near_rows = rows_at(section * half, half)
    far_rows = rows_at(half - section * half, half)
    for step, piece in enumerate(pieces):
        spot = my_line() ^ step
        mine = rows_at(spot * half, half)
        piece[near_rows, :] = keep[mine, :]
        piece[far_rows, :] = came[mine, :]

    @pl.when(section == 0)
    def _():
        for step, piece in enumerate(pieces):
            base = (my_line() ^ step) * block
            near, far = rows_at(base + block, block), rows_at(rows + base + half, half)
            far = pl.ds(far.start, block)
            piece[block:, :] = (zero_near[near, :] + came[far, :].astype(F32)).astype(BF)

    @pl.when(section == 1)
    def _():
        for step, piece in enumerate(pieces):
            spot = my_line() ^ step
            piece[block : block + half, :] = came[rows_at(rows + spot * half, half), :]
            piece[block + half :, :] = one_near[rows_at(spot * half, half), :]


def settle_kernel(piece0, piece1, piece2, piece3, results, input_grads):
    block = piece0.shape[0] // 2
    for step, piece in enumerate((piece0, piece1, piece2, piece3)):
        micro = my_line() ^ step
        results[0, micro, 0] = piece[:block, :]
        input_grads[0, micro, 0] = piece[block:, :]


def write_half(core, terms, targets, held, sems):
    width = terms.shape[2]
    unit_rows = width // 2
    copies = []
    for place in range(6):
        number = 6 * core + place
        for part in range(2):
            quarter, spot = divmod(2 * place + part, 3)
            value = terms[my_flip(core) ^ quarter, spot * unit_rows : (spot + 1) * unit_rows, :]
            held[place, part * unit_rows : (part + 1) * unit_rows, :] = value.astype(F32)
        which = 0 if number < 3 else 1 if number == 3 else 2 if number < 8 else 3
        first = (number, 0, number - 4, number - 8)[which] * width
        rows = pl.ds(first if which == 3 else 0, width)
        columns = pl.ds(0 if which in (1, 3) else first, width)
        copies.append(
            pltpu.make_async_copy(
                held.at[place], targets[which].at[0, rows, columns], sems.at[place]
            )
        )
        copies[-1].start()
    for copy in copies:
        copy.wait()


def by_section(body):
    for core in range(2):
        pl.when(my_section() == core)(partial(body, core))


def near_kernel(zero, one, gain_attn, qkv, out, gain_ffn, up, down, held, sems, gains, gain_sems):
    spare = zero.shape[1] - GAIN_ROWS

    def body(core):
        terms = (zero, one)[core]
        sums = terms[0, spare:, :].astype(F32)
        copies = []
        for index, target in enumerate((gain_attn, gain_ffn)):
            gains[index] = sums[index : index + 1, :]
            copies.append(pltpu.make_async_copy(gains.at[index], target, gain_sems.at[index]))
            copies[-1].start()
        write_half(core, terms, (qkv, out, up, down), held, sems)
        for copy in copies:
            copy.wait()

    by_section(body)


def far_kernel(qkv_in, out_in, up_in, down_in, zero, one, qkv, out, up, down, held, sems):
    by_section(
        lambda core: write_half(1 - core, (zero, one)[core], (qkv, out, up, down), held, sems)
    )


SWAP = [(0, 1), (1, 0)]
PLANE = ("section", "rep")


def crossed(flips):
    return [(4 * s + g, 4 * s + (g ^ flips[s])) for s in range(2) for g in range(4)]


FIRST = crossed((1, 2))
SECOND = crossed((2, 1))


def along_line(value, step):
    return lax.ppermute(value, "dp", [(z, z ^ step) for z in range(4)])


def reduce_terms(keep, came, home, steps, before, between=None):
    bar = lax.optimization_barrier
    first = lax.ppermute(keep[2:4] + came[2:4], PLANE, FIRST)
    second = lax.ppermute(keep[1] + came[1] + first[1], PLANE, SECOND)
    total = bar(keep[0] + came[0] + first[0] + second)
    total, home[before] = bar((total, home[before]))
    total = bar(total + along_line(total, steps[0]))
    if between is not None:
        total, home[between] = bar((total, home[between]))
    total = bar(total + along_line(total, steps[1]))
    pair = jnp.stack([total, lax.ppermute(total, PLANE, SECOND)])
    return pair, lax.ppermute(pair, PLANE, FIRST)


def lines(
    block_input,
    output_grad,
    seq_lengths,
    attn_gain,
    qkv_proj,
    out_proj,
    ffn_gain,
    up_proj,
    down_proj,
):
    section = lax.axis_index("section")
    micro_count, _, block, width = block_input.shape
    hidden_units = up_proj.shape[2]
    half = block // 2
    rows, reach = micro_count * half, block + half
    reached = rows + rows + half
    term_rows = 6 * width // 4 + GAIN_ROWS

    *packed, window_mask, strided_mask = call(
        pack_kernel,
        (),
        (block_input, output_grad, attn_gain, ffn_gain, seq_lengths),
        (
            ((block + 16, width), BF),
            *((((block, width), BF),) * (micro_count - 1)),
            ((rows, reach), F32),
            ((rows, rows), F32),
        ),
        8,
        scratch=(
            pltpu.VMEM((2, 1, width), BF),
            pltpu.SMEM(seq_lengths.shape, jnp.int32),
            pltpu.SemaphoreType.DMA((2 * micro_count,)),
            pltpu.SemaphoreType.DMA((3,)),
        ),
        held=5,
    )
    near = [packed[0]] + [along_line(packed[step], step) for step in range(1, micro_count)]
    far = [lax.ppermute(piece, "section", SWAP) for piece in near]
    own = (qkv_proj[0], out_proj[0], up_proj[0], down_proj[0])
    near[1], *own = lax.optimization_barrier((near[1], *own))
    swapped = [lax.ppermute(weight, "section", SWAP) for weight in own]
    weights = tuple(
        jnp.stack([jnp.where(section == 0, a, b), jnp.where(section == 0, b, a)])
        for a, b in zip(own, swapped)
    )
    gains_near, gains_far = near[0][block:].astype(F32), far[0][block:].astype(F32)
    weights += (
        jnp.stack(
            [
                jnp.where(section == 0, gains_near, gains_far),
                jnp.where(section == 0, gains_far, gains_near),
            ]
        ),
    )
    ffn_saved = (
        ((rows, width), BF),
        ((rows, width), F32),
        ((rows, 128), F32),
        ((rows, width), BF),
        ((rows, hidden_units), BF),
        ((rows, hidden_units), F32),
    )
    (
        _,
        normal_all,
        inverse_all,
        normed_all,
        query,
        padded,
        probs_zero,
        attended_zero,
        cotangent,
        result_zero,
        *saved_zero,
    ) = call(
        zero_forward_kernel,
        (),
        (window_mask, *near, *far, *weights),
        (
            ((reached + half, width), BF),
            ((reached, width), F32),
            ((reached, 128), F32),
            ((reached, width), BF),
            ((rows, width), BF),
            ((reached, 2 * width), BF),
            ((HEADS, rows, reach), F32),
            ((rows, width), BF),
            ((rows, width), BF),
            *ffn_saved,
        ),
    )
    result_one, grad_one, keep_one, send_one = call(
        one_kernel,
        (),
        (strided_mask, result_zero, cotangent, *weights),
        (((rows, width), BF), ((rows, width), BF), *(((4, term_rows, width), BF),) * 2),
        micros=4.0,
        scratch=(
            pltpu.VMEM((rows, width), F32),
            pltpu.VMEM((rows, 128), F32),
            pltpu.VMEM((rows, width), BF),
            pltpu.VMEM((rows, 3 * width), BF),
            pltpu.VMEM((HEADS, rows, rows), F32),
            pltpu.VMEM((rows, width), BF),
            *(pltpu.VMEM(*shape) for shape in ffn_saved[1:]),
            pltpu.VMEM((rows, hidden_units), BF),
            pltpu.VMEM((2, 4, term_rows, width), BF),
        ),
    )
    middle_zero, mid_inverse_zero, second_zero, active_zero, slope_zero = saved_zero
    came_one = lax.ppermute(send_one, "section", SWAP)
    result_keep, grad_line, swap, keep_zero, send_zero = call(
        zero_both_kernel,
        (),
        (
            grad_one,
            *weights,
            middle_zero,
            mid_inverse_zero,
            slope_zero,
            normal_all,
            inverse_all,
            normed_all,
            query,
            padded,
            probs_zero,
            result_zero,
            result_one,
            second_zero,
            active_zero,
            attended_zero,
        ),
        (
            ((rows, width), BF),
            ((reached + half, width), F32),
            ((rows + reached, width), BF),
            *(((4, term_rows, width), BF),) * 2,
        ),
        micros=4.0,
        scratch=(
            pltpu.VMEM((rows, width), F32),
            pltpu.VMEM((rows, width), BF),
            pltpu.VMEM((rows, hidden_units), BF),
            pltpu.VMEM((1, width), F32),
            pltpu.VMEM((2, 4, term_rows, width), BF),
        ),
    )
    came = lax.ppermute(swap, "section", SWAP)
    shared = call(
        share_kernel,
        (),
        (result_keep, grad_one, grad_line, came),
        (((2 * block, width), BF),) * micro_count,
        8,
    )
    home = [shared[0]] + [along_line(shared[step], step) for step in range(1, micro_count)]
    came_zero = lax.ppermute(send_zero, "section", SWAP)
    zero_pair, zero_first = reduce_terms(keep_zero, came_zero, home, (1, 2), 1)
    one_pair, one_first = reduce_terms(keep_one, came_one, home, (2, 1), 3, 2)
    results, input_grads = call(
        settle_kernel,
        (),
        home,
        (((1, micro_count, 1, block, width), BF),) * 2,
        8,
    )

    def both_cores(parts):
        near = jnp.concatenate(parts)
        return near, jnp.concatenate([lax.ppermute(part, "section", SWAP) for part in parts])

    zero_near, zero_far = both_cores((zero_pair, zero_first))
    one_near, one_far = both_cores((one_pair, one_first))
    sums = (
        ((1, width, 3 * width), F32),
        ((1, width, width), F32),
        ((1, width, hidden_units), F32),
        ((1, hidden_units, width), F32),
    )
    held = (pltpu.VMEM((6, width, width), F32), pltpu.SemaphoreType.DMA((6,)))
    gain_attn_sum, qkv_half, out_half, gain_ffn_sum, up_half, down_half = call(
        near_kernel,
        (),
        (zero_near, one_near),
        (((1, width), F32), *sums[:2], ((1, width), F32), *sums[2:]),
        16,
        scratch=(*held, pltpu.VMEM((2, 1, width), F32), pltpu.SemaphoreType.DMA((2,))),
        out_held=(0, 1, 2, 3, 4, 5),
    )
    qkv_sum, out_sum, up_sum, down_sum = call(
        far_kernel,
        (),
        (qkv_half, out_half, up_half, down_half, zero_far, one_far),
        sums,
        16,
        scratch=held,
        held=4,
        out_held=(0, 1, 2, 3),
        aliases={0: 0, 1: 1, 2: 2, 3: 3},
    )
    return (
        results,
        input_grads,
        gain_attn_sum,
        qkv_sum,
        out_sum,
        gain_ffn_sum,
        up_sum,
        down_sum,
    )


def local(*arrays):
    micro_count, _, tok_rows, model_width = arrays[0].shape
    one_line_per_chip = (
        lax.axis_size("section") == 2
        and lax.axis_size("dp") == 4
        and lax.axis_size("rep") == 4
        and micro_count == 4
        and tok_rows == STRIDE
        and model_width == 256
        and arrays[7].shape[2] == 4 * model_width
    )
    return lines(*arrays) if one_line_per_chip else general(*arrays)


def solution(mesh):
    placed = (
        P(None, "rep", "dp", None),
        P(None, "rep", "dp", None),
        P(),
        P("section", None),
        P("section", None, None),
        P("section", None, None),
        P("section", None),
        P("section", None, None),
        P("section", None, None),
    )
    return jax.shard_map(
        local,
        mesh=mesh,
        in_specs=placed,
        out_specs=(
            P("section", None, "rep", "dp", None),
            P("section", None, "rep", "dp", None),
            P("section", None),
            P("section", None, None),
            P("section", None, None),
            P("section", None),
            P("section", None, None),
            P("section", None, None),
        ),
        check_vma=False,
    )
```
